32 devices in a mesh: section: 2 (over y), row: 4 (over z), col: 4 (over x, core).
Axes of the slice: x: 2, y: 2, z: 4, core: 2. Of those that a mesh axis runs over, the one named last changes fastest.
Arguments:
- inputs: bfloat16 [2, 2048, 1024], P(None, 'row', 'col'), may hold values from -6 to 6
- cotangent: bfloat16 [2, 2048, 1024], P(None, 'row', 'col'), may hold values from -6 to 6
- lengths: int32 [2, 8], replicated, may hold values from 0 to 512, as said below
- deal: int32 [2, 8], replicated, may hold values from 0 to 7, as said below
- query_key_value_weight: bfloat16 [2, 1024, 3, 1024], P('section', 'row', None, 'col'), may hold values from -0.1875 to 0.1875
- out_weight: bfloat16 [2, 1024, 1024], P('section', 'col', 'row'), may hold values from -0.375 to 0.375
- up_weight: bfloat16 [2, 1024, 4096], P('section', 'row', 'col'), may hold values from -0.1875 to 0.1875
- down_weight: bfloat16 [2, 4096, 1024], P('section', 'col', 'row'), may hold values from -0.09375 to 0.09375
- norm_gain: float32 [2, 2, 1024], P('section', None, 'col'), may hold values from 0.1 to 1.9
- norm_shift: float32 [2, 2, 1024], P('section', None, 'col'), may hold values from -1.75 to 1.75
- proj_bias: float32 [2, 4, 1024], P('section', None, 'col'), may hold values from -1.75 to 1.75
- up_bias: float32 [2, 4096], P('section', 'col'), may hold values from -1.75 to 1.75
Outputs:
- hidden_out: bfloat16 [2, 2, 2048, 1024], P('section', None, 'row', 'col')
- in_grad: float32 [2, 2, 2048, 1024], P('section', None, 'row', 'col')
- qkv_grad: float32 [2, 1024, 3, 1024], P('section', 'row', None, 'col')
- out_grad: float32 [2, 1024, 1024], P('section', 'col', 'row')
- up_grad: float32 [2, 1024, 4096], P('section', 'row', 'col')
- down_grad: float32 [2, 4096, 1024], P('section', 'col', 'row')
- gain_grad: float32 [2, 2, 1024], P('section', None, 'col')
- shift_grad: float32 [2, 2, 1024], P('section', None, 'col')
- bias_grad: float32 [2, 4, 1024], P('section', None, 'col')
- up_bias_grad: float32 [2, 4096], P('section', 'col')
The draws below stay inside these ranges and needn't reach their ends.
Inputs may be any that keep to these rules, and one draw needn't show every extreme that they name: Row m holds micro-batch m's sequence lengths in given order. The two sequences with deal values 2 r and 2 r + 1 belong to row device r and together hold at most 512 tokens; in every micro-batch some device holds exactly 512. Each row is a permutation of 0 to 7; sequence i goes to row device deal // 2, first there if deal is even.
All inputs are finite; a program needn't handle non-finite values.
Results may differ from the reference program's by a relative error of at most 0.015.
Values may be sent and summed in bfloat16 or wider, within the bound.
No kernel may reach another device: no remote copies, remote signals or barrier semaphores. Data moves between devices by JAX's collectives and lax.ppermute only.
A program may use at most 192 MiB of HBM per device.

```python
import jax
import jax.numpy as jnp
from jax import lax

D = 1024
HEADS = 16
HEAD_DIM = 64
FF = 4096
TOK_DEV = 512
MICRO = 2
TOKENS = 2048
NSEQ = 8
N_ROW = 4


def draw_plan(key):
    holders = NSEQ // 2

    def one_batch(sub_key):
        key_first, key_second, key_chosen, key_order = jax.random.split(sub_key, 4)
        leading = jax.random.randint(key_first, (holders,), TOK_DEV // 4, TOK_DEV + 1)
        second = jax.random.randint(key_second, (holders,), 0, TOK_DEV - leading + 1)
        chosen = jax.random.randint(key_chosen, (), 0, holders)
        devices = jnp.arange(holders)
        leading = jnp.where(devices == chosen, TOK_DEV, leading)
        second = jnp.where(devices == chosen, 0, second)
        owned = jnp.stack([leading, second], axis=1).reshape(NSEQ)
        ordering = jax.random.permutation(key_order, NSEQ)
        return (owned[ordering].astype(jnp.int32), ordering.astype(jnp.int32))
    return jax.vmap(one_batch)(jax.random.split(key, MICRO))


def draw_lengths(key, part):
    planned = draw_plan(key)
    return planned[0]


def draw_deal(key, part):
    planned = draw_plan(key)
    return planned[1]


def steps_of(own_key, extent, shards, low, largest):
    level, own = 1.0, jax.random.fold_in(own_key, 6)
    for dim, parts in shards:
        steps = jnp.exp(jax.random.uniform(jax.random.fold_in(own, dim), (parts,), jnp.float32, low / len(shards), largest / len(shards)))
        level = level * jnp.repeat(steps, extent[dim] // parts).reshape([-1 if axis == dim else 1 for axis in range(len(extent))])
    return level


def scatter_about(own_key, dims, width, limit, shards=(), kind=jnp.bfloat16):
    drawn = width * jax.random.normal(own_key, dims, jnp.float32)
    if shards:
        drawn = drawn * steps_of(own_key, dims, shards, -0.22, 0.18)
    return jnp.clip(drawn, -limit, limit).astype(kind)


def setup_inputs(seed: int = 0) -> dict:
    keys = jax.random.split(jax.random.key(seed), 13)
    inputs = scatter_about(keys[0], (MICRO, TOKENS, D), 1.0, 6.0, ((1, 4), (2, 4)))
    cotangent = scatter_about(keys[1], (MICRO, TOKENS, D), 1.0, 6.0, ((1, 4), (2, 4)))
    lengths = draw_lengths(jax.random.fold_in(keys[12], 71), 0)
    deal = draw_deal(jax.random.fold_in(keys[12], 71), 0)
    query_key_value_weight = scatter_about(keys[4], (2, D, 3, D), D ** -0.5, 0.1875, ((0, 2), (1, 4), (3, 4)))
    out_weight = scatter_about(keys[5], (2, D, D), (D // 4) ** -0.5, 0.375, ((0, 2), (1, 4), (2, 4)))
    up_weight = scatter_about(keys[6], (2, D, FF), D ** -0.5, 0.1875, ((0, 2), (1, 4), (2, 4)))
    down_weight = scatter_about(keys[7], (2, FF, D), FF ** -0.5, 0.09375, ((0, 2), (1, 4), (2, 4)))
    norm_gain = jnp.clip(1.0 + 0.18 * jax.random.normal(keys[8], (2, 2, D), jnp.float32), 0.1, 1.9)
    norm_shift = scatter_about(keys[9], (2, 2, D), 0.3, 1.75, ((0, 2), (2, 4)), jnp.float32)
    proj_bias = scatter_about(keys[10], (2, 4, D), 0.3, 1.75, ((0, 2), (2, 4)), jnp.float32)
    up_bias = scatter_about(keys[11], (2, FF), 0.3, 1.75, ((0, 2), (1, 4)), jnp.float32)
    return {"inputs": inputs, "cotangent": cotangent, "lengths": lengths, "deal": deal, "query_key_value_weight": query_key_value_weight, "out_weight": out_weight, "up_weight": up_weight, "down_weight": down_weight, "norm_gain": norm_gain, "norm_shift": norm_shift, "proj_bias": proj_bias, "up_bias": up_bias}


epsilon = 1e-05
masked_score = -1e+30
exact_precision = lax.Precision.HIGHEST

@jax.custom_vjp
def low(v):
    return lax.optimization_barrier(v.astype(jnp.bfloat16)).astype(jnp.float32)

@jax.custom_vjp
def low_back(v):
    return v

def low_keep(v):
    return (low(v), None)

def low_pass(kept, grad):
    return (grad,)

def back_keep(v):
    return (v, None)

def back_low(kept, grad):
    return (low(grad),)
low.defvjp(low_keep, low_pass)
low_back.defvjp(back_keep, back_low)

def gelu_tanh(values):
    return jax.nn.gelu(values, approximate=True)

def layouts(lengths, deal):
    starts = (jnp.cumsum(lengths, axis=1) - lengths).astype(jnp.int32)
    ordering = jnp.arange(NSEQ, dtype=jnp.int32)
    matches = deal[:, :, None] == ordering[None, None, :]
    own_len = lax.optimization_barrier(jnp.sum(jnp.where(matches, lengths[:, :, None], 0), axis=1)).astype(jnp.int32)
    own_start = lax.optimization_barrier(jnp.sum(jnp.where(matches, starts[:, :, None], 0), axis=1)).astype(jnp.int32)
    first_len = own_len[:, 0::2][:, :, None]
    second_len = own_len[:, 1::2][:, :, None]
    slot_ids = jnp.arange(TOK_DEV, dtype=jnp.int32)[None, None, :]
    in_first = slot_ids < first_len
    in_second = jnp.logical_and(jnp.logical_not(in_first), slot_ids < first_len + second_len)
    usable = jnp.logical_or(in_first, in_second)
    position = jnp.where(in_first, slot_ids, slot_ids - first_len).astype(jnp.int32)
    source = jnp.where(in_first, own_start[:, 0::2][:, :, None] + slot_ids, own_start[:, 1::2][:, :, None] + position)
    source = jnp.where(usable, source, 0).astype(jnp.int32)
    segment = jnp.where(in_first, 0, jnp.where(in_second, 1, 2)).astype(jnp.int32)
    flat_source = jnp.where(usable, source, TOKENS).astype(jnp.int32).reshape(MICRO, N_ROW * TOK_DEV)
    all_slots = jnp.arange(N_ROW * TOK_DEV, dtype=jnp.int32)
    returned = jax.vmap(lambda target: jnp.zeros((TOKENS,), jnp.int32).at[target].set(all_slots, mode='drop'))(flat_source)
    is_live = jax.vmap(lambda target: jnp.zeros((TOKENS,), jnp.int32).at[target].set(1, mode='drop'))(flat_source) > 0
    return (source.reshape(MICRO, N_ROW * TOK_DEV), usable, segment, position, returned, is_live)

def layer_norm(hidden, gain, shift):
    average = lax.optimization_barrier(jnp.mean(hidden, axis=-1, keepdims=True))
    square = lax.optimization_barrier(jnp.mean(hidden * hidden, axis=-1, keepdims=True))
    inverse = lax.rsqrt(square - average * average + epsilon)
    return (hidden - average) * inverse * gain + shift

def layer_pack(hidden, segment, position, usable, params):
    query_key_value_weight, out_weight, up_weight, down_weight, norm_gain, norm_shift, proj_bias, up_bias = params
    normalized_rows = low(layer_norm(hidden, norm_gain[0], norm_shift[0]))
    query_key_value_columns = jnp.einsum('kp,pnf->knf', normalized_rows, query_key_value_weight, precision=exact_precision)
    queries = low_back(low(query_key_value_columns[:, 0] + proj_bias[0])).reshape(TOK_DEV, HEADS, HEAD_DIM)
    key_rows = low_back(low(query_key_value_columns[:, 1])).reshape(TOK_DEV, HEADS, HEAD_DIM)
    value_rows = low_back(low(query_key_value_columns[:, 2] + proj_bias[1])).reshape(TOK_DEV, HEADS, HEAD_DIM)
    slopes = jnp.exp2(-8.0 * (jnp.arange(HEADS, dtype=jnp.float32) + 1.0) / HEADS)
    block_rows = min(512, TOK_DEV)

    def attend(offset):
        query_block = lax.dynamic_slice_in_dim(queries, offset, block_rows, 0)
        block_segment = lax.dynamic_slice_in_dim(segment, offset, block_rows, 0)
        block_position = lax.dynamic_slice_in_dim(position, offset, block_rows, 0)
        scores = jnp.einsum('qhe,khe->hqk', query_block, key_rows, precision=exact_precision) * HEAD_DIM ** (-0.5)
        distance = (block_position[:, None] - position[None, :]).astype(jnp.float32)
        allowed = jnp.logical_and(block_segment[:, None] == segment[None, :], jnp.logical_and(block_segment[:, None] < 2, distance >= 0))
        scores = scores - slopes[:, None, None] * distance[None]
        scores = low_back(jnp.where(allowed[None], scores, masked_score))
        soft_weights = jax.nn.softmax(scores, axis=-1)
        return jnp.einsum('hqk,khe->qhe', low(soft_weights), value_rows, precision=exact_precision)
    mixed_heads = lax.map(jax.checkpoint(attend), jnp.arange(0, TOK_DEV, block_rows, dtype=jnp.int32))
    attended = low_back(low(mixed_heads.reshape(TOK_DEV, D)))
    branch = low_back(jnp.dot(attended, out_weight, precision=exact_precision) + proj_bias[2])
    middle = hidden + branch
    normed_two = low(layer_norm(middle, norm_gain[1], norm_shift[1]))
    upper_in = low_back(jnp.dot(normed_two, up_weight, precision=exact_precision) + up_bias)
    activated = low(gelu_tanh(upper_in))
    down_out = low_back(jnp.dot(activated, down_weight, precision=exact_precision) + proj_bias[3])
    return jnp.where(usable[:, None], middle + down_out, 0.0)

def run_layer(packed, segment, position, usable, params):
    checked = jax.checkpoint(layer_pack)
    return lax.map(lambda pack_args: checked(pack_args[0], pack_args[1], pack_args[2], pack_args[3], params), (packed, segment, position, usable))

def reference(inputs, cotangent, lengths, deal, query_key_value_weight, out_weight, up_weight, down_weight, norm_gain, norm_shift, proj_bias, up_bias):
    source, usable, segment, position, returned, is_live = layouts(lengths, deal)
    pack_count = MICRO * N_ROW
    usable_packs = usable.reshape(pack_count, TOK_DEV)
    segment_packs = segment.reshape(pack_count, TOK_DEV)
    position_packs = position.reshape(pack_count, TOK_DEV)

    def deal_rows(values):
        taken_rows = jax.vmap(lambda rows_in, pick_ids: jnp.take(rows_in, pick_ids, axis=0))(values, source)
        taken_rows = jnp.where(usable.reshape(MICRO, N_ROW * TOK_DEV)[:, :, None], taken_rows, 0.0)
        return taken_rows.reshape(pack_count, TOK_DEV, D)

    def undeal(packed):
        flat_rows = packed.reshape(MICRO, N_ROW * TOK_DEV, D)
        taken_rows = jax.vmap(lambda rows_in, pick_ids: jnp.take(rows_in, pick_ids, axis=0))(flat_rows, returned)
        return jnp.where(is_live[:, :, None], taken_rows, 0.0)

    def forward(given, extra_grad, *params):
        first_section = tuple((member[0] for member in params))
        second_section = tuple((member[1] for member in params))
        first_out = undeal(run_layer(deal_rows(given), segment_packs, position_packs, usable_packs, first_section))
        middle_in = low_back(low(first_out)) + extra_grad
        second_out = undeal(run_layer(deal_rows(middle_in), segment_packs, position_packs, usable_packs, second_section))
        return (second_out, low(first_out))
    params = tuple((member.astype(jnp.float32) for member in (query_key_value_weight, out_weight, up_weight, down_weight, norm_gain, norm_shift, proj_bias, up_bias)))
    given = inputs.astype(jnp.float32)
    result, pullback, first_out = jax.vjp(forward, given, jnp.zeros_like(given), *params, has_aux=True)
    gradients = pullback(cotangent.astype(jnp.float32))
    hidden_out = jnp.stack([first_out, result]).astype(jnp.bfloat16)
    in_grad = jnp.stack([gradients[0], gradients[1]])
    return (hidden_out, in_grad, gradients[2], gradients[3], gradients[4], gradients[5], gradients[6], gradients[7], gradients[8], gradients[9])
```

```python
import jax
import jax.numpy as jnp
from jax import lax
from jax.sharding import PartitionSpec as P

HEAD_DIM = 64
epsilon = 1e-05
masked_score = -1e30
F32 = jnp.float32
BF16 = jnp.bfloat16


def mm(a, b, dims):
    return lax.dot_general(a, b, ((dims[0], dims[1]), ((), ())), preferred_element_type=F32)


def nn(a, b):
    return mm(a, b, ((1,), (0,)))


def nt(a, b):
    return mm(a, b, ((1,), (1,)))


def tn(a, b):
    return mm(a, b, ((0,), (0,)))


def swap_bit(array, axis, bit):
    count = lax.axis_size(axis)
    return lax.ppermute(array, axis, [(i, i ^ bit) for i in range(count)])


def spread_tokens(own):
    count = lax.axis_size("col")
    blocks = {0: own}
    bit = count // 2
    while bit >= 1:
        held = sorted(blocks)
        sent = swap_bit(jnp.concatenate([blocks[b] for b in held], axis=0), "col", bit)
        size = own.shape[0]
        for place, b in enumerate(held):
            blocks[b ^ bit] = sent[place * size : (place + 1) * size]
        bit //= 2
    return jnp.concatenate([blocks[b] for b in range(count)], axis=0)


def sum_tokens(partial):
    count = lax.axis_size("col")
    size = partial.shape[0] // count
    blocks = {b: partial[b * size : (b + 1) * size] for b in range(count)}
    bit = 1
    while bit < count:
        far = [b for b in sorted(blocks) if b & bit]
        sent = swap_bit(
            jnp.concatenate([blocks[b].astype(BF16) for b in far], axis=0), "col", bit
        )
        for place, b in enumerate(far):
            blocks[b ^ bit] = blocks[b ^ bit] + sent[place * size : (place + 1) * size].astype(F32)
            del blocks[b]
        bit *= 2
    return blocks[0]


def owned_layout(lengths, deal, holder, rows_dev):
    starts = jnp.cumsum(lengths) - lengths
    first = deal == 2 * holder
    second = deal == 2 * holder + 1
    first_len = jnp.sum(jnp.where(first, lengths, 0))
    second_len = jnp.sum(jnp.where(second, lengths, 0))
    first_start = jnp.sum(jnp.where(first, starts, 0))
    second_start = jnp.sum(jnp.where(second, starts, 0))
    slots = jnp.arange(rows_dev, dtype=jnp.int32)
    in_first = slots < first_len
    in_second = jnp.logical_and(jnp.logical_not(in_first), slots < first_len + second_len)
    usable = jnp.logical_or(in_first, in_second)
    position = jnp.where(in_first, slots, slots - first_len)
    source = jnp.where(in_first, first_start + slots, second_start + position)
    source = jnp.where(usable, source, -1)
    segment = jnp.where(in_first, 0, jnp.where(in_second, 1, 2)).astype(jnp.int32)
    return source, usable, segment, position


def given_targets(lengths, deal, positions, rows_dev):
    starts = jnp.cumsum(lengths) - lengths
    before = deal[None, :] == (deal - 1)[:, None]
    partner_len = jnp.sum(jnp.where(before, lengths[None, :], 0), axis=1)
    offset = jnp.where(deal % 2 == 1, partner_len, 0)
    base = deal // 2 * rows_dev + offset - starts
    inside = jnp.logical_and(
        positions[:, None] >= starts[None, :], positions[:, None] < (starts + lengths)[None, :]
    )
    target = jnp.sum(jnp.where(inside, base[None, :] + positions[:, None], 0), axis=1)
    return jnp.where(jnp.any(inside, axis=1), target, -1)


def pick_rows(rows, wanted):
    onehot = (wanted[:, None] == jnp.arange(rows.shape[0], dtype=jnp.int32)[None, :]).astype(BF16)
    return nn(onehot, rows)


def normalize(hidden, gain, shift):
    average = jnp.mean(hidden, axis=1, keepdims=True)
    square = jnp.mean(hidden * hidden, axis=1, keepdims=True)
    inverse = lax.rsqrt(square - average * average + epsilon)
    centered = (hidden - average) * inverse
    return centered, inverse, (centered * gain + shift).astype(BF16)


def norm_backward(grad_norm, centered, inverse, gain):
    grad_cent = grad_norm * gain
    summed = jnp.mean(grad_cent, axis=1, keepdims=True)
    cross = jnp.mean(grad_cent * centered, axis=1, keepdims=True)
    grad_hidden = inverse * (grad_cent - summed - centered * cross)
    return grad_hidden, jnp.sum(grad_norm * centered, axis=0), jnp.sum(grad_norm, axis=0)


def gelu_tanh(values):
    return jax.nn.gelu(values, approximate=True)


def masked_scores(queries, key_rows, segment, position, slopes):
    scores = jnp.einsum(
        "qhe,khe->hqk", queries, key_rows, preferred_element_type=F32
    ) * HEAD_DIM ** (-0.5)
    distance = (position[:, None] - position[None, :]).astype(F32)
    allowed = jnp.logical_and(
        segment[:, None] == segment[None, :],
        jnp.logical_and(segment[:, None] < 2, distance >= 0),
    )
    scores = scores - slopes[:, None, None] * distance[None]
    return jnp.where(allowed[None], scores, masked_score)


def attend_forward(queries, key_rows, value_rows, segment, position, slopes):
    rows = queries.shape[0]
    scores = masked_scores(queries, key_rows, segment, position, slopes)
    highest = jnp.max(scores, axis=2, keepdims=True)
    exp_scores = jnp.exp(scores - highest)
    summed = jnp.sum(exp_scores, axis=2, keepdims=True)
    soft = (exp_scores / summed).astype(BF16)
    mixed = jnp.einsum("hqk,khe->qhe", soft, value_rows, preferred_element_type=F32)
    return mixed.reshape(rows, -1).astype(BF16), highest + jnp.log(summed)


def attend_backward(queries, key_rows, value_rows, segment, position, slopes, logsum, grad_mixed):
    scale = HEAD_DIM ** (-0.5)
    rows = queries.shape[0]
    scores = masked_scores(queries, key_rows, segment, position, slopes)
    soft = jnp.exp(scores - logsum)
    grad_prob = jnp.einsum("qhe,khe->hqk", grad_mixed, value_rows, preferred_element_type=F32)
    row_dot = jnp.sum(soft * grad_prob, axis=2, keepdims=True)
    grad_score = (soft * (grad_prob - row_dot)).astype(BF16)
    grad_query = (
        jnp.einsum("hqk,khe->qhe", grad_score, key_rows, preferred_element_type=F32) * scale
    )
    grad_key = jnp.einsum("hqk,qhe->khe", grad_score, queries, preferred_element_type=F32) * scale
    grad_value = jnp.einsum(
        "hqk,qhe->khe", soft.astype(BF16), grad_mixed, preferred_element_type=F32
    )
    return jnp.concatenate(
        [g.astype(BF16).reshape(rows, -1) for g in (grad_query, grad_key, grad_value)], axis=1
    )


def times_rows(left, weight):
    half = weight[0].shape[0]
    return nn(left[:, :half], weight[0]) + nn(left[:, half:], weight[1])


def times_rows_back(left, weight):
    return jnp.concatenate([nt(left, weight[0]), nt(left, weight[1])], axis=1)


def layer_forward(hidden, layout, weights, small):
    usable, segment, position, slopes = layout
    attn_w, up_w, down_w = weights
    width = attn_w[0].shape[1] // 4
    gain, shift, bias_q, bias_v, bias_out, bias_down, up_bias = small
    centered, inverse, normed = normalize(hidden, gain[0], shift[0])
    rows_all = spread_tokens(normed)
    rows = rows_all.shape[0]
    qkv_w = [w[:, : 3 * width] for w in attn_w]
    out_w = [w[:, 3 * width :] for w in attn_w]
    qkv = times_rows(rows_all, qkv_w)
    queries = (qkv[:, :width] + bias_q).astype(BF16).reshape(rows, -1, HEAD_DIM)
    key_rows = qkv[:, width : 2 * width].astype(BF16).reshape(rows, -1, HEAD_DIM)
    value_rows = (qkv[:, 2 * width :] + bias_v).astype(BF16).reshape(rows, -1, HEAD_DIM)
    attended, logsum = attend_forward(queries, key_rows, value_rows, segment, position, slopes)
    branch = sum_tokens(times_rows_back(attended, out_w)) + bias_out
    middle = hidden + branch
    centered_two, inverse_two, normed_two = normalize(middle, gain[1], shift[1])
    rows_two = spread_tokens(normed_two)
    upper_in = times_rows(rows_two, up_w) + up_bias
    activated = gelu_tanh(upper_in).astype(BF16)
    down_out = sum_tokens(times_rows_back(activated, down_w)) + bias_down
    result = jnp.where(usable[:, None], middle + down_out, 0.0)
    stored = (
        centered,
        inverse,
        rows_all,
        queries,
        key_rows,
        value_rows,
        logsum,
        attended,
        centered_two,
        inverse_two,
        rows_two,
        upper_in,
        activated,
    )
    return result, stored


def layer_backward(grad_out, layout, weights, small, stored):
    usable, segment, position, slopes = layout
    attn_w, up_w, down_w = weights
    width = attn_w[0].shape[1] // 4
    gain = small[0]
    (
        centered,
        inverse,
        rows_all,
        queries,
        key_rows,
        value_rows,
        logsum,
        attended,
        centered_two,
        inverse_two,
        rows_two,
        upper_in,
        activated,
    ) = stored
    qkv_w = [w[:, : 3 * width] for w in attn_w]
    out_w = [w[:, 3 * width :] for w in attn_w]
    grad_down = grad_out.astype(BF16)
    down_all = spread_tokens(grad_down)
    grad_act = times_rows(down_all, down_w)
    grad_upper = jax.vjp(gelu_tanh, upper_in)[1](grad_act)[0].astype(BF16)
    grad_norm_two = sum_tokens(times_rows_back(grad_upper, up_w))
    down_term = tn(down_all, activated).astype(BF16)
    up_term = tn(rows_two, grad_upper).astype(BF16)
    grad_mid, gain_two, shift_two = norm_backward(
        grad_norm_two, centered_two, inverse_two, gain[1]
    )
    grad_mid = grad_out + grad_mid
    grad_branch = grad_mid.astype(BF16)
    branch_all = spread_tokens(grad_branch)
    grad_attended = times_rows(branch_all, out_w).astype(BF16).reshape(queries.shape)
    grad_qkv = attend_backward(
        queries, key_rows, value_rows, segment, position, slopes, logsum, grad_attended
    )
    grad_norm = sum_tokens(times_rows_back(grad_qkv, qkv_w))
    attn_term = jnp.concatenate(
        [tn(rows_all, grad_qkv).astype(BF16), tn(branch_all, attended).astype(BF16)], axis=1
    )
    grad_in, gain_one, shift_one = norm_backward(grad_norm, centered, inverse, gain[0])
    grad_input = grad_mid + grad_in
    token_sums = jnp.stack(
        [
            gain_one,
            gain_two,
            shift_one,
            shift_two,
            jnp.sum(grad_branch, axis=0, dtype=F32),
            jnp.sum(grad_down, axis=0, dtype=F32),
        ]
    )
    qkv_sums = jnp.sum(grad_qkv, axis=0, dtype=F32)
    column_sums = jnp.concatenate(
        [qkv_sums[:width], qkv_sums[2 * width :], jnp.sum(grad_upper, axis=0, dtype=F32)]
    )
    return grad_input, (attn_term, up_term, down_term), token_sums, column_sums


def on_device(
    inputs,
    cotangent,
    lengths,
    deal,
    query_key_value_weight,
    out_weight,
    up_weight,
    down_weight,
    norm_gain,
    norm_shift,
    proj_bias,
    up_bias,
):
    section = lax.axis_index("section")
    holder = lax.axis_index("row")
    column = lax.axis_index("col")
    rows_count, cols_count = lax.axis_size("row"), lax.axis_size("col")
    micro_count, rows_dev, width = inputs.shape
    model = width * cols_count
    heads_dev = width // HEAD_DIM
    heads = heads_dev * cols_count
    tokens = rows_dev // cols_count
    block = model // rows_count
    half = block // 2
    is_zero = section == 0

    def pick(zero, one):
        return jnp.where(is_zero, zero, one)

    def own_first(array, axis):
        shape = array.shape
        split = array.reshape(shape[:axis] + (rows_count, 2, half) + shape[axis + 1 :])
        parts = [lax.index_in_dim(split, i, axis + 1, keepdims=False) for i in (0, 1)]
        flat = [p.reshape(shape[:axis] + (model // 2,) + shape[axis + 1 :]) for p in parts]
        return jnp.concatenate([pick(flat[0], flat[1]), pick(flat[1], flat[0])], axis=axis)

    def true_order(array, axis):
        shape = array.shape
        mine = lax.slice_in_dim(array, 0, model // 2, axis=axis)
        other = lax.slice_in_dim(array, model // 2, model, axis=axis)
        parts = [
            p.reshape(shape[:axis] + (rows_count, 1, half) + shape[axis + 1 :])
            for p in (pick(mine, other), pick(other, mine))
        ]
        return jnp.concatenate(parts, axis=axis + 1).reshape(shape)

    packed = (
        jnp.concatenate(
            [query_key_value_weight[0].reshape(block, 3 * width), out_weight[0].T], axis=1
        ),
        up_weight[0],
        down_weight[0].T,
    )
    kept = [pick(w[:half], w[half:]) for w in packed]
    given = [swap_bit(pick(w[half:], w[:half]), "section", 1) for w in packed]
    halves = (
        [pick(k, g) for k, g in zip(kept, given)],
        [pick(g, k) for k, g in zip(kept, given)],
    )

    def gather_weight(piece):
        mine = lax.all_gather(piece, "row", axis=0, tiled=True)
        return (mine, swap_bit(mine, "section", 1))

    mine_small = jnp.concatenate(
        [norm_gain[0], norm_shift[0], proj_bias[0], up_bias[0].reshape(-1, width)], axis=0
    )
    all_small = lax.all_gather(mine_small, ("section", "col"), axis=0, tiled=False)
    all_small = all_small.reshape((2, cols_count) + mine_small.shape)

    def layer_small(layer):
        table = all_small[layer]
        whole = own_first(jnp.transpose(table[:, :8], (1, 0, 2)).reshape(8, model), 1)
        own = jnp.take(table, column, axis=0)
        return (
            whole[0:2],
            whole[2:4],
            own[4],
            own[5],
            whole[6],
            whole[7],
            own[8:].reshape(-1),
        )

    source, usable, segment, position = owned_layout(
        lengths[section], deal[section], holder, rows_dev
    )
    order = jnp.bitwise_xor(column, jnp.arange(cols_count, dtype=jnp.int32))

    def xor_order(values):
        return values.reshape(cols_count, tokens)[order].reshape(rows_dev)

    own_usable = usable.reshape(cols_count, tokens)[column]
    head_ids = column * heads_dev + jnp.arange(heads_dev, dtype=jnp.int32)
    slopes = jnp.exp2(-8.0 * (head_ids.astype(F32) + 1.0) / heads)
    layout = (own_usable, xor_order(segment), xor_order(position), slopes)

    def deal_rows(array):
        portion = lax.all_gather(pick(array[0], array[1]), "row", axis=0, tiled=True)
        owned = pick_rows(portion, source).astype(BF16)
        own = lax.all_to_all(
            owned.reshape(cols_count, tokens, width), "col", split_axis=0, concat_axis=0
        )
        return own_first(jnp.transpose(own, (1, 0, 2)).reshape(tokens, model), 1)

    weights = [[None] * 3, [None] * 3]
    first_rows = deal_rows(inputs)
    for layer in range(2):
        for kind in range(3):
            weights[layer][kind] = gather_weight(halves[layer][kind])
    smalls = [layer_small(0), layer_small(1)]

    hidden_zero, stored_zero = layer_forward(first_rows.astype(F32), layout, weights[0], smalls[0])
    middle_in = hidden_zero.astype(BF16)
    hidden_one, stored_one = layer_forward(
        middle_in.astype(F32), layout, weights[1], smalls[1]
    )
    last_out = hidden_one.astype(BF16)

    positions = holder * rows_dev + jnp.arange(rows_dev, dtype=jnp.int32)
    targets = jax.vmap(given_targets, (0, 0, None, None))(lengths, deal, positions, rows_dev)

    def give_back(zero, one):
        def by_features(own):
            parts = true_order(own, 1).reshape(tokens, cols_count, width)
            got = lax.all_to_all(
                jnp.transpose(parts, (1, 0, 2)), "col", split_axis=0, concat_axis=0
            )
            return got.reshape(rows_dev, width)

        stays = by_features(pick(zero, one))
        comes = swap_bit(by_features(pick(one, zero)), "section", 1)
        both = jnp.stack([pick(stays, comes), pick(comes, stays)])
        whole = lax.all_gather(both, "row", axis=1, tiled=True)
        return jnp.stack([pick_rows(whole[m], targets[m]) for m in range(micro_count)])

    hidden_out = give_back(middle_in, last_out).astype(BF16)

    grad_one = deal_rows(cotangent).astype(F32)
    grad_one_in, terms_one, token_one, column_one = layer_backward(
        grad_one, layout, weights[1], smalls[1], stored_one
    )
    grad_zero = grad_one_in.astype(BF16)
    grad_zero = jnp.where(own_usable[:, None], grad_zero, jnp.zeros_like(grad_zero)).astype(F32)
    grad_zero_in, terms_zero, token_zero, column_zero = layer_backward(
        grad_zero, layout, weights[0], smalls[0], stored_zero
    )

    def reduce_weight(term):
        mine, other = term[: model // 2], term[model // 2 :]
        total = (mine.astype(F32) + swap_bit(other, "section", 1).astype(F32)).astype(BF16)
        return lax.psum_scatter(total, "row", scatter_dimension=0, tiled=True)

    sums_one = [reduce_weight(t) for t in terms_one]
    sums_zero = [reduce_weight(t) for t in terms_zero]
    finals = []
    for zero, one in zip(sums_zero, sums_one):
        mine = pick(zero, one)
        other = swap_bit(pick(one, zero), "section", 1)
        finals.append(
            jnp.concatenate([pick(mine, other), pick(other, mine)], axis=0).astype(F32)
        )
    qkv_grad = finals[0][:, : 3 * width].reshape(block, 3, width)
    out_grad = finals[0][:, 3 * width :].T
    up_grad = finals[1]
    down_grad = finals[2].T

    in_grad = give_back(grad_zero_in.astype(BF16), grad_one_in.astype(BF16))

    token_sums = jnp.stack([true_order(token_zero, 1), true_order(token_one, 1)])
    token_sums = lax.psum(token_sums, ("section", "row", "col"))
    column_sums = lax.psum(jnp.stack([column_zero, column_one]), ("section", "row"))
    token_sums = lax.dynamic_slice_in_dim(
        pick(token_sums[0], token_sums[1]), column * width, width, axis=1
    )
    column_sums = pick(column_sums[0], column_sums[1])
    bias_grad = jnp.concatenate(
        [column_sums[: 2 * width].reshape(2, width), token_sums[4:6]], axis=0
    )
    return (
        hidden_out[None],
        in_grad[None],
        qkv_grad[None],
        out_grad[None],
        up_grad[None],
        down_grad[None],
        token_sums[0:2][None],
        token_sums[2:4][None],
        bias_grad[None],
        column_sums[2 * width :][None],
    )


def solution(mesh):
    placed = (
        P(None, "row", "col"),
        P(None, "row", "col"),
        P(),
        P(),
        P("section", "row", None, "col"),
        P("section", "col", "row"),
        P("section", "row", "col"),
        P("section", "col", "row"),
        P("section", None, "col"),
        P("section", None, "col"),
        P("section", None, "col"),
        P("section", "col"),
    )
    return jax.shard_map(
        on_device,
        mesh=mesh,
        in_specs=placed,
        out_specs=(
            P("section", None, "row", "col"),
            P("section", None, "row", "col"),
            P("section", "row", None, "col"),
            P("section", "col", "row"),
            P("section", "row", "col"),
            P("section", "col", "row"),
            P("section", None, "col"),
            P("section", None, "col"),
            P("section", None, "col"),
            P("section", "col"),
        ),
        check_vma=False,
    )
```

```python
import jax
import jax.numpy as jnp
from jax import lax
from jax.sharding import PartitionSpec as P

HEAD_DIM = 64
epsilon = 1e-05
masked_score = -1e30
F32 = jnp.float32
BF16 = jnp.bfloat16


def mm(a, b, dims):
    return lax.dot_general(a, b, ((dims[0], dims[1]), ((), ())), preferred_element_type=F32)


def nn(a, b):
    return mm(a, b, ((1,), (0,)))


def nt(a, b):
    return mm(a, b, ((1,), (1,)))


def tn(a, b):
    return mm(a, b, ((0,), (0,)))


def swap_bit(array, axis, bit):
    count = lax.axis_size(axis)
    return lax.ppermute(array, axis, [(i, i ^ bit) for i in range(count)])


def column_bits():
    count = lax.axis_size("col")
    return [1 << i for i in reversed(range(count.bit_length() - 1))]


def spread_order():
    order = [0]
    for bit in column_bits():
        order = order + [o ^ bit for o in order]
    return order


def spread_tokens(own):
    held = own
    for bit in column_bits():
        held = jnp.concatenate([held, swap_bit(held, "col", bit)], axis=0)
    return held


def sum_tokens(partial):
    held = partial
    for bit in reversed(column_bits()):
        half = held.shape[0] // 2
        held = held[:half] + swap_bit(held[half:].astype(BF16), "col", bit).astype(F32)
    return held


def gather_direct(array):
    count = lax.axis_size("row")
    copies = jnp.broadcast_to(array[None], (count,) + array.shape)
    return lax.all_to_all(copies, "row", split_axis=0, concat_axis=0)


def together(*values):
    return lax.optimization_barrier(values)


def owned_layout(lengths, deal, holder, rows_dev):
    starts = jnp.cumsum(lengths) - lengths
    first = deal == 2 * holder
    second = deal == 2 * holder + 1
    first_len = jnp.sum(jnp.where(first, lengths, 0))
    second_len = jnp.sum(jnp.where(second, lengths, 0))
    first_start = jnp.sum(jnp.where(first, starts, 0))
    second_start = jnp.sum(jnp.where(second, starts, 0))
    slots = jnp.arange(rows_dev, dtype=jnp.int32)
    in_first = slots < first_len
    in_second = jnp.logical_and(jnp.logical_not(in_first), slots < first_len + second_len)
    usable = jnp.logical_or(in_first, in_second)
    position = jnp.where(in_first, slots, slots - first_len)
    source = jnp.where(in_first, first_start + slots, second_start + position)
    source = jnp.where(usable, source, -1)
    segment = jnp.where(in_first, 0, jnp.where(in_second, 1, 2)).astype(jnp.int32)
    return source, usable, segment, position


def given_targets(lengths, deal, positions, rows_dev):
    starts = jnp.cumsum(lengths) - lengths
    before = deal[None, :] == (deal - 1)[:, None]
    partner_len = jnp.sum(jnp.where(before, lengths[None, :], 0), axis=1)
    offset = jnp.where(deal % 2 == 1, partner_len, 0)
    base = deal // 2 * rows_dev + offset - starts
    inside = jnp.logical_and(
        positions[:, None] >= starts[None, :], positions[:, None] < (starts + lengths)[None, :]
    )
    target = jnp.sum(jnp.where(inside, base[None, :] + positions[:, None], 0), axis=1)
    return jnp.where(jnp.any(inside, axis=1), target, -1)


def pick_rows(rows, wanted):
    onehot = (wanted[:, None] == jnp.arange(rows.shape[0], dtype=jnp.int32)[None, :]).astype(BF16)
    return nn(onehot, rows)


def normalize(hidden, gain, shift):
    average = jnp.mean(hidden, axis=1, keepdims=True)
    square = jnp.mean(hidden * hidden, axis=1, keepdims=True)
    inverse = lax.rsqrt(square - average * average + epsilon)
    centered = (hidden - average) * inverse
    return centered, inverse, (centered * gain + shift).astype(BF16)


def norm_backward(grad_norm, centered, inverse, gain):
    grad_cent = grad_norm * gain
    summed = jnp.mean(grad_cent, axis=1, keepdims=True)
    cross = jnp.mean(grad_cent * centered, axis=1, keepdims=True)
    grad_hidden = inverse * (grad_cent - summed - centered * cross)
    return grad_hidden, jnp.sum(grad_norm * centered, axis=0), jnp.sum(grad_norm, axis=0)


def gelu_tanh(values):
    return jax.nn.gelu(values, approximate=True)


def masked_scores(queries, key_rows, segment, position, slopes):
    scores = jnp.einsum(
        "qhe,khe->hqk", queries, key_rows, preferred_element_type=F32
    ) * HEAD_DIM ** (-0.5)
    distance = (position[:, None] - position[None, :]).astype(F32)
    allowed = jnp.logical_and(
        segment[:, None] == segment[None, :],
        jnp.logical_and(segment[:, None] < 2, distance >= 0),
    )
    scores = scores - slopes[:, None, None] * distance[None]
    return jnp.where(allowed[None], scores, masked_score)


def attend_forward(queries, key_rows, value_rows, segment, position, slopes):
    rows = queries.shape[0]
    scores = masked_scores(queries, key_rows, segment, position, slopes)
    highest = jnp.max(scores, axis=2, keepdims=True)
    exp_scores = jnp.exp(scores - highest)
    summed = jnp.sum(exp_scores, axis=2, keepdims=True)
    soft = (exp_scores / summed).astype(BF16)
    mixed = jnp.einsum("hqk,khe->qhe", soft, value_rows, preferred_element_type=F32)
    return mixed.reshape(rows, -1).astype(BF16), highest + jnp.log(summed)


def attend_backward(queries, key_rows, value_rows, segment, position, slopes, logsum, grad_mixed):
    scale = HEAD_DIM ** (-0.5)
    rows = queries.shape[0]
    scores = masked_scores(queries, key_rows, segment, position, slopes)
    soft = jnp.exp(scores - logsum)
    grad_prob = jnp.einsum("qhe,khe->hqk", grad_mixed, value_rows, preferred_element_type=F32)
    row_dot = jnp.sum(soft * grad_prob, axis=2, keepdims=True)
    grad_score = (soft * (grad_prob - row_dot)).astype(BF16)
    grad_query = (
        jnp.einsum("hqk,khe->qhe", grad_score, key_rows, preferred_element_type=F32) * scale
    )
    grad_key = jnp.einsum("hqk,qhe->khe", grad_score, queries, preferred_element_type=F32) * scale
    grad_value = jnp.einsum(
        "hqk,qhe->khe", soft.astype(BF16), grad_mixed, preferred_element_type=F32
    )
    return jnp.concatenate(
        [g.astype(BF16).reshape(rows, -1) for g in (grad_query, grad_key, grad_value)], axis=1
    )


def times_rows(left, weight):
    half = weight[0].shape[0]
    return nn(left[:, :half], weight[0]) + nn(left[:, half:], weight[1])


def times_rows_back(left, weight):
    return jnp.concatenate([nt(left, weight[0]), nt(left, weight[1])], axis=1)


def layer_forward(hidden, layout, weights, small):
    usable, segment, position, slopes = layout
    attn_w, up_w, down_w = weights
    width = attn_w[0].shape[1] // 4
    gain, shift, bias_q, bias_v, bias_out, bias_down, up_bias = small
    centered, inverse, normed = normalize(hidden, gain[0], shift[0])
    rows_all = spread_tokens(normed)
    rows = rows_all.shape[0]
    qkv_w = [w[:, : 3 * width] for w in attn_w]
    out_w = [w[:, 3 * width :] for w in attn_w]
    qkv = times_rows(rows_all, qkv_w)
    queries = (qkv[:, :width] + bias_q).astype(BF16).reshape(rows, -1, HEAD_DIM)
    key_rows = qkv[:, width : 2 * width].astype(BF16).reshape(rows, -1, HEAD_DIM)
    value_rows = (qkv[:, 2 * width :] + bias_v).astype(BF16).reshape(rows, -1, HEAD_DIM)
    attended, logsum = attend_forward(queries, key_rows, value_rows, segment, position, slopes)
    branch = sum_tokens(times_rows_back(attended, out_w)) + bias_out
    middle = hidden + branch
    centered_two, inverse_two, normed_two = normalize(middle, gain[1], shift[1])
    rows_two = spread_tokens(normed_two)
    upper_in = times_rows(rows_two, up_w) + up_bias
    activated = gelu_tanh(upper_in).astype(BF16)
    down_out = sum_tokens(times_rows_back(activated, down_w)) + bias_down
    result = jnp.where(usable[:, None], middle + down_out, 0.0)
    stored = (
        centered,
        inverse,
        rows_all,
        queries,
        key_rows,
        value_rows,
        logsum,
        attended,
        centered_two,
        inverse_two,
        rows_two,
        upper_in,
        activated,
    )
    return result, stored


def ffn_backward(grad_out, weights, small, stored, meanwhile):
    _, up_w, down_w = weights
    gain = small[0]
    centered_two, inverse_two, rows_two, upper_in, activated = stored[8:]
    half = up_w[0].shape[0]
    grad_down = grad_out.astype(BF16)
    down_all = spread_tokens(grad_down)
    if meanwhile:
        down_all, *meanwhile = together(down_all, *meanwhile)
    grad_act = times_rows(down_all, down_w)
    grad_upper = jax.vjp(gelu_tanh, upper_in)[1](grad_act)[0].astype(BF16)
    grad_norm = sum_tokens(times_rows_back(grad_upper, up_w))
    terms = [
        [tn(rows_two[:, part], grad_upper).astype(BF16), tn(down_all[:, part], activated).astype(BF16)]
        for part in (slice(0, half), slice(half, None))
    ]
    grad_mid, gain_two, shift_two = norm_backward(grad_norm, centered_two, inverse_two, gain[1])
    grad_mid = grad_out + grad_mid
    token_sums = [gain_two, shift_two, jnp.sum(grad_down, axis=0, dtype=F32)]
    return grad_mid, terms, token_sums, jnp.sum(grad_upper, axis=0, dtype=F32), meanwhile


def attn_backward(grad_mid, layout, weights, small, stored, meanwhile):
    usable, segment, position, slopes = layout
    attn_w = weights[0]
    width = attn_w[0].shape[1] // 4
    half = attn_w[0].shape[0]
    gain = small[0]
    centered, inverse, rows_all, queries, key_rows, value_rows, logsum, attended = stored[:8]
    qkv_w = [w[:, : 3 * width] for w in attn_w]
    out_w = [w[:, 3 * width :] for w in attn_w]
    grad_branch = grad_mid.astype(BF16)
    branch_all = spread_tokens(grad_branch)
    if meanwhile:
        branch_all, *meanwhile = together(branch_all, *meanwhile)
    grad_attended = times_rows(branch_all, out_w).astype(BF16).reshape(queries.shape)
    grad_qkv = attend_backward(
        queries, key_rows, value_rows, segment, position, slopes, logsum, grad_attended
    )
    grad_norm = sum_tokens(times_rows_back(grad_qkv, qkv_w))
    terms = [
        jnp.concatenate(
            [
                tn(rows_all[:, part], grad_qkv).astype(BF16),
                tn(branch_all[:, part], attended).astype(BF16),
            ],
            axis=1,
        )
        for part in (slice(0, half), slice(half, None))
    ]
    grad_in, gain_one, shift_one = norm_backward(grad_norm, centered, inverse, gain[0])
    token_sums = [gain_one, shift_one, jnp.sum(grad_branch, axis=0, dtype=F32)]
    qkv_sums = jnp.sum(grad_qkv, axis=0, dtype=F32)
    column_sums = jnp.concatenate([qkv_sums[:width], qkv_sums[2 * width :]])
    return grad_mid + grad_in, terms, token_sums, column_sums, meanwhile


def on_device(
    inputs,
    cotangent,
    lengths,
    deal,
    query_key_value_weight,
    out_weight,
    up_weight,
    down_weight,
    norm_gain,
    norm_shift,
    proj_bias,
    up_bias,
):
    section = lax.axis_index("section")
    holder = lax.axis_index("row")
    column = lax.axis_index("col")
    rows_count, cols_count = lax.axis_size("row"), lax.axis_size("col")
    micro_count, rows_dev, width = inputs.shape
    model = width * cols_count
    heads_dev = width // HEAD_DIM
    heads = heads_dev * cols_count
    tokens = rows_dev // cols_count
    block = model // rows_count
    half = block // 2
    is_zero = section == 0

    def pick(zero, one):
        return jnp.where(is_zero, zero, one)

    def own_first(array, axis):
        shape = array.shape
        split = array.reshape(shape[:axis] + (rows_count, 2, half) + shape[axis + 1 :])
        parts = [lax.index_in_dim(split, i, axis + 1, keepdims=False) for i in (0, 1)]
        flat = [p.reshape(shape[:axis] + (model // 2,) + shape[axis + 1 :]) for p in parts]
        return jnp.concatenate([pick(flat[0], flat[1]), pick(flat[1], flat[0])], axis=axis)

    def true_order(array, axis):
        shape = array.shape
        mine = lax.slice_in_dim(array, 0, model // 2, axis=axis)
        other = lax.slice_in_dim(array, model // 2, model, axis=axis)
        parts = [
            p.reshape(shape[:axis] + (rows_count, 1, half) + shape[axis + 1 :])
            for p in (pick(mine, other), pick(other, mine))
        ]
        return jnp.concatenate(parts, axis=axis + 1).reshape(shape)

    packed = (
        jnp.concatenate(
            [query_key_value_weight[0].reshape(block, 3 * width), out_weight[0].T], axis=1
        ),
        up_weight[0],
        down_weight[0].T,
    )
    packed = (packed[0], jnp.concatenate(packed[1:], axis=1))
    kept = [pick(w[:half], w[half:]) for w in packed]
    given = [swap_bit(pick(w[half:], w[:half]), "section", 1) for w in packed]
    halves = (
        [pick(k, g) for k, g in zip(kept, given)],
        [pick(g, k) for k, g in zip(kept, given)],
    )

    def gather_weights(pieces):
        attn = lax.all_gather(pieces[0], "row", axis=0, tiled=True)
        ffn = lax.all_gather(pieces[1], "row", axis=0, tiled=True)
        up, down = ffn[:, : ffn.shape[1] // 2], ffn[:, ffn.shape[1] // 2 :]
        return [(mine, swap_bit(mine, "section", 1)) for mine in (attn, up, down)]

    mine_small = jnp.concatenate(
        [norm_gain[0], norm_shift[0], proj_bias[0], up_bias[0].reshape(-1, width)], axis=0
    )
    all_small = lax.all_gather(mine_small, ("section", "col"), axis=0, tiled=False)
    all_small = all_small.reshape((2, cols_count) + mine_small.shape)

    def layer_small(layer):
        table = all_small[layer]
        whole = own_first(jnp.transpose(table[:, :8], (1, 0, 2)).reshape(8, model), 1)
        own = jnp.take(table, column, axis=0)
        return (
            whole[0:2],
            whole[2:4],
            own[4],
            own[5],
            whole[6],
            whole[7],
            own[8:].reshape(-1),
        )

    source, usable, segment, position = owned_layout(
        lengths[section], deal[section], holder, rows_dev
    )
    order = jnp.bitwise_xor(column, jnp.array(spread_order(), jnp.int32))

    def xor_order(values):
        return values.reshape(cols_count, tokens)[order].reshape(rows_dev)

    own_usable = usable.reshape(cols_count, tokens)[column]
    head_ids = column * heads_dev + jnp.arange(heads_dev, dtype=jnp.int32)
    slopes = jnp.exp2(-8.0 * (head_ids.astype(F32) + 1.0) / heads)
    layout = (own_usable, xor_order(segment), xor_order(position), slopes)

    def deal_rows(array):
        portion = gather_direct(pick(array[0], array[1])).reshape(-1, width)
        owned = pick_rows(portion, source).astype(BF16)
        own = lax.all_to_all(
            owned.reshape(cols_count, tokens, width), "col", split_axis=0, concat_axis=0
        )
        return own_first(jnp.transpose(own, (1, 0, 2)).reshape(tokens, model), 1)

    first_rows = deal_rows(inputs)
    weights = [gather_weights(halves[0]), gather_weights(halves[1])]
    smalls = [layer_small(0), layer_small(1)]

    hidden_zero, stored_zero = layer_forward(first_rows.astype(F32), layout, weights[0], smalls[0])
    middle_in = hidden_zero.astype(BF16)
    hidden_one, stored_one = layer_forward(
        middle_in.astype(F32), layout, weights[1], smalls[1]
    )
    last_out = hidden_one.astype(BF16)

    positions = holder * rows_dev + jnp.arange(rows_dev, dtype=jnp.int32)
    targets = given_targets(lengths[section], deal[section], positions, rows_dev)

    def by_features(own, lanes):
        parts = true_order(own.reshape(-1, model), 1).reshape(tokens, lanes, cols_count, width)
        return jnp.transpose(parts, (2, 1, 0, 3))

    both = jnp.concatenate([middle_in[:, None], last_out[:, None]], axis=1)
    both = lax.all_to_all(by_features(both, 2), "col", split_axis=0, concat_axis=0)
    both = jnp.transpose(both, (0, 2, 1, 3)).reshape(rows_dev, 2 * width)
    both = lax.all_gather(both, "row", axis=0, tiled=True)
    both = pick_rows(both, targets).astype(BF16)
    stays = pick(both[:, :width], both[:, width:])
    comes = swap_bit(pick(both[:, width:], both[:, :width]), "section", 1)
    hidden_out = jnp.stack([pick(stays, comes), pick(comes, stays)])

    extra = 16

    def rows_and_sums(grad_in, token_sums, column_sums):
        sums = true_order(jnp.stack(token_sums), 1).reshape(-1, cols_count, width)
        count = sums.shape[0]
        sums = jnp.pad(jnp.transpose(sums, (1, 0, 2)), ((0, 0), (0, extra - count), (0, 0)))
        rows = by_features(grad_in, 1)[:, 0]
        got = lax.all_to_all(
            jnp.concatenate([rows, sums.astype(BF16)], axis=1), "col", split_axis=0, concat_axis=0
        )
        sums = jnp.sum(got[:, tokens : tokens + count].astype(F32), axis=0)
        sums = jnp.concatenate([sums, jnp.concatenate(column_sums).reshape(-1, width)], axis=0)
        sums = jnp.pad(sums, ((0, extra - sums.shape[0]), (0, 0)))
        rows = jnp.concatenate([got[:, :tokens].reshape(rows_dev, width), sums.astype(BF16)], axis=0)
        all_rows = gather_direct(rows)
        picked = pick_rows(all_rows[:, :rows_dev].reshape(-1, width), targets)
        return jnp.concatenate([picked, jnp.sum(all_rows[:, rows_dev:].astype(F32), axis=0)], axis=0)

    def send_term(terms):
        return [swap_bit(t, "section", 1) for t in terms[1]]

    def add_term(terms, come):
        parts = [(m.astype(F32) + c.astype(F32)).astype(BF16) for m, c in zip(terms[0], come)]
        return jnp.concatenate(parts, axis=1) if len(parts) > 1 else parts[0]

    def reduce_rows(total):
        return lax.psum_scatter(total, "row", scatter_dimension=0, tiled=True)

    grad_one = deal_rows(cotangent).astype(F32)
    grad_mid, ffn_one, sums_a, up_sum, _ = ffn_backward(
        grad_one, weights[1], smalls[1], stored_one, []
    )
    come_ffn_one = send_term(ffn_one)
    grad_one_in, attn_one, sums_b, qv_sum, _ = attn_backward(
        grad_mid, layout, weights[1], smalls[1], stored_one, []
    )
    come_attn_one = send_term([[attn_one[0]], [attn_one[1]]])
    back_one = rows_and_sums(
        grad_one_in.astype(BF16),
        [sums_b[0], sums_a[0], sums_b[1], sums_a[1], sums_b[2], sums_a[2]],
        [qv_sum, up_sum],
    )
    grad_zero = jnp.where(own_usable[:, None], grad_one_in.astype(BF16), 0.0).astype(F32)
    grad_mid, ffn_zero, sums_a, up_sum, come_ffn_one = ffn_backward(
        grad_zero, weights[0], smalls[0], stored_zero, come_ffn_one
    )
    ffn_one = reduce_rows(add_term(ffn_one, come_ffn_one))
    come_ffn_zero = send_term(ffn_zero)
    grad_zero_in, attn_zero, sums_b, qv_sum, come_attn_one = attn_backward(
        grad_mid, layout, weights[0], smalls[0], stored_zero, come_attn_one
    )
    attn_one = reduce_rows(add_term([[attn_one[0]]], come_attn_one))
    come_attn_zero = send_term([[attn_zero[0]], [attn_zero[1]]])
    back_zero = rows_and_sums(
        grad_zero_in.astype(BF16),
        [sums_b[0], sums_a[0], sums_b[1], sums_a[1], sums_b[2], sums_a[2]],
        [qv_sum, up_sum],
    )
    ffn_zero = reduce_rows(add_term(ffn_zero, come_ffn_zero))
    attn_zero = reduce_rows(add_term([[attn_zero[0]]], come_attn_zero))

    def both_halves(zero, one):
        mine = pick(zero, one)
        other = swap_bit(pick(one, zero), "section", 1)
        return jnp.concatenate([pick(mine, other), pick(other, mine)], axis=0).astype(F32)

    ffn_grad = both_halves(ffn_zero, ffn_one)
    attn_grad = both_halves(attn_zero, attn_one)
    qkv_grad = attn_grad[:, : 3 * width].reshape(block, 3, width)
    out_grad = attn_grad[:, 3 * width :].T
    up_grad = ffn_grad[:, : ffn_grad.shape[1] // 2]
    down_grad = ffn_grad[:, ffn_grad.shape[1] // 2 :].T

    stays = pick(back_zero, back_one)
    comes = swap_bit(pick(back_one, back_zero).astype(BF16), "section", 1).astype(F32)
    kept, came = stays[:rows_dev], comes[:rows_dev]
    in_grad = jnp.stack([pick(kept, came), pick(came, kept)])
    sums = stays[rows_dev:] + comes[rows_dev:]
    bias_grad = jnp.concatenate([sums[6:8], sums[4:6]], axis=0)
    hidden_units = up_bias.shape[1]
    return (
        hidden_out[None],
        in_grad[None],
        qkv_grad[None],
        out_grad[None],
        up_grad[None],
        down_grad[None],
        sums[0:2][None],
        sums[2:4][None],
        bias_grad[None],
        sums[8 : 8 + hidden_units // width].reshape(1, hidden_units),
    )


def solution(mesh):
    placed = (
        P(None, "row", "col"),
        P(None, "row", "col"),
        P(),
        P(),
        P("section", "row", None, "col"),
        P("section", "col", "row"),
        P("section", "row", "col"),
        P("section", "col", "row"),
        P("section", None, "col"),
        P("section", None, "col"),
        P("section", None, "col"),
        P("section", "col"),
    )
    return jax.shard_map(
        on_device,
        mesh=mesh,
        in_specs=placed,
        out_specs=(
            P("section", None, "row", "col"),
            P("section", None, "row", "col"),
            P("section", "row", None, "col"),
            P("section", "col", "row"),
            P("section", "row", "col"),
            P("section", "col", "row"),
            P("section", None, "col"),
            P("section", None, "col"),
            P("section", None, "col"),
            P("section", "col"),
        ),
        check_vma=False,
    )
```

```python
import jax
import jax.numpy as jnp
from jax import lax
from jax.sharding import PartitionSpec as P

HEAD_DIM = 64
epsilon = 1e-05
masked_score = -1e30
F32 = jnp.float32
BF16 = jnp.bfloat16
PLANE = ("section", "col")


def mm(a, b, dims):
    return lax.dot_general(a, b, ((dims[0], dims[1]), ((), ())), preferred_element_type=F32)


def nn(a, b):
    return mm(a, b, ((1,), (0,)))


def nt(a, b):
    return mm(a, b, ((1,), (1,)))


def tn(a, b):
    return mm(a, b, ((0,), (0,)))


def plane_size():
    return lax.axis_size("section") * lax.axis_size("col")


def send(array, mask):
    return lax.ppermute(array, PLANE, [(i, i ^ mask) for i in range(plane_size())])


def far_masks():
    return list(range(2, plane_size(), 2))


def spread_order():
    near = [0] + far_masks()
    return near + [m ^ 1 for m in near]


def spread(own):
    near = jnp.concatenate([own] + [send(own, m) for m in far_masks()], axis=1)
    return jnp.concatenate([near, send(near, 1)], axis=1)


def sum_up(partial):
    half = partial.shape[1] // 2
    masks = far_masks()
    size = half // (len(masks) + 1)
    near = partial[:, :half] + send(partial[:, half:].astype(BF16), 1).astype(F32)
    total = near[:, :size]
    for i, m in enumerate(masks):
        total = total + send(near[:, (i + 1) * size : (i + 2) * size].astype(BF16), m).astype(F32)
    return total


def gather_direct(array):
    count = lax.axis_size("row")
    copies = jnp.broadcast_to(array[None], (count,) + array.shape)
    return lax.all_to_all(copies, "row", split_axis=0, concat_axis=0)


def owned_layout(lengths, deal, holder, rows_dev):
    starts = jnp.cumsum(lengths) - lengths
    first = deal == 2 * holder
    second = deal == 2 * holder + 1
    first_len = jnp.sum(jnp.where(first, lengths, 0))
    second_len = jnp.sum(jnp.where(second, lengths, 0))
    first_start = jnp.sum(jnp.where(first, starts, 0))
    second_start = jnp.sum(jnp.where(second, starts, 0))
    slots = jnp.arange(rows_dev, dtype=jnp.int32)
    in_first = slots < first_len
    in_second = jnp.logical_and(jnp.logical_not(in_first), slots < first_len + second_len)
    usable = jnp.logical_or(in_first, in_second)
    position = jnp.where(in_first, slots, slots - first_len)
    source = jnp.where(in_first, first_start + slots, second_start + position)
    source = jnp.where(usable, source, -1)
    segment = jnp.where(in_first, 0, jnp.where(in_second, 1, 2)).astype(jnp.int32)
    return source, usable, segment, position


def given_targets(lengths, deal, positions, rows_dev):
    starts = jnp.cumsum(lengths) - lengths
    before = deal[None, :] == (deal - 1)[:, None]
    partner_len = jnp.sum(jnp.where(before, lengths[None, :], 0), axis=1)
    offset = jnp.where(deal % 2 == 1, partner_len, 0)
    base = deal // 2 * rows_dev + offset - starts
    inside = jnp.logical_and(
        positions[:, None] >= starts[None, :], positions[:, None] < (starts + lengths)[None, :]
    )
    target = jnp.sum(jnp.where(inside, base[None, :] + positions[:, None], 0), axis=1)
    return jnp.where(jnp.any(inside, axis=1), target, -1)


def pick_rows(rows, wanted):
    onehot = (wanted[:, None] == jnp.arange(rows.shape[0], dtype=jnp.int32)[None, :]).astype(BF16)
    return nn(onehot, rows)


def normalize(hidden, gain, shift):
    average = jnp.mean(hidden, axis=-1, keepdims=True)
    square = jnp.mean(hidden * hidden, axis=-1, keepdims=True)
    inverse = lax.rsqrt(square - average * average + epsilon)
    centered = (hidden - average) * inverse
    return centered, inverse, (centered * gain + shift).astype(BF16)


def norm_backward(grad_norm, centered, inverse, gain):
    grad_cent = grad_norm * gain
    summed = jnp.mean(grad_cent, axis=-1, keepdims=True)
    cross = jnp.mean(grad_cent * centered, axis=-1, keepdims=True)
    grad_hidden = inverse * (grad_cent - summed - centered * cross)
    return grad_hidden, jnp.sum(grad_norm * centered, axis=(0, 1)), jnp.sum(grad_norm, axis=(0, 1))


def gelu_tanh(values):
    return jax.nn.gelu(values, approximate=True)


def masked_scores(queries, key_rows, segment, position, slopes):
    scores = jnp.einsum(
        "mqhe,mkhe->mhqk", queries, key_rows, preferred_element_type=F32
    ) * HEAD_DIM ** (-0.5)
    distance = (position[:, :, None] - position[:, None, :]).astype(F32)
    allowed = jnp.logical_and(
        segment[:, :, None] == segment[:, None, :],
        jnp.logical_and(segment[:, :, None] < 2, distance >= 0),
    )
    scores = scores - slopes[:, None, None] * distance[:, None]
    return jnp.where(allowed[:, None], scores, masked_score)


def attend_forward(queries, key_rows, value_rows, segment, position, slopes):
    scores = masked_scores(queries, key_rows, segment, position, slopes)
    highest = jnp.max(scores, axis=3, keepdims=True)
    exp_scores = jnp.exp(scores - highest)
    summed = jnp.sum(exp_scores, axis=3, keepdims=True)
    soft = (exp_scores / summed).astype(BF16)
    mixed = jnp.einsum("mhqk,mkhe->mqhe", soft, value_rows, preferred_element_type=F32)
    return mixed.reshape(mixed.shape[:2] + (-1,)).astype(BF16), highest + jnp.log(summed)


def attend_backward(queries, key_rows, value_rows, segment, position, slopes, logsum, grad_mixed):
    scale = HEAD_DIM ** (-0.5)
    flat = queries.shape[:2] + (-1,)
    scores = masked_scores(queries, key_rows, segment, position, slopes)
    soft = jnp.exp(scores - logsum)
    grad_prob = jnp.einsum("mqhe,mkhe->mhqk", grad_mixed, value_rows, preferred_element_type=F32)
    row_dot = jnp.sum(soft * grad_prob, axis=3, keepdims=True)
    grad_score = (soft * (grad_prob - row_dot)).astype(BF16)
    grad_query = (
        jnp.einsum("mhqk,mkhe->mqhe", grad_score, key_rows, preferred_element_type=F32) * scale
    )
    grad_key = (
        jnp.einsum("mhqk,mqhe->mkhe", grad_score, queries, preferred_element_type=F32) * scale
    )
    grad_value = jnp.einsum(
        "mhqk,mqhe->mkhe", soft.astype(BF16), grad_mixed, preferred_element_type=F32
    )
    return jnp.concatenate(
        [g.astype(BF16).reshape(flat) for g in (grad_query, grad_key, grad_value)], axis=2
    )


def rows_of(array):
    return array.reshape(-1, array.shape[-1])


def layer_forward(hidden, layout, weights, small):
    usable, segment, position, slopes = layout
    attn_w, up_w, down_w = weights
    width = attn_w.shape[1] // 4
    gain, shift, bias_q, bias_v, bias_out, bias_down, up_bias = small
    centered, inverse, normed = normalize(hidden, gain[0], shift[0])
    rows_all = spread(normed)
    micro, tokens, model = rows_all.shape
    heads = (micro, tokens, -1, HEAD_DIM)
    qkv = nn(rows_of(rows_all), attn_w[:, : 3 * width]).reshape(micro, tokens, -1)
    queries = (qkv[:, :, :width] + bias_q).astype(BF16).reshape(heads)
    key_rows = qkv[:, :, width : 2 * width].astype(BF16).reshape(heads)
    value_rows = (qkv[:, :, 2 * width :] + bias_v).astype(BF16).reshape(heads)
    attended, logsum = attend_forward(queries, key_rows, value_rows, segment, position, slopes)
    branch = sum_up(nt(rows_of(attended), attn_w[:, 3 * width :]).reshape(micro, tokens, model))
    middle = hidden + branch + bias_out
    centered_two, inverse_two, normed_two = normalize(middle, gain[1], shift[1])
    rows_two = spread(normed_two)
    upper_in = nn(rows_of(rows_two), up_w) + up_bias
    activated = gelu_tanh(upper_in).astype(BF16)
    down_out = sum_up(nt(activated, down_w).reshape(micro, tokens, model)) + bias_down
    result = jnp.where(usable[:, :, None], middle + down_out, 0.0)
    attn_stored = (centered, inverse, rows_all, queries, key_rows, value_rows, logsum, attended)
    ffn_stored = (centered_two, inverse_two, rows_two, upper_in, activated)
    return result, attn_stored, ffn_stored


def ffn_backward(grad_out, weights, small, stored):
    _, up_w, down_w = weights
    gain = small[0]
    centered, inverse, rows_two, upper_in, activated = stored
    grad_down = grad_out.astype(BF16)
    down_all = spread(grad_down)
    grad_act = nn(rows_of(down_all), down_w)
    grad_upper = jax.vjp(gelu_tanh, upper_in)[1](grad_act)[0].astype(BF16)
    grad_norm = sum_up(nt(grad_upper, up_w).reshape(down_all.shape))
    term = jnp.concatenate(
        [
            tn(rows_of(rows_two), grad_upper).astype(BF16),
            tn(rows_of(down_all), activated).astype(BF16),
        ],
        axis=1,
    )
    grad_mid, gain_sum, shift_sum = norm_backward(grad_norm, centered, inverse, gain[1])
    token_sums = [gain_sum, shift_sum, jnp.sum(grad_down, axis=(0, 1), dtype=F32)]
    return grad_out + grad_mid, term, token_sums, jnp.sum(grad_upper, axis=0, dtype=F32)


def attn_backward(grad_mid, layout, weights, small, stored):
    usable, segment, position, slopes = layout
    attn_w = weights[0]
    width = attn_w.shape[1] // 4
    gain = small[0]
    centered, inverse, rows_all, queries, key_rows, value_rows, logsum, attended = stored
    grad_branch = grad_mid.astype(BF16)
    branch_all = spread(grad_branch)
    grad_attended = nn(rows_of(branch_all), attn_w[:, 3 * width :]).astype(BF16)
    grad_qkv = attend_backward(
        queries,
        key_rows,
        value_rows,
        segment,
        position,
        slopes,
        logsum,
        grad_attended.reshape(queries.shape),
    )
    grad_qkv = rows_of(grad_qkv)
    grad_norm = sum_up(nt(grad_qkv, attn_w[:, : 3 * width]).reshape(branch_all.shape))
    term = jnp.concatenate(
        [
            tn(rows_of(rows_all), grad_qkv).astype(BF16),
            tn(rows_of(branch_all), rows_of(attended)).astype(BF16),
        ],
        axis=1,
    )
    grad_in, gain_sum, shift_sum = norm_backward(grad_norm, centered, inverse, gain[0])
    token_sums = [gain_sum, shift_sum, jnp.sum(grad_branch, axis=(0, 1), dtype=F32)]
    qkv_sums = jnp.sum(grad_qkv, axis=0, dtype=F32)
    column_sums = jnp.concatenate([qkv_sums[:width], qkv_sums[2 * width :]])
    return grad_mid + grad_in, term, token_sums, column_sums


def on_device(
    inputs,
    cotangent,
    lengths,
    deal,
    query_key_value_weight,
    out_weight,
    up_weight,
    down_weight,
    norm_gain,
    norm_shift,
    proj_bias,
    up_bias,
):
    section = lax.axis_index("section")
    holder = lax.axis_index("row")
    column = lax.axis_index("col")
    cols_count = lax.axis_size("col")
    micro_count, rows_dev, width = inputs.shape
    model = width * cols_count
    count = plane_size()
    place = section * cols_count + column
    tokens = rows_dev // count
    block = query_key_value_weight.shape[1]
    half = width // 2
    heads_dev = half // HEAD_DIM
    hidden_half = up_weight.shape[2] // 2
    is_zero = section == 0

    def pick(zero, one):
        return jnp.where(is_zero, zero, one)

    def halves(array, axis):
        size = array.shape[axis] // 2
        return (
            lax.slice_in_dim(array, 0, size, axis=axis),
            lax.slice_in_dim(array, size, 2 * size, axis=axis),
        )

    attn_parts = [
        jnp.concatenate([q.reshape(block, 3 * half), o.T], axis=1)
        for q, o in zip(halves(query_key_value_weight[0], 2), halves(out_weight[0], 0))
    ]
    ffn_parts = [
        jnp.concatenate([u, d.T], axis=1)
        for u, d in zip(halves(up_weight[0], 1), halves(down_weight[0], 0))
    ]

    def both_layers(parts):
        kept, given = pick(parts[0], parts[1]), pick(parts[1], parts[0])
        came = send(given, cols_count)
        return pick(kept, came), pick(came, kept)

    attn_pieces = both_layers(attn_parts)
    ffn_pieces = both_layers(ffn_parts)

    def gather_weights(layer):
        attn = lax.all_gather(attn_pieces[layer], "row", axis=0, tiled=True)
        ffn = lax.all_gather(ffn_pieces[layer], "row", axis=0, tiled=True)
        return attn, ffn[:, :hidden_half], ffn[:, hidden_half:]

    mine_small = jnp.concatenate(
        [norm_gain[0], norm_shift[0], proj_bias[0], up_bias[0].reshape(-1, width)], axis=0
    )
    all_small = lax.all_gather(mine_small, PLANE, axis=0, tiled=False)
    all_small = all_small.reshape((2, cols_count) + mine_small.shape)

    def layer_small(layer):
        table = all_small[layer]
        whole = jnp.transpose(table[:, :8], (1, 0, 2)).reshape(8, model)
        own = lax.dynamic_index_in_dim(table, column, axis=0, keepdims=False)
        own_half = pick(own[:, :half], own[:, half:])
        hidden = own[8:].reshape(2, hidden_half)
        return (
            whole[0:2],
            whole[2:4],
            own_half[4],
            own_half[5],
            whole[6],
            whole[7],
            pick(hidden[0], hidden[1]),
        )

    source, usable, segment, position = jax.vmap(owned_layout, (0, 0, None, None))(
        lengths, deal, holder, rows_dev
    )
    source = pick(source[0], source[1])
    order = jnp.bitwise_xor(place, jnp.array(spread_order(), jnp.int32))

    def in_spread_order(values):
        values = values.reshape(micro_count, count, tokens)
        return jnp.take(values, order, axis=1).reshape(micro_count, rows_dev)

    own_usable = lax.dynamic_index_in_dim(
        usable.reshape(micro_count, count, tokens), place, axis=1, keepdims=False
    )
    head_ids = (
        column * (2 * heads_dev) + section * heads_dev + jnp.arange(heads_dev, dtype=jnp.int32)
    )
    slopes = jnp.exp2(-8.0 * (head_ids.astype(F32) + 1.0) / (model // HEAD_DIM))
    layout = (own_usable, in_spread_order(segment), in_spread_order(position), slopes)

    def deal_rows(array):
        portion = gather_direct(pick(array[0], array[1])).reshape(-1, width)
        owned = pick_rows(portion, source).astype(BF16)
        own = lax.all_to_all(
            owned.reshape(count, tokens, width), PLANE, split_axis=0, concat_axis=0
        )
        own = own.reshape(micro_count, cols_count, tokens, width)
        return jnp.transpose(own, (0, 2, 1, 3)).reshape(micro_count, tokens, model)

    first_rows = deal_rows(inputs)
    weights = [gather_weights(0), gather_weights(1)]
    smalls = [layer_small(0), layer_small(1)]

    hidden_zero, attn_zero, ffn_zero = layer_forward(
        first_rows.astype(F32), layout, weights[0], smalls[0]
    )
    middle_in = hidden_zero.astype(BF16)
    hidden_one, attn_one, ffn_one = layer_forward(
        middle_in.astype(F32), layout, weights[1], smalls[1]
    )
    last_out = hidden_one.astype(BF16)

    positions = holder * rows_dev + jnp.arange(rows_dev, dtype=jnp.int32)
    targets = given_targets(lengths[section], deal[section], positions, rows_dev)

    def to_columns(own):
        parts = own.reshape(micro_count, tokens, cols_count, width)
        return jnp.transpose(parts, (0, 2, 1, 3)).reshape(count, tokens, width)

    both = jnp.concatenate([to_columns(middle_in), to_columns(last_out)], axis=2)
    both = lax.all_to_all(both, PLANE, split_axis=0, concat_axis=0).reshape(rows_dev, 2 * width)
    both = lax.all_gather(both, "row", axis=0, tiled=True)
    both = pick_rows(both, targets).astype(BF16)
    stays = pick(both[:, :width], both[:, width:])
    comes = send(pick(both[:, width:], both[:, :width]), cols_count)
    hidden_out = jnp.stack([pick(stays, comes), pick(comes, stays)])

    extra = 16

    def rows_and_sums(grad_in, token_sums, column_sums):
        sums = jnp.stack(token_sums).reshape(-1, cols_count, width)
        lanes = sums.shape[0]
        sums = jnp.pad(jnp.transpose(sums, (1, 0, 2)), ((0, 0), (0, extra - lanes), (0, 0)))
        sums = jnp.concatenate([sums.astype(BF16)] * micro_count, axis=0)
        got = lax.all_to_all(
            jnp.concatenate([to_columns(grad_in), sums], axis=1),
            PLANE,
            split_axis=0,
            concat_axis=0,
        )
        sums = jnp.sum(got[:, tokens : tokens + lanes].astype(F32), axis=0)
        sums = jnp.concatenate([sums, jnp.concatenate(column_sums).reshape(-1, width)], axis=0)
        sums = jnp.pad(sums, ((0, extra - sums.shape[0]), (0, 0)))
        rows = jnp.concatenate([got[:, :tokens].reshape(rows_dev, width), sums.astype(BF16)], axis=0)
        all_rows = gather_direct(rows)
        picked = pick_rows(all_rows[:, :rows_dev].reshape(-1, width), targets)
        return jnp.concatenate([picked, jnp.sum(all_rows[:, rows_dev:].astype(F32), axis=0)], axis=0)

    def reduce_rows(total):
        return lax.psum_scatter(total, "row", scatter_dimension=0, tiled=True)

    grad_one = deal_rows(cotangent).astype(F32)
    grad_mid, term, sums_a, up_sum = ffn_backward(grad_one, weights[1], smalls[1], ffn_one)
    ffn_term_one = reduce_rows(term)
    grad_one_in, term, sums_b, qv_sum = attn_backward(
        grad_mid, layout, weights[1], smalls[1], attn_one
    )
    attn_term_one = reduce_rows(term)
    grad_one_in = grad_one_in.astype(BF16)
    back_one = rows_and_sums(
        grad_one_in,
        [sums_b[0], sums_a[0], sums_b[1], sums_a[1], sums_b[2], sums_a[2]],
        [qv_sum, up_sum],
    )
    grad_zero = jnp.where(own_usable[:, :, None], grad_one_in, jnp.zeros_like(grad_one_in))
    grad_mid, term, sums_a, up_sum = ffn_backward(
        grad_zero.astype(F32), weights[0], smalls[0], ffn_zero
    )
    ffn_term_zero = reduce_rows(term)
    grad_zero_in, term, sums_b, qv_sum = attn_backward(
        grad_mid, layout, weights[0], smalls[0], attn_zero
    )
    attn_term_zero = reduce_rows(term)
    back_zero = rows_and_sums(
        grad_zero_in.astype(BF16),
        [sums_b[0], sums_a[0], sums_b[1], sums_a[1], sums_b[2], sums_a[2]],
        [qv_sum, up_sum],
    )

    def both_halves(zero, one):
        mine = pick(zero, one)
        other = send(pick(one, zero), cols_count)
        return pick(mine, other).astype(F32), pick(other, mine).astype(F32)

    attn_grad = jnp.stack(
        [g.reshape(block, 4, half) for g in both_halves(attn_term_zero, attn_term_one)], axis=2
    ).reshape(block, 4, width)
    ffn_grad = both_halves(ffn_term_zero, ffn_term_one)
    up_grad = jnp.concatenate([g[:, :hidden_half] for g in ffn_grad], axis=1)
    down_grad = jnp.concatenate([g[:, hidden_half:].T for g in ffn_grad], axis=0)

    stays = pick(back_zero, back_one)
    comes = send(pick(back_one, back_zero).astype(BF16), cols_count).astype(F32)
    kept, came = stays[:rows_dev], comes[:rows_dev]
    in_grad = jnp.stack([pick(kept, came), pick(came, kept)])
    sums = stays[rows_dev:]
    kept, came = sums[6:].reshape(-1), comes[rows_dev + 6 :].reshape(-1)
    first, second = pick(kept, came), pick(came, kept)
    bias_grad = jnp.stack(
        [
            jnp.concatenate([first[:half], second[:half]]),
            jnp.concatenate([first[half:width], second[half:width]]),
            sums[4],
            sums[5],
        ]
    )
    up_sums = jnp.concatenate(
        [first[width : width + hidden_half], second[width : width + hidden_half]]
    )
    return (
        hidden_out[None],
        in_grad[None],
        attn_grad[:, :3][None],
        attn_grad[:, 3].T[None],
        up_grad[None],
        down_grad[None],
        sums[0:2][None],
        sums[2:4][None],
        bias_grad[None],
        up_sums[None],
    )


def solution(mesh):
    placed = (
        P(None, "row", "col"),
        P(None, "row", "col"),
        P(),
        P(),
        P("section", "row", None, "col"),
        P("section", "col", "row"),
        P("section", "row", "col"),
        P("section", "col", "row"),
        P("section", None, "col"),
        P("section", None, "col"),
        P("section", None, "col"),
        P("section", "col"),
    )
    return jax.shard_map(
        on_device,
        mesh=mesh,
        in_specs=placed,
        out_specs=(
            P("section", None, "row", "col"),
            P("section", None, "row", "col"),
            P("section", "row", None, "col"),
            P("section", "col", "row"),
            P("section", "row", "col"),
            P("section", "col", "row"),
            P("section", None, "col"),
            P("section", None, "col"),
            P("section", None, "col"),
            P("section", "col"),
        ),
        check_vma=False,
    )
```

```python
import functools

import jax
import jax.numpy as jnp
from jax import lax
from jax.experimental import pallas as pl
from jax.experimental.pallas import tpu as pltpu
from jax.sharding import PartitionSpec as P

HEAD_DIM = 64
epsilon = 1e-05
far_away = 1e34
F32 = jnp.float32
BF16 = jnp.bfloat16
PLANE = ("section", "col")
ROOM = 28


def mm(a, b, dims):
    return lax.dot_general(a, b, ((dims[0], dims[1]), ((), ())), preferred_element_type=F32)


def nn(a, b):
    return mm(a, b, ((1,), (0,)))


def nt(a, b):
    return mm(a, b, ((1,), (1,)))


def tn(a, b):
    return mm(a, b, ((0,), (0,)))


def plane_size():
    return lax.axis_size("section") * lax.axis_size("col")


def send(array, mask):
    return lax.ppermute(array, PLANE, [(i, i ^ mask) for i in range(plane_size())])


def far_masks():
    return list(range(2, plane_size(), 2))


def spread_order():
    near = [0] + far_masks()
    return near + [m ^ 1 for m in near]


def spread(own):
    near = [own] + [send(own, m) for m in far_masks()]
    return near + [send(n, 1) for n in near]


def together(*values):
    return lax.optimization_barrier(values)


def gather_direct(array):
    count = lax.axis_size("row")
    copies = jnp.broadcast_to(array[None], (count,) + array.shape)
    return lax.all_to_all(copies, "row", split_axis=0, concat_axis=0)


def owned_layout(lengths, deal, holder, rows_dev):
    starts = jnp.cumsum(lengths) - lengths
    first = deal == 2 * holder
    second = deal == 2 * holder + 1
    first_len = jnp.sum(jnp.where(first, lengths, 0))
    second_len = jnp.sum(jnp.where(second, lengths, 0))
    first_start = jnp.sum(jnp.where(first, starts, 0))
    second_start = jnp.sum(jnp.where(second, starts, 0))
    slots = jnp.arange(rows_dev, dtype=jnp.int32)
    in_first = slots < first_len
    in_second = jnp.logical_and(jnp.logical_not(in_first), slots < first_len + second_len)
    usable = jnp.logical_or(in_first, in_second)
    position = jnp.where(in_first, slots, slots - first_len)
    source = jnp.where(in_first, first_start + slots, second_start + position)
    source = jnp.where(usable, source, -1)
    segment = jnp.where(in_first, 0, jnp.where(in_second, 1, 2)).astype(jnp.int32)
    return source, usable, segment, position


def given_targets(lengths, deal, positions, rows_dev):
    starts = jnp.cumsum(lengths) - lengths
    before = deal[None, :] == (deal - 1)[:, None]
    partner_len = jnp.sum(jnp.where(before, lengths[None, :], 0), axis=1)
    offset = jnp.where(deal % 2 == 1, partner_len, 0)
    base = deal // 2 * rows_dev + offset - starts
    inside = jnp.logical_and(
        positions[:, None] >= starts[None, :], positions[:, None] < (starts + lengths)[None, :]
    )
    target = jnp.sum(jnp.where(inside, base[None, :] + positions[:, None], 0), axis=1)
    return jnp.where(jnp.any(inside, axis=1), target, -1)


def pick_rows(rows, wanted):
    onehot = (wanted[:, None] == jnp.arange(rows.shape[0], dtype=jnp.int32)[None, :]).astype(BF16)
    return nn(onehot, rows)


class Moves:
    def __init__(self):
        self.loads, self.stores, self.started = {}, {}, []

    def need(self, *refs):
        for ref in refs:
            if id(ref) in self.loads:
                self.loads.pop(id(ref)).wait()

    def put(self, *refs):
        for ref in refs:
            if id(ref) in self.stores:
                copy = self.stores.pop(id(ref))
                copy.start()
                self.started.append(copy)

    def finish(self):
        for copy in self.started:
            copy.wait()


def run(kernel, outs, *args, scalars=0, scratch=(), room=10, cost=0, load=(), store=()):
    vmem, hbm, smem = [pl.BlockSpec(memory_space=m) for m in (pltpu.VMEM, pltpu.HBM, pltpu.SMEM)]
    n_in, n_out = len(args), len(outs)
    load = [i % n_in for i in load]
    buffers = [(args[i].shape, args[i].dtype) for i in load] + [outs[i] for i in store]

    def body(*refs):
        refs = list(refs)
        ins, results, rest = refs[:n_in], refs[n_in : n_in + n_out], refs[n_in + n_out :]
        own, held = rest[: len(scratch)], rest[len(scratch) : len(scratch) + len(buffers)]
        moves = Moves()
        for i, place in enumerate(load):
            copy = pltpu.make_async_copy(ins[place], held[i], rest[-1].at[i])
            copy.start()
            moves.loads[id(held[i])] = copy
            ins[place] = held[i]
        for i, place in enumerate(store, len(load)):
            copy = pltpu.make_async_copy(held[i], results[place], rest[-1].at[i])
            moves.stores[id(held[i])] = copy
            results[place] = held[i]
        kernel(moves, *ins, *results, *own)
        moves.finish()

    shapes = [pltpu.VMEM(shape, kind) for shape, kind in [*scratch, *buffers]]
    call = pl.pallas_call(
        body,
        out_shape=[
            pltpu.HBM(shape, kind) if i in store else jax.ShapeDtypeStruct(shape, kind)
            for i, (shape, kind) in enumerate(outs)
        ],
        in_specs=[
            hbm if i in load else smem if i >= n_in - scalars else vmem for i in range(n_in)
        ],
        out_specs=[hbm if i in store else vmem for i in range(n_out)],
        scratch_shapes=shapes + [pltpu.SemaphoreType.DMA((len(buffers),))] * bool(buffers),
        cost_estimate=pl.CostEstimate(flops=cost, bytes_accessed=0, transcendentals=0),
        compiler_params=pltpu.CompilerParams(vmem_limit_bytes=room * 2**20),
    )
    args = [
        pltpu.with_memory_space_constraint(a, pltpu.HBM) if i in load else a
        for i, a in enumerate(args)
    ]
    return list(call(*args))


def collect(blocks, rows_ref):
    size = blocks[0].shape[0]
    for i, block in enumerate(blocks):
        rows_ref[i * size : (i + 1) * size, :] = block[...]


def tiles(total, most=256):
    size = min(total, most)
    return [slice(i, i + size) for i in range(0, total, size)]


def norm_stats(hidden):
    average = jnp.mean(hidden, axis=1, keepdims=True)
    square = jnp.mean(hidden * hidden, axis=1, keepdims=True)
    inverse = lax.rsqrt(square - average * average + epsilon)
    return (hidden - average) * inverse, inverse


def norm_kernel(moves, hidden, gain, shift, normed):
    centered, _ = norm_stats(hidden[...].astype(F32))
    normed[...] = (centered * gain[...] + shift[...]).astype(BF16)


def add_norm_kernel(count, moves, *refs):
    parts, (hidden, bias, gain, shift, middle, normed) = refs[:count], refs[count:]
    total = bias[...] + parts[1][...].astype(F32)
    for part in parts[2:]:
        total = total + part[...].astype(F32)
    moves.need(parts[0], hidden)
    total = total + parts[0][...] + hidden[...].astype(F32)
    middle[...] = total
    moves.put(middle)
    centered, _ = norm_stats(total)
    normed[...] = (centered * gain[...] + shift[...]).astype(BF16)


def end_norm_kernel(count, moves, *refs):
    parts, (hidden, bias, gain, shift, usable, result, normed) = refs[:count], refs[count:]
    total = bias[...] + parts[1][...].astype(F32)
    for part in parts[2:]:
        total = total + part[...].astype(F32)
    moves.need(parts[0], hidden)
    total = total + parts[0][...] + hidden[...]
    rounded = jnp.where(usable[...] > 0, total, 0.0).astype(BF16)
    result[...] = rounded
    moves.put(result)
    centered, _ = norm_stats(rounded.astype(F32))
    normed[...] = (centered * gain[...] + shift[...]).astype(BF16)


def norm_back_kernel(count, moves, *refs):
    parts, rest = refs[:count], refs[count:]
    hidden, gain, grad_out, grad_in, rounded, sums = rest
    grad = parts[1][...].astype(F32)
    for part in parts[2:]:
        grad = grad + part[...].astype(F32)
    moves.need(hidden, parts[0], grad_out)
    grad = grad + parts[0][...]
    centered, inverse = norm_stats(hidden[...].astype(F32))
    grad_cent = grad * gain[...]
    mean = jnp.mean(grad_cent, axis=1, keepdims=True)
    cross = jnp.mean(grad_cent * centered, axis=1, keepdims=True)
    total = grad_out[...].astype(F32) + inverse * (grad_cent - mean - centered * cross)
    low = total.astype(BF16)
    grad_in[...] = total
    moves.put(grad_in)
    rounded[...] = low
    sums[0:1, :] = jnp.sum(grad * centered, axis=0, keepdims=True)
    sums[1:2, :] = jnp.sum(grad, axis=0, keepdims=True)
    sums[2:3, :] = jnp.sum(low.astype(F32), axis=0, keepdims=True)


def fold_kernel(moves, near, came, kept, *outs):
    size = kept.shape[0]
    kept[...] = near[:size, :].astype(F32) + came[:size, :].astype(F32)
    moves.put(kept)
    for i, out in enumerate(outs):
        part = slice((i + 1) * size, (i + 2) * size)
        out[...] = (near[part, :].astype(F32) + came[part, :].astype(F32)).astype(BF16)


def put_partial(left, weight, near, far):
    half = near.shape[0]
    for part in tiles(weight.shape[0]):
        got = nt(left, weight[part, :]).astype(BF16)
        near[:, part] = got[:half]
        far[:, part] = got[half:]


def collect_micro(micro, blocks, rows_ref):
    size = blocks[0].shape[0] // micro
    for i, block in enumerate(blocks):
        for m in range(micro):
            start = (m * len(blocks) + i) * size
            rows_ref[start : start + size, :] = block[m * size : (m + 1) * size, :]


def put_partial_micro(micro, count, left, weight, near, far):
    size = near.shape[0] * 2 // (count * micro)
    for part in tiles(weight.shape[0]):
        got = nt(left, weight[part, :]).astype(BF16)
        for i in range(count):
            out = near if i < count // 2 else far
            for m in range(micro):
                start = (i % (count // 2) * micro + m) * size
                source = (m * count + i) * size
                out[start : start + size, part] = got[source : source + size]


def attn_forward_kernel(micro, count, moves, *refs):
    blocks, rest = refs[:count], refs[count:]
    (weight, bias_q, bias_v, seg_col, pos_col, seg_row, pos_row, slopes) = rest[:8]
    rows, qkv, soft, attended, near, far, distance = rest[8:]
    collect_micro(micro, blocks, rows)
    moves.put(rows)
    width = attended.shape[1]
    heads = width // HEAD_DIM
    tokens = rows.shape[0] // micro
    full = nn(rows[...], weight[:, : 3 * width])
    queries = (full[:, :width] + bias_q[...]).astype(BF16)
    key_rows = full[:, width : 2 * width].astype(BF16)
    value_rows = (full[:, 2 * width :] + bias_v[...]).astype(BF16)
    qkv[:, :width] = queries
    qkv[:, width : 2 * width] = key_rows
    qkv[:, 2 * width :] = value_rows
    moves.put(qkv)
    values_t = value_rows.astype(F32).T.astype(BF16)
    mixed = [[] for _ in range(heads)]
    for m in range(micro):
        own = slice(m * tokens, (m + 1) * tokens)
        seg_r, pos_r, seg_c, pos_c = seg_row[m], pos_row[m], seg_col[m], pos_col[m]
        allowed = jnp.logical_and(seg_c == seg_r, jnp.logical_and(seg_r < 2, pos_r >= pos_c))
        distance[...] = jnp.where(allowed, (pos_r - pos_c).astype(F32), far_away)
        for j in range(heads):
            lanes = slice(j * HEAD_DIM, (j + 1) * HEAD_DIM)
            for part in tiles(tokens, 128):
                asking = slice(own.start + part.start, own.start + part.stop)
                scores = nt(key_rows[own, lanes], queries[asking, lanes])
                scores = scores * HEAD_DIM ** (-0.5) - slopes[j] * distance[:, part]
                highest = jnp.max(scores, axis=0, keepdims=True)
                raised = jnp.exp(scores - highest)
                weights = raised * (1.0 / jnp.sum(raised, axis=0, keepdims=True))
                weights = weights.astype(BF16)
                soft[m * heads + j, :, part] = weights
                mixed[j].append(nn(values_t[lanes, own], weights))
    mixed = [jnp.concatenate(columns, axis=1) for columns in mixed]
    out = jnp.concatenate(mixed, axis=0).T.astype(BF16)
    attended[...] = out
    moves.put(soft, attended)
    put_partial_micro(micro, count, out, weight[:, 3 * width :], near, far)


def attn_backward_kernel(micro, count, moves, *refs):
    blocks, rest = refs[:count], refs[count:]
    weight, qkv, soft = rest[:3]
    rows, grad_qkv, sums, near, far, held = rest[3:]
    collect_micro(micro, blocks, rows)
    moves.put(rows)
    width = qkv.shape[1] // 3
    heads = width // HEAD_DIM
    tokens = rows.shape[0] // micro
    scale = HEAD_DIM ** (-0.5)
    grad_attended = nn(rows[...], weight[:, 3 * width :]).astype(BF16)
    moves.need(qkv, soft)
    keys_t = qkv[:, width : 2 * width].astype(F32).T.astype(BF16)
    grads_q = [[] for _ in range(heads)]
    for m in range(micro):
        own = slice(m * tokens, (m + 1) * tokens)
        for j in range(heads):
            lanes = slice(j * HEAD_DIM, (j + 1) * HEAD_DIM)
            key_lanes = slice(width + lanes.start, width + lanes.stop)
            value_lanes = slice(2 * width + lanes.start, 2 * width + lanes.stop)
            grad_head = grad_attended[own, lanes]
            for part in tiles(tokens, 128):
                grad_prob = nt(qkv[own, value_lanes], grad_head[part, :])
                weights = soft[m * heads + j, :, part].astype(F32)
                row_dot = jnp.sum(weights * grad_prob, axis=0, keepdims=True)
                held[:, part] = (weights * (grad_prob - row_dot)).astype(BF16)
            grad_score = held[...]
            grad_key = nn(grad_score, qkv[own, lanes]) * scale
            grad_qkv[own, key_lanes] = grad_key.astype(BF16)
            grad_qkv[own, value_lanes] = nn(soft[m * heads + j], grad_head).astype(BF16)
            grads_q[j].append(nn(keys_t[lanes, own], grad_score))
    grads_q = [jnp.concatenate(columns, axis=1) for columns in grads_q]
    grad_qkv[:, :width] = (jnp.concatenate(grads_q, axis=0).T * scale).astype(BF16)
    moves.put(grad_qkv)
    sums[...] = jnp.sum(grad_qkv[...].astype(F32), axis=0, keepdims=True)
    put_partial_micro(micro, count, grad_qkv[...], weight[:, : 3 * width], near, far)


def gelu_and_slope(u):
    root = (2.0 / 3.141592653589793) ** 0.5
    square = u * u
    tanh = jnp.tanh(u * (root + (root * 0.044715) * square))
    half = 0.5 + 0.5 * tanh
    inner = root + (3.0 * root * 0.044715) * square
    return u * half, half + (0.5 * u) * (1.0 - tanh * tanh) * inner


def ffn_forward_kernel(count, moves, *refs):
    blocks, (up_w, down_w, up_bias) = refs[:count], refs[count : count + 3]
    rows, activated, slope, near, far = refs[count + 3 :]
    collect(blocks, rows)
    moves.put(rows)
    for part in tiles(up_w.shape[1]):
        u = nn(rows[...], up_w[:, part]) + up_bias[:, part]
        act, grad = gelu_and_slope(u)
        activated[:, part] = act.astype(BF16)
        slope[:, part] = grad.astype(BF16)
    moves.put(activated, slope)
    put_partial(activated[...], down_w, near, far)


def ffn_turn_kernel(micro, count, moves, *refs):
    blocks, (grads, up_w, down_w, up_bias, order) = refs[:count], refs[count : count + 5]
    rows, grad_rows, activated, grad_upper, sums, near, far = refs[count + 5 :]
    collect(blocks, rows)
    size, width = blocks[0].shape[0] // micro, grads.shape[2]
    for i in range(count):
        start = pl.multiple_of(order[i] * size, size)
        for j in range(count):
            m, column = divmod(j, count // micro)
            row = (i * micro + m) * size
            grad_rows[row : row + size, column * width : (column + 1) * width] = grads[
                j, pl.ds(start, size), :
            ]
    moves.put(rows, grad_rows)
    for part in tiles(up_w.shape[1]):
        u = nn(rows[...], up_w[:, part]) + up_bias[:, part]
        act, slope = gelu_and_slope(u)
        activated[:, part] = act.astype(BF16)
        grad = (nn(grad_rows[...], down_w[:, part]) * slope).astype(BF16)
        grad_upper[:, part] = grad
        sums[:, part] = jnp.sum(grad.astype(F32), axis=0, keepdims=True)
    moves.put(activated, grad_upper)
    put_partial(grad_upper[...], up_w, near, far)


def down_kernel(micro, moves, activated, down_w, middle, bias, order, out):
    count, _, width = out.shape
    size = middle.shape[0] // micro
    for column in range(count // micro):
        lanes = slice(column * width, (column + 1) * width)
        got = nt(activated[...], down_w[lanes, :])
        for i in range(count):
            start = pl.multiple_of(order[i] * size, size)
            for m in range(micro):
                row = (i * micro + m) * size
                part = got[row : row + size]
                if i == 0:
                    part = part + middle[m * size : (m + 1) * size, lanes] + bias[:, lanes]
                out[m * (count // micro) + column, pl.ds(start, size), :] = part.astype(BF16)


def ffn_backward_kernel(count, moves, *refs):
    blocks, (up_w, down_w, slope) = refs[:count], refs[count : count + 3]
    rows, grad_upper, sums, near, far = refs[count + 3 :]
    collect(blocks, rows)
    moves.put(rows)
    moves.need(slope)
    for part in tiles(up_w.shape[1]):
        grad = (nn(rows[...], down_w[:, part]) * slope[:, part].astype(F32)).astype(BF16)
        grad_upper[:, part] = grad
        sums[:, part] = jnp.sum(grad.astype(F32), axis=0, keepdims=True)
    moves.put(grad_upper)
    put_partial(grad_upper[...], up_w, near, far)


def sum_up(near, far, later=()):
    half, model = near.shape
    masks = far_masks()
    size = half // (len(masks) + 1)
    came = send(far, 1)
    outs = [((size, model), F32)] + [((size, model), BF16)] * len(masks)
    kept, *others = run(fold_kernel, outs, near, came, store=(0,))
    if later:
        kept, *later = together(kept, *later)
    return [kept] + [send(o, m) for o, m in zip(others, masks)], later


def attn_forward(normed, layout, weights, small):
    _, seg_col, pos_col, seg_row, pos_row, slopes = layout
    weight = weights[0]
    micro = seg_col.shape[0]
    model, width = weight.shape[0], weight.shape[1] // 4
    blocks = spread(normed)
    count, size = len(blocks), normed.shape[0]
    tokens = count * size
    heads = width // HEAD_DIM
    rows, qkv, soft, attended, near, far = run(
        functools.partial(attn_forward_kernel, micro, count),
        [
            ((tokens, model), BF16),
            ((tokens, 3 * width), BF16),
            ((micro * heads, tokens // micro, tokens // micro), BF16),
            ((tokens, width), BF16),
            ((tokens // 2, model), BF16),
            ((tokens // 2, model), BF16),
        ],
        *blocks,
        weight,
        small["bias_q"],
        small["bias_v"],
        seg_col,
        pos_col,
        seg_row,
        pos_row,
        slopes,
        scalars=1,
        scratch=[((tokens // micro, tokens // micro), F32)],
        store=(0, 1, 2, 3),
        room=ROOM,
    )
    return sum_up(near, far)[0], (rows, qkv, soft, attended)


def ffn_forward(normed, weights, small):
    _, up_w, down_w = weights
    model, hidden = up_w.shape
    blocks = spread(normed)
    count, size = len(blocks), normed.shape[0]
    tokens = count * size
    rows, activated, slope, near, far = run(
        functools.partial(ffn_forward_kernel, count),
        [
            ((tokens, model), BF16),
            ((tokens, hidden), BF16),
            ((tokens, hidden), BF16),
            ((tokens // 2, model), BF16),
            ((tokens // 2, model), BF16),
        ],
        *blocks,
        up_w,
        down_w,
        small["up_bias"],
        room=ROOM,
        store=(0, 1, 2),
    )
    return sum_up(near, far)[0], (rows, activated, slope)


def ffn_turn(normed, middle, grads, order, micro, weights, small):
    _, up_w, down_w = weights
    model, hidden = up_w.shape
    blocks = spread(normed)
    count, size = len(blocks), normed.shape[0]
    tokens = count * size
    halves = [((tokens // 2, model), BF16), ((tokens // 2, model), BF16)]
    rows, grad_rows, activated, grad_upper, sums, near, far = run(
        functools.partial(ffn_turn_kernel, micro, count),
        [
            ((tokens, model), BF16),
            ((tokens, model), BF16),
            ((tokens, hidden), BF16),
            ((tokens, hidden), BF16),
            ((1, hidden), F32),
        ]
        + halves,
        *blocks,
        grads,
        up_w,
        down_w,
        small["up_bias"],
        order,
        scalars=1,
        room=ROOM,
        store=(0, 1, 2, 3),
    )
    grad_parts, factors = sum_up(near, far, (rows, grad_upper, grad_rows, activated))
    out = run(
        functools.partial(down_kernel, micro),
        [(grads.shape, BF16)],
        factors[3],
        down_w,
        middle,
        small["bias_down"],
        order,
        scalars=1,
        room=ROOM,
    )[0]
    return grad_parts, factors, sums, out


def ffn_backward(grad_down, weights, stored):
    _, up_w, down_w = weights
    model, hidden = up_w.shape
    rows_two, activated, slope = stored
    blocks = spread(grad_down)
    count, size = len(blocks), grad_down.shape[0]
    tokens = count * size
    rows, grad_upper, sums, near, far = run(
        functools.partial(ffn_backward_kernel, count),
        [
            ((tokens, model), BF16),
            ((tokens, hidden), BF16),
            ((1, hidden), F32),
            ((tokens // 2, model), BF16),
            ((tokens // 2, model), BF16),
        ],
        *blocks,
        up_w,
        down_w,
        slope,
        room=ROOM,
        load=(-1,),
        store=(0, 1),
    )
    return *sum_up(near, far, (rows_two, grad_upper, rows, activated)), sums


def attn_backward(grad_branch, micro, weights, stored):
    weight = weights[0]
    model, width = weight.shape[0], weight.shape[1] // 4
    rows_one, qkv, soft, attended = stored
    blocks = spread(grad_branch)
    count, size = len(blocks), grad_branch.shape[0]
    tokens = count * size
    rows, grad_qkv, sums, near, far = run(
        functools.partial(attn_backward_kernel, micro, count),
        [
            ((tokens, model), BF16),
            ((tokens, 3 * width), BF16),
            ((1, 3 * width), F32),
            ((tokens // 2, model), BF16),
            ((tokens // 2, model), BF16),
        ],
        *blocks,
        weight,
        qkv,
        soft,
        scratch=[((tokens // micro, tokens // micro), BF16)],
        load=(-1, -2),
        store=(0, 1),
        room=ROOM,
    )
    return *sum_up(near, far, (rows_one, grad_qkv, rows, attended)), sums


def norm_back(parts, hidden, gain, grad_out):
    shape = hidden.shape
    return run(
        functools.partial(norm_back_kernel, len(parts)),
        [(shape, F32), (shape, BF16), ((3, shape[1]), F32)],
        *parts,
        hidden,
        gain,
        grad_out,
        load=(0, len(parts), len(parts) + 2),
        store=(0,),
    )


def weight_term(factors):
    pairs = zip(factors[0::2], factors[1::2])
    return jnp.concatenate([tn(left, right).astype(BF16) for left, right in pairs], axis=1)


def on_device(
    inputs,
    cotangent,
    lengths,
    deal,
    query_key_value_weight,
    out_weight,
    up_weight,
    down_weight,
    norm_gain,
    norm_shift,
    proj_bias,
    up_bias,
):
    section = lax.axis_index("section")
    holder = lax.axis_index("row")
    column = lax.axis_index("col")
    cols_count = lax.axis_size("col")
    micro_count, rows_dev, width = inputs.shape
    model = width * cols_count
    count = plane_size()
    place = section * cols_count + column
    tokens = rows_dev // count
    block = query_key_value_weight.shape[1]
    half = width // 2
    heads_dev = half // HEAD_DIM
    hidden_half = up_weight.shape[2] // 2
    is_zero = section == 0

    def pick(zero, one):
        return jnp.where(is_zero, zero, one)

    def halves(array, axis):
        size = array.shape[axis] // 2
        return (
            lax.slice_in_dim(array, 0, size, axis=axis),
            lax.slice_in_dim(array, size, 2 * size, axis=axis),
        )

    attn_parts = [
        jnp.concatenate([q.reshape(block, 3 * half), o.T], axis=1)
        for q, o in zip(halves(query_key_value_weight[0], 2), halves(out_weight[0], 0))
    ]
    ffn_parts = [
        jnp.concatenate([u, d.T], axis=1)
        for u, d in zip(halves(up_weight[0], 1), halves(down_weight[0], 0))
    ]

    def both_layers(parts):
        kept, given = pick(parts[0], parts[1]), pick(parts[1], parts[0])
        came = send(given, cols_count)
        return pick(kept, came), pick(came, kept)

    def gather_weights(layer):
        attn = lax.all_gather(attn_pieces[layer], "row", axis=0, tiled=True)
        ffn = lax.all_gather(ffn_pieces[layer], "row", axis=0, tiled=True)
        return attn, ffn[:, :hidden_half], ffn[:, hidden_half:]

    mine_small = jnp.concatenate(
        [norm_gain[0], norm_shift[0], proj_bias[0], up_bias[0].reshape(-1, width)], axis=0
    )
    all_small = lax.all_gather(mine_small, PLANE, axis=0, tiled=False)
    all_small = all_small.reshape((2, cols_count) + mine_small.shape)

    def layer_small(layer):
        table = all_small[layer]
        whole = jnp.transpose(table[:, :8], (1, 0, 2)).reshape(8, model)
        own = lax.dynamic_index_in_dim(table, column, axis=0, keepdims=False)
        own_half = pick(own[:, :half], own[:, half:])
        hidden = own[8:].reshape(2, hidden_half)
        return {
            "gain": (whole[0:1], whole[1:2]),
            "shift": (whole[2:3], whole[3:4]),
            "bias_q": own_half[4:5],
            "bias_v": own_half[5:6],
            "bias_out": whole[6:7],
            "bias_down": whole[7:8],
            "up_bias": pick(hidden[0:1], hidden[1:2]),
        }

    source, usable, segment, position = jax.vmap(owned_layout, (0, 0, None, None))(
        lengths, deal, holder, rows_dev
    )
    source = pick(source[0], source[1])
    order = jnp.bitwise_xor(place, jnp.array(spread_order(), jnp.int32))

    def in_spread_order(values):
        values = values.reshape(micro_count, count, tokens)
        return jnp.take(values, order, axis=1).reshape(micro_count, rows_dev)

    own_usable = lax.dynamic_index_in_dim(
        usable.reshape(micro_count, count, tokens), place, axis=1, keepdims=False
    )
    head_ids = (
        column * (2 * heads_dev) + section * heads_dev + jnp.arange(heads_dev, dtype=jnp.int32)
    )
    slopes = jnp.exp2(-8.0 * (head_ids.astype(F32) + 1.0) / (model // HEAD_DIM))
    segment, position = in_spread_order(segment), in_spread_order(position)
    own_usable = own_usable.astype(jnp.int32).reshape(-1, 1)
    layout = (
        own_usable,
        segment[:, :, None],
        position[:, :, None],
        segment[:, None],
        position[:, None],
        slopes,
    )

    def deal_rows(portion):
        return pick_rows(portion.reshape(-1, width), source).astype(BF16)

    def to_tokens(owned):
        own = lax.all_to_all(
            owned.reshape(count, tokens, width), PLANE, split_axis=0, concat_axis=0
        )
        own = own.reshape(micro_count, cols_count, tokens, width)
        return jnp.transpose(own, (0, 2, 1, 3)).reshape(micro_count * tokens, model)

    portion = gather_direct(pick(inputs[0], inputs[1]))
    attn_pieces = both_layers(attn_parts)
    ffn_pieces = both_layers(ffn_parts)
    all_small, attn_first = together(all_small, attn_pieces[0])
    attn_pieces = (attn_first, attn_pieces[1])
    portion, all_small, *ffn_pieces = together(portion, all_small, *ffn_pieces)
    first_rows = to_tokens(deal_rows(portion))
    weights = [gather_weights(0), gather_weights(1)]
    smalls = [layer_small(0), layer_small(1)]

    def to_columns(own):
        parts = own.reshape(micro_count, tokens, cols_count, width)
        return jnp.transpose(parts, (0, 2, 1, 3)).reshape(count, tokens, width)

    shape = (micro_count * tokens, model)

    def middle_norm(parts, hidden, layer):
        small = smalls[layer]
        return run(
            functools.partial(add_norm_kernel, len(parts)),
            [(shape, F32), (shape, BF16)],
            *parts,
            hidden,
            small["bias_out"],
            small["gain"][1],
            small["shift"][1],
            load=(0, len(parts)),
            store=(0,),
        )

    def end_norm(parts, middle, layer):
        small, following = smalls[layer], smalls[min(layer + 1, 1)]
        return run(
            functools.partial(end_norm_kernel, len(parts)),
            [(shape, BF16), (shape, BF16)],
            *parts,
            middle,
            small["bias_down"],
            following["gain"][0],
            following["shift"][0],
            own_usable,
            load=(0, len(parts)),
            store=(0,),
        )

    small = smalls[0]
    normed = run(norm_kernel, [(shape, BF16)], first_rows, small["gain"][0], small["shift"][0])[0]
    parts, attn_zero = attn_forward(normed, layout, weights[0], small)
    parts[0], cotangent = together(parts[0], cotangent)
    given_grads = gather_direct(pick(cotangent[0], cotangent[1]))
    middle_zero, normed = middle_norm(parts, first_rows, 0)
    parts, ffn_zero = ffn_forward(normed, weights[0], small)
    middle_in, normed = end_norm(parts, middle_zero, 0)
    normed, given_grads = together(normed, given_grads)
    given_grads = lax.all_gather(deal_rows(given_grads), PLANE)
    parts, attn_one = attn_forward(normed, layout, weights[1], smalls[1])
    hidden_zero = to_columns(middle_in)
    hidden_zero = lax.all_to_all(hidden_zero, PLANE, split_axis=0, concat_axis=0)
    parts[0], hidden_zero = together(parts[0], hidden_zero)
    hidden_zero = lax.all_gather(hidden_zero.reshape(rows_dev, width), "row", tiled=True)
    middle_one, normed = middle_norm(parts, middle_in, 1)
    normed, given_grads = together(normed, given_grads)
    grad_parts, factors, up_sums, last_out = ffn_turn(
        normed, middle_one, given_grads, order, micro_count, weights[1], smalls[1]
    )
    last_out = lax.psum_scatter(last_out, PLANE, scatter_dimension=0)
    grad_parts[0], hidden_zero = together(grad_parts[0], hidden_zero)
    cotangent_rows = factors[2][: shape[0]]
    positions = holder * rows_dev + jnp.arange(rows_dev, dtype=jnp.int32)
    targets = given_targets(lengths[section], deal[section], positions, rows_dev)

    extra = 16

    def start_return(grad_in, a, b):
        sums = jnp.stack([a[0], b[0], a[1], b[1], b[2], b[3]]).reshape(-1, cols_count, width)
        sums = jnp.pad(jnp.transpose(sums, (1, 0, 2)), ((0, 0), (0, extra - 6), (0, 0)))
        sums = jnp.concatenate([sums.astype(BF16)] * micro_count, axis=0)
        rows = jnp.concatenate([to_columns(grad_in), sums], axis=1)
        return lax.all_to_all(rows, PLANE, split_axis=0, concat_axis=0)

    def gather_return(got, qkv_sums, up_sums):
        column_sums = [qkv_sums[:half], qkv_sums[2 * half :], up_sums[0]]
        sums = jnp.sum(got[:, tokens : tokens + 6].astype(F32), axis=0)
        sums = jnp.concatenate([sums, jnp.concatenate(column_sums).reshape(-1, width)], axis=0)
        sums = jnp.pad(sums, ((0, extra - sums.shape[0]), (0, 0)))
        rows = [got[:, :tokens].reshape(rows_dev, width), sums.astype(BF16)]
        return jnp.concatenate(rows, axis=0)

    def finish_return(all_rows):
        picked = pick_rows(all_rows[:, :rows_dev].reshape(-1, width), targets)
        return jnp.concatenate([picked, jnp.sum(all_rows[:, rows_dev:].astype(F32), axis=0)], axis=0)

    def reduce_rows(total):
        return lax.psum_scatter(total, "row", scatter_dimension=0, tiled=True)

    def ffn_back(grad_parts, grad, factors, layer, middle):
        mid, low, sums = norm_back(grad_parts, middle, smalls[layer]["gain"][1], grad)
        sums = [sums[0], sums[1], sums[2], jnp.sum(grad, axis=0, dtype=F32)]
        return mid, low, sums, weight_term(factors)

    def attn_back(mid, low, layer, hidden, stored):
        parts, factors, qkv_sums = attn_backward(low, micro_count, weights[layer], stored)
        _, low, sums = norm_back(parts, hidden, smalls[layer]["gain"][0], mid)
        return low, sums, qkv_sums[0], weight_term(factors)

    mid, low, sums_b, ffn_term_one = ffn_back(grad_parts, cotangent_rows, factors, 1, middle_one)
    ffn_term_one = reduce_rows(ffn_term_one)
    grad_one, sums_a, qkv_sums, attn_term_one = attn_back(mid, low, 1, middle_in, attn_one)
    attn_term_one = reduce_rows(attn_term_one)
    back_one = start_return(grad_one, sums_a, sums_b)
    late_sums = (qkv_sums, up_sums)
    grad_zero = jnp.where(own_usable > 0, grad_one, jnp.zeros_like(grad_one))
    grad_zero, last_out = together(grad_zero, last_out)
    grad_parts, factors, up_sums = ffn_backward(grad_zero, weights[0], ffn_zero)
    mid, low, sums_b, ffn_term_zero = ffn_back(grad_parts, grad_zero, factors, 0, middle_zero)
    low, ffn_term_one, back_one = together(low, ffn_term_one, back_one)
    ffn_term_zero = reduce_rows(ffn_term_zero)
    back_one = gather_return(back_one, *late_sums)
    parts, factors, qkv_sums = attn_backward(low, micro_count, weights[0], attn_zero)
    term = weight_term(factors)
    term = lax.all_to_all(
        term.reshape(-1, block, term.shape[1]), "row", split_axis=0, concat_axis=0
    )
    parts[0], term, attn_term_one, ffn_term_zero, last_out, back_one = together(
        parts[0], term, attn_term_one, ffn_term_zero, last_out, back_one
    )
    last_out = lax.all_gather(last_out, "row", tiled=True)
    back_one = lax.all_gather(back_one, "row")
    _, grad_in, sums_a = norm_back(parts, first_rows, smalls[0]["gain"][0], mid)
    back_zero = gather_return(start_return(grad_in, sums_a, sums_b), qkv_sums[0], up_sums)
    back_zero = gather_direct(back_zero)
    back_zero, back_one = finish_return(back_zero), finish_return(back_one)
    attn_term_zero = jnp.sum(term.astype(F32), axis=0).astype(BF16)
    hidden = [pick_rows(h, targets).astype(BF16) for h in (hidden_zero, last_out)]
    stays, comes = pick(hidden[0], hidden[1]), send(pick(hidden[1], hidden[0]), cols_count)
    hidden_out = jnp.stack([pick(stays, comes), pick(comes, stays)])

    def both_halves(zero, one):
        mine = pick(zero, one)
        other = send(pick(one, zero), cols_count)
        return pick(mine, other).astype(F32), pick(other, mine).astype(F32)

    attn_grad = jnp.stack(
        [g.reshape(block, 4, half) for g in both_halves(attn_term_zero, attn_term_one)], axis=2
    ).reshape(block, 4, width)
    ffn_grad = both_halves(ffn_term_zero, ffn_term_one)
    up_grad = jnp.concatenate([g[:, :hidden_half] for g in ffn_grad], axis=1)
    down_grad = jnp.concatenate([g[:, hidden_half:].T for g in ffn_grad], axis=0)

    stays = pick(back_zero, back_one)
    comes = send(pick(back_one, back_zero).astype(BF16), cols_count).astype(F32)
    kept, came = stays[:rows_dev], comes[:rows_dev]
    in_grad = jnp.stack([pick(kept, came), pick(came, kept)])
    sums = stays[rows_dev:]
    kept, came = sums[6:].reshape(-1), comes[rows_dev + 6 :].reshape(-1)
    first, second = pick(kept, came), pick(came, kept)
    bias_grad = jnp.stack(
        [
            jnp.concatenate([first[:half], second[:half]]),
            jnp.concatenate([first[half:width], second[half:width]]),
            sums[4],
            sums[5],
        ]
    )
    up_sums = jnp.concatenate(
        [first[width : width + hidden_half], second[width : width + hidden_half]]
    )
    return (
        hidden_out[None],
        in_grad[None],
        attn_grad[:, :3][None],
        attn_grad[:, 3].T[None],
        up_grad[None],
        down_grad[None],
        sums[0:2][None],
        sums[2:4][None],
        bias_grad[None],
        up_sums[None],
    )


def solution(mesh):
    placed = (
        P(None, "row", "col"),
        P(None, "row", "col"),
        P(),
        P(),
        P("section", "row", None, "col"),
        P("section", "col", "row"),
        P("section", "row", "col"),
        P("section", "col", "row"),
        P("section", None, "col"),
        P("section", None, "col"),
        P("section", None, "col"),
        P("section", "col"),
    )
    return jax.shard_map(
        on_device,
        mesh=mesh,
        in_specs=placed,
        out_specs=(
            P("section", None, "row", "col"),
            P("section", None, "row", "col"),
            P("section", "row", None, "col"),
            P("section", "col", "row"),
            P("section", "row", "col"),
            P("section", "col", "row"),
            P("section", None, "col"),
            P("section", None, "col"),
            P("section", None, "col"),
            P("section", "col"),
        ),
        check_vma=False,
    )
```

```python
import functools

import jax
import jax.numpy as jnp
from jax import lax
from jax.experimental import pallas as pl
from jax.experimental.pallas import tpu as pltpu
from jax.sharding import PartitionSpec as P

HEAD_DIM = 64
epsilon = 1e-05
far_away = 1e34
F32 = jnp.float32
BF16 = jnp.bfloat16
PLANE = ("section", "col")
ROOM = 28
PIECES = 4
BLOCK_COST = 9200000000
TERM_COST = 5000000000
NORM_COST = 2500000000


def mm(a, b, dims):
    return lax.dot_general(a, b, ((dims[0], dims[1]), ((), ())), preferred_element_type=F32)


def nn(a, b):
    return mm(a, b, ((1,), (0,)))


def nt(a, b):
    return mm(a, b, ((1,), (1,)))


def tn(a, b):
    return mm(a, b, ((0,), (0,)))


def plane_size():
    return lax.axis_size("section") * lax.axis_size("col")


def send(array, mask):
    return lax.ppermute(array, PLANE, [(i, i ^ mask) for i in range(plane_size())])


def far_masks():
    return list(range(2, plane_size(), 2))


def spread(own):
    return [own] + [send(own, m) for m in far_masks()]


def sum_up(kept, sends, later=()):
    if later:
        kept, *later = together(kept, *later)
    return [kept] + [send(o, m) for o, m in zip(sends, far_masks())], later


def together(*values):
    return lax.optimization_barrier(values)


def gather_direct(array):
    count = lax.axis_size("row")
    copies = jnp.broadcast_to(array[None], (count,) + array.shape)
    return lax.all_to_all(copies, "row", split_axis=0, concat_axis=0)


def owned_layout(lengths, deal, holder, rows_dev):
    starts = jnp.cumsum(lengths) - lengths
    first = deal == 2 * holder
    second = deal == 2 * holder + 1
    first_len = jnp.sum(jnp.where(first, lengths, 0))
    second_len = jnp.sum(jnp.where(second, lengths, 0))
    first_start = jnp.sum(jnp.where(first, starts, 0))
    second_start = jnp.sum(jnp.where(second, starts, 0))
    slots = jnp.arange(rows_dev, dtype=jnp.int32)
    in_first = slots < first_len
    in_second = jnp.logical_and(jnp.logical_not(in_first), slots < first_len + second_len)
    usable = jnp.logical_or(in_first, in_second)
    position = jnp.where(in_first, slots, slots - first_len)
    source = jnp.where(in_first, first_start + slots, second_start + position)
    source = jnp.where(usable, source, -1)
    segment = jnp.where(in_first, 0, jnp.where(in_second, 1, 2)).astype(jnp.int32)
    return source, usable, segment, position


def given_targets(lengths, deal, positions, rows_dev):
    starts = jnp.cumsum(lengths) - lengths
    before = deal[None, :] == (deal - 1)[:, None]
    partner_len = jnp.sum(jnp.where(before, lengths[None, :], 0), axis=1)
    offset = jnp.where(deal % 2 == 1, partner_len, 0)
    base = deal // 2 * rows_dev + offset - starts
    inside = jnp.logical_and(
        positions[:, None] >= starts[None, :], positions[:, None] < (starts + lengths)[None, :]
    )
    target = jnp.sum(jnp.where(inside, base[None, :] + positions[:, None], 0), axis=1)
    return jnp.where(jnp.any(inside, axis=1), target, -1)


def pick_rows(rows, wanted):
    onehot = (wanted[:, None] == jnp.arange(rows.shape[0], dtype=jnp.int32)[None, :]).astype(BF16)
    return nn(onehot, rows)


class Moves:
    def __init__(self):
        self.loads, self.stores, self.started = {}, {}, []

    def need(self, *refs):
        for ref in refs:
            if id(ref) in self.loads:
                self.loads.pop(id(ref)).wait()

    def put(self, *refs):
        for ref in refs:
            if id(ref) in self.stores:
                copy = self.stores.pop(id(ref))
                copy.start()
                self.started.append(copy)

    def finish(self):
        for copy in self.started:
            copy.wait()


def run(kernel, outs, *args, scalars=0, scratch=(), room=10, cost=0, load=(), store=()):
    vmem, hbm, smem = [pl.BlockSpec(memory_space=m) for m in (pltpu.VMEM, pltpu.HBM, pltpu.SMEM)]
    n_in, n_out = len(args), len(outs)
    load = [i % n_in for i in load]
    buffers = [(args[i].shape, args[i].dtype) for i in load] + [outs[i] for i in store]

    def body(*refs):
        refs = list(refs)
        ins, results, rest = refs[:n_in], refs[n_in : n_in + n_out], refs[n_in + n_out :]
        own, held = rest[: len(scratch)], rest[len(scratch) : len(scratch) + len(buffers)]
        moves = Moves()
        for i, place in enumerate(load):
            copy = pltpu.make_async_copy(ins[place], held[i], rest[-1].at[i])
            copy.start()
            moves.loads[id(held[i])] = copy
            ins[place] = held[i]
        for i, place in enumerate(store, len(load)):
            copy = pltpu.make_async_copy(held[i], results[place], rest[-1].at[i])
            moves.stores[id(held[i])] = copy
            results[place] = held[i]
        kernel(moves, *ins, *results, *own)
        moves.finish()

    shapes = [pltpu.VMEM(shape, kind) for shape, kind in [*scratch, *buffers]]
    call = pl.pallas_call(
        body,
        out_shape=[
            pltpu.HBM(shape, kind) if i in store else jax.ShapeDtypeStruct(shape, kind)
            for i, (shape, kind) in enumerate(outs)
        ],
        in_specs=[
            hbm if i in load else smem if i >= n_in - scalars else vmem for i in range(n_in)
        ],
        out_specs=[hbm if i in store else vmem for i in range(n_out)],
        scratch_shapes=shapes + [pltpu.SemaphoreType.DMA((len(buffers),))] * bool(buffers),
        cost_estimate=pl.CostEstimate(flops=cost, bytes_accessed=0, transcendentals=0),
        compiler_params=pltpu.CompilerParams(vmem_limit_bytes=room * 2**20),
    )
    args = [
        pltpu.with_memory_space_constraint(a, pltpu.HBM) if i in load else a
        for i, a in enumerate(args)
    ]
    return list(call(*args))


def collect(blocks, rows_ref):
    size = blocks[0].shape[0]
    for i, block in enumerate(blocks):
        rows_ref[i * size : (i + 1) * size, :] = block[...]


def tiles(total, most=256):
    size = min(total, most)
    return [slice(i, i + size) for i in range(0, total, size)]


def norm_stats(hidden):
    average = jnp.mean(hidden, axis=1, keepdims=True)
    square = jnp.mean(hidden * hidden, axis=1, keepdims=True)
    inverse = lax.rsqrt(square - average * average + epsilon)
    return (hidden - average) * inverse, inverse


def norm_kernel(moves, hidden, gain, shift, normed):
    centered, _ = norm_stats(hidden[...].astype(F32))
    normed[...] = (centered * gain[...] + shift[...]).astype(BF16)


def add_norm_kernel(count, moves, *refs):
    parts, (hidden, bias, gain, shift, middle, normed) = refs[:count], refs[count:]
    total = bias[...] + parts[1][...].astype(F32)
    for part in parts[2:]:
        total = total + part[...].astype(F32)
    moves.need(parts[0], hidden)
    total = total + parts[0][...] + hidden[...].astype(F32)
    middle[...] = total
    moves.put(middle)
    centered, _ = norm_stats(total)
    normed[...] = (centered * gain[...] + shift[...]).astype(BF16)


def end_norm_kernel(count, moves, *refs):
    parts, (hidden, bias, gain, shift, usable, result, normed) = refs[:count], refs[count:]
    total = bias[...] + parts[1][...].astype(F32)
    for part in parts[2:]:
        total = total + part[...].astype(F32)
    moves.need(parts[0], hidden)
    total = total + parts[0][...] + hidden[...]
    rounded = jnp.where(usable[...] > 0, total, 0.0).astype(BF16)
    result[...] = rounded
    moves.put(result)
    centered, _ = norm_stats(rounded.astype(F32))
    normed[...] = (centered * gain[...] + shift[...]).astype(BF16)


def norm_back_kernel(count, moves, *refs):
    parts, rest = refs[:count], refs[count:]
    hidden, gain, grad_out, grad_in, rounded, sums = rest
    grad = parts[1][...].astype(F32)
    for part in parts[2:]:
        grad = grad + part[...].astype(F32)
    moves.need(hidden, parts[0], grad_out)
    grad = grad + parts[0][...]
    centered, inverse = norm_stats(hidden[...].astype(F32))
    grad_cent = grad * gain[...]
    mean = jnp.mean(grad_cent, axis=1, keepdims=True)
    cross = jnp.mean(grad_cent * centered, axis=1, keepdims=True)
    total = grad_out[...].astype(F32) + inverse * (grad_cent - mean - centered * cross)
    low = total.astype(BF16)
    grad_in[...] = total
    moves.put(grad_in)
    rounded[...] = low
    sums[0:1, :] = jnp.sum(grad * centered, axis=0, keepdims=True)
    sums[1:2, :] = jnp.sum(grad, axis=0, keepdims=True)
    sums[2:3, :] = jnp.sum(low.astype(F32), axis=0, keepdims=True)


class Slices:
    def __init__(self, refs):
        self.mine, *self.other = refs
        self.rows = self.mine.shape[0] // PIECES

    def times(self, left, k, columns):
        if k == 0:
            return nn(left[...], self.mine[:, columns])
        total = 0.0
        for i, piece in enumerate(self.other):
            total = total + nn(left[:, i * self.rows : (i + 1) * self.rows], piece[:, columns])
        return total

    def back(self, lefts, part, columns):
        piece = self.other[part.start // self.rows]
        inside = slice(part.start % self.rows, part.start % self.rows + part.stop - part.start)
        return nt(lefts[0], self.mine[part, columns]) + nt(lefts[1], piece[inside, columns])


def put_partial(lefts, weights, columns, kept, sends):
    size = kept.shape[0]
    for part in tiles(weights.mine.shape[0], min(256, weights.rows)):
        got = weights.back(lefts, part, columns)
        kept[:, part] = got[:size]
        for i, out in enumerate(sends):
            out[:, part] = got[(i + 1) * size : (i + 2) * size].astype(BF16)


def attn_forward_kernel(count, moves, *refs):
    blocks, rest = refs[:count], refs[count:]
    weights, rest = Slices(rest[: PIECES + 1]), rest[PIECES + 1 :]
    biases, seg_col, pos_col, seg_row, pos_row, slopes = rest[:6]
    rows, qkv, soft, attended, kept, *sends, distance = rest[6:]
    collect(blocks, rows)
    moves.put(rows)
    width = weights.mine.shape[1] // 4
    heads = width // HEAD_DIM
    tokens = rows.shape[0]
    seg_r, pos_r, seg_c, pos_c = seg_row[...], pos_row[...], seg_col[...], pos_col[...]
    allowed = jnp.logical_and(seg_c == seg_r, jnp.logical_and(seg_r < 2, pos_r >= pos_c))
    distance[...] = jnp.where(allowed, (pos_r - pos_c).astype(F32), far_away)
    lefts = []
    for k in range(2):
        base = 3 * width * k
        full = weights.times(rows, k, slice(0, 3 * width))
        queries = (full[:, :width] + biases[2 * k : 2 * k + 1, :]).astype(BF16)
        key_rows = full[:, width : 2 * width].astype(BF16)
        value_rows = (full[:, 2 * width :] + biases[2 * k + 1 : 2 * k + 2, :]).astype(BF16)
        qkv[:, base : base + width] = queries
        qkv[:, base + width : base + 2 * width] = key_rows
        qkv[:, base + 2 * width : base + 3 * width] = value_rows
        values_t = value_rows.astype(F32).T.astype(BF16)
        mixed = []
        for j in range(heads):
            lanes = slice(j * HEAD_DIM, (j + 1) * HEAD_DIM)
            columns = []
            for part in tiles(tokens, 128):
                scores = nt(key_rows[:, lanes], queries[part, lanes])
                slope = slopes[k * heads + j]
                scores = scores * HEAD_DIM ** (-0.5) - slope * distance[:, part]
                highest = jnp.max(scores, axis=0, keepdims=True)
                raised = jnp.exp(scores - highest)
                weights_t = raised * (1.0 / jnp.sum(raised, axis=0, keepdims=True))
                weights_t = weights_t.astype(BF16)
                soft[k * heads + j, :, part] = weights_t
                columns.append(nn(values_t[lanes, :], weights_t))
            mixed.append(jnp.concatenate(columns, axis=1))
        out = jnp.concatenate(mixed, axis=0).T.astype(BF16)
        attended[:, k * width : (k + 1) * width] = out
        lefts.append(out)
    moves.put(qkv, soft, attended)
    put_partial(lefts, weights, slice(3 * width, 4 * width), kept, sends)
    moves.put(kept)


def attn_backward_kernel(count, moves, *refs):
    blocks, rest = refs[:count], refs[count:]
    weights, rest = Slices(rest[: PIECES + 1]), rest[PIECES + 1 :]
    qkv, soft, rows, grad_qkv, sums, kept, *sends, held = rest
    collect(blocks, rows)
    moves.put(rows)
    width = weights.mine.shape[1] // 4
    heads = width // HEAD_DIM
    tokens = rows.shape[0]
    scale = HEAD_DIM ** (-0.5)
    outs = slice(3 * width, 4 * width)
    grads_attended = [weights.times(rows, k, outs).astype(BF16) for k in range(2)]
    moves.need(qkv, soft)
    for k in range(2):
        base = 3 * width * k
        keys_t = qkv[:, base + width : base + 2 * width].astype(F32).T.astype(BF16)
        grads_q = []
        for j in range(heads):
            lanes = slice(j * HEAD_DIM, (j + 1) * HEAD_DIM)
            query_lanes, key_lanes, value_lanes = [
                slice(base + n * width + lanes.start, base + n * width + lanes.stop)
                for n in range(3)
            ]
            grad_head = grads_attended[k][:, lanes]
            for part in tiles(tokens, 128):
                grad_prob = nt(qkv[:, value_lanes], grad_head[part, :])
                weights_t = soft[k * heads + j, :, part].astype(F32)
                row_dot = jnp.sum(weights_t * grad_prob, axis=0, keepdims=True)
                held[:, part] = (weights_t * (grad_prob - row_dot)).astype(BF16)
            grad_score = held[...]
            grad_key = nn(grad_score, qkv[:, query_lanes]) * scale
            grad_qkv[:, key_lanes] = grad_key.astype(BF16)
            grad_qkv[:, value_lanes] = nn(soft[k * heads + j], grad_head).astype(BF16)
            grads_q.append(nn(keys_t[lanes, :], grad_score))
        grad_query = jnp.concatenate(grads_q, axis=0).T * scale
        grad_qkv[:, base : base + width] = grad_query.astype(BF16)
    moves.put(grad_qkv)
    sums[...] = jnp.sum(grad_qkv[...].astype(F32), axis=0, keepdims=True)
    lefts = [grad_qkv[:, : 3 * width], grad_qkv[:, 3 * width :]]
    put_partial(lefts, weights, slice(0, 3 * width), kept, sends)
    moves.put(kept)


def gelu_and_slope(u):
    root = (2.0 / 3.141592653589793) ** 0.5
    square = u * u
    tanh = jnp.tanh(u * (root + (root * 0.044715) * square))
    half = 0.5 + 0.5 * tanh
    inner = root + (3.0 * root * 0.044715) * square
    return u * half, half + (0.5 * u) * (1.0 - tanh * tanh) * inner


def ffn_slices(weights):
    hidden = weights.mine.shape[1] // 2
    for k in range(2):
        for part in tiles(hidden):
            down = slice(hidden + part.start, hidden + part.stop)
            yield k, part, down, slice(k * hidden + part.start, k * hidden + part.stop)


def put_down(activated, weights, kept, sends):
    hidden = weights.mine.shape[1] // 2
    lefts = [activated[:, :hidden], activated[:, hidden:]]
    put_partial(lefts, weights, slice(hidden, 2 * hidden), kept, sends)


def put_up(grad_upper, weights, kept, sends):
    hidden = weights.mine.shape[1] // 2
    lefts = [grad_upper[:, :hidden], grad_upper[:, hidden:]]
    put_partial(lefts, weights, slice(0, hidden), kept, sends)


def ffn_forward_kernel(count, moves, *refs):
    blocks, rest = refs[:count], refs[count:]
    weights, rest = Slices(rest[: PIECES + 1]), rest[PIECES + 1 :]
    up_bias, rows, activated, slope, kept, *sends = rest
    collect(blocks, rows)
    moves.put(rows)
    for k, up, _, units in ffn_slices(weights):
        u = weights.times(rows, k, up) + up_bias[:, units]
        act, grad = gelu_and_slope(u)
        activated[:, units] = act.astype(BF16)
        slope[:, units] = grad.astype(BF16)
    moves.put(activated, slope)
    put_down(activated, weights, kept, sends)
    moves.put(kept)


def ffn_turn_kernel(count, moves, *refs):
    blocks, rest = refs[:count], refs[count:]
    grads, weights, rest = rest[0], Slices(rest[1 : PIECES + 2]), rest[PIECES + 2 :]
    up_bias, order, rows, grad_rows, activated, grad_upper, sums, kept, *sends = rest
    collect(blocks, rows)
    size, width = blocks[0].shape[0], grads.shape[2]
    columns = rows.shape[1] // width
    for i in range(count):
        start = pl.multiple_of(order[i] * size, size)
        for j in range(columns):
            grad_rows[i * size : (i + 1) * size, j * width : (j + 1) * width] = grads[
                j, pl.ds(start, size), :
            ]
    moves.put(rows, grad_rows)
    for k, up, down, units in ffn_slices(weights):
        u = weights.times(rows, k, up) + up_bias[:, units]
        act, slope = gelu_and_slope(u)
        activated[:, units] = act.astype(BF16)
        grad = (weights.times(grad_rows, k, down) * slope).astype(BF16)
        grad_upper[:, units] = grad
        sums[:, units] = jnp.sum(grad.astype(F32), axis=0, keepdims=True)
    moves.put(activated, grad_upper)
    put_up(grad_upper, weights, kept, sends)
    moves.put(kept)


def down_kernel(moves, activated, *refs):
    weights, (kept, *sends) = Slices(refs[: PIECES + 1]), refs[PIECES + 1 :]
    put_down(activated, weights, kept, sends)
    moves.put(kept)


def output_kernel(count, moves, *refs):
    parts, (hidden, bias, result) = refs[:count], refs[count:]
    total = bias[...] + parts[1][...].astype(F32)
    for part in parts[2:]:
        total = total + part[...].astype(F32)
    moves.need(parts[0], hidden)
    result[...] = (total + parts[0][...] + hidden[...]).astype(BF16)


def ffn_backward_kernel(count, moves, *refs):
    blocks, rest = refs[:count], refs[count:]
    weights, rest = Slices(rest[: PIECES + 1]), rest[PIECES + 1 :]
    slope, rows, grad_upper, sums, kept, *sends = rest
    collect(blocks, rows)
    moves.put(rows)
    moves.need(slope)
    for k, _, down, units in ffn_slices(weights):
        grad = weights.times(rows, k, down) * slope[:, units].astype(F32)
        grad = grad.astype(BF16)
        grad_upper[:, units] = grad
        sums[:, units] = jnp.sum(grad.astype(F32), axis=0, keepdims=True)
    moves.put(grad_upper)
    put_up(grad_upper, weights, kept, sends)
    moves.put(kept)


def by_blocks(kernel, own, outs, operands, **settings):
    blocks = spread(own)
    count = len(blocks)
    shape = own.shape
    partial = [(shape, F32)] + [(shape, BF16)] * (count - 1)
    store = settings.pop("store", ()) + (len(outs),)
    beside = settings.pop("beside", ())
    got = run(
        functools.partial(kernel, count),
        outs + partial,
        *blocks,
        *operands,
        room=ROOM,
        cost=BLOCK_COST,
        store=store,
        **settings,
    )
    kept, *beside = together(got[len(outs)], *beside)
    return got[: len(outs)], kept, got[len(outs) + 1 :], beside


def attn_forward(normed, layout, weights, small, beside=()):
    size, model = normed.shape
    tokens, width = size * (plane_size() // 2), weights[0].shape[1] // 4
    results, kept, sends, beside = by_blocks(
        attn_forward_kernel,
        normed,
        [
            ((tokens, model), BF16),
            ((tokens, 6 * width), BF16),
            ((2 * width // HEAD_DIM, tokens, tokens), BF16),
            ((tokens, 2 * width), BF16),
        ],
        [*weights, small["attn_bias"], *layout],
        scalars=1,
        scratch=[((tokens, tokens), F32)],
        store=(0, 1, 2, 3),
        beside=beside,
    )
    return sum_up(kept, sends)[0], results, beside


def ffn_forward(normed, weights, small, beside=()):
    size, model = normed.shape
    tokens, hidden = size * (plane_size() // 2), weights[0].shape[1]
    results, kept, sends, beside = by_blocks(
        ffn_forward_kernel,
        normed,
        [((tokens, model), BF16), ((tokens, hidden), BF16), ((tokens, hidden), BF16)],
        [*weights, small["up_bias"]],
        store=(0, 1, 2),
        beside=beside,
    )
    return sum_up(kept, sends)[0], results, beside


def ffn_turn(normed, grads, order, weights, small):
    size, model = normed.shape
    tokens, hidden = size * (plane_size() // 2), weights[0].shape[1]
    (rows, grad_rows, activated, grad_upper, sums), kept, sends, _ = by_blocks(
        ffn_turn_kernel,
        normed,
        [
            ((tokens, model), BF16),
            ((tokens, model), BF16),
            ((tokens, hidden), BF16),
            ((tokens, hidden), BF16),
            ((1, hidden), F32),
        ],
        [grads, *weights, small["up_bias"], order],
        scalars=1,
        store=(0, 1, 2, 3),
    )
    grad_parts, factors = sum_up(kept, sends, (rows, grad_upper, grad_rows, activated))
    kept, *sends = run(
        down_kernel,
        [(a.shape, a.dtype) for a in [kept] + sends],
        factors[3],
        *weights,
        room=ROOM,
        store=(0,),
    )
    return grad_parts, factors, sums, (kept, sends)


def ffn_backward(grad_down, weights, stored, beside=()):
    size, model = grad_down.shape
    tokens, hidden = size * (plane_size() // 2), weights[0].shape[1]
    rows_two, activated, slope = stored
    (rows, grad_upper, sums), kept, sends, beside = by_blocks(
        ffn_backward_kernel,
        grad_down,
        [((tokens, model), BF16), ((tokens, hidden), BF16), ((1, hidden), F32)],
        [*weights, slope],
        load=(-1,),
        store=(0, 1),
        beside=beside,
    )
    return *sum_up(kept, sends, (rows_two, grad_upper, rows, activated)), sums, beside


def attn_backward(grad_branch, weights, stored, beside=()):
    size, model = grad_branch.shape
    tokens, width = size * (plane_size() // 2), weights[0].shape[1] // 4
    rows_one, qkv, soft, attended = stored
    (rows, grad_qkv, sums), kept, sends, beside = by_blocks(
        attn_backward_kernel,
        grad_branch,
        [((tokens, model), BF16), ((tokens, 6 * width), BF16), ((1, 6 * width), F32)],
        [*weights, qkv, soft],
        scratch=[((tokens, tokens), BF16)],
        load=(-1, -2),
        store=(0, 1),
        beside=beside,
    )
    return *sum_up(kept, sends, (rows_one, grad_qkv, rows, attended)), sums, beside


def norm_back(parts, hidden, gain, grad_out, work=()):
    shape = hidden.shape
    hidden, *work = together(hidden, *work)
    got = run(
        functools.partial(norm_back_kernel, len(parts)),
        [(shape, F32), (shape, BF16), ((3, shape[1]), F32)],
        *parts,
        hidden,
        gain,
        grad_out,
        load=(0, len(parts), len(parts) + 2),
        store=(0,),
        cost=NORM_COST,
    )
    return *got, work


def weight_kernel(moves, first, first_grad, second, second_grad, mine, *other):
    ends = first_grad.shape[1] // 2, second_grad.shape[1] // 2
    size = mine.shape[0] // PIECES

    def put(k, part, value, columns):
        if k == 0:
            mine[part, columns] = value
        else:
            inside = slice(part.start % size, part.start % size + part.stop - part.start)
            other[part.start // size][inside, columns] = value

    for k in (1, 0):
        moves.need(first, first_grad)
        for part in tiles(first.shape[1], min(256, size)):
            grad = first_grad[:, k * ends[0] : (k + 1) * ends[0]]
            put(k, part, tn(first[:, part], grad).astype(BF16), slice(0, ends[0]))
        moves.need(second, second_grad)
        for part in tiles(second.shape[1], min(256, size)):
            grad = second_grad[:, k * ends[1] : (k + 1) * ends[1]]
            put(k, part, tn(second[:, part], grad).astype(BF16), slice(ends[0], ends[0] + ends[1]))


def weight_terms(factors):
    columns = (factors[1].shape[1] + factors[3].shape[1]) // 2
    rows = factors[0].shape[1]
    return run(
        weight_kernel,
        [((rows, columns), BF16)] + [((rows // PIECES, columns), BF16)] * PIECES,
        *factors,
        room=ROOM,
        cost=TERM_COST,
        load=(0, 1, 2, 3),
    )


def both_cores(mine, *other):
    came = jnp.concatenate([send(piece, 1) for piece in other], axis=0)
    return (mine.astype(F32) + came.astype(F32)).astype(BF16)


def on_device(
    inputs,
    cotangent,
    lengths,
    deal,
    query_key_value_weight,
    out_weight,
    up_weight,
    down_weight,
    norm_gain,
    norm_shift,
    proj_bias,
    up_bias,
):
    section = lax.axis_index("section")
    holder = lax.axis_index("row")
    column = lax.axis_index("col")
    cols_count = lax.axis_size("col")
    micro_count, rows_dev, width = inputs.shape
    model = width * cols_count
    count = plane_size()
    place = section * cols_count + column
    chips = count // 2
    tokens = rows_dev // chips
    core, chip = place % 2, place // 2
    block = query_key_value_weight.shape[1]
    half = width // 2
    heads_dev = half // HEAD_DIM
    hidden_half = up_weight.shape[2] // 2
    is_zero = section == 0

    def pick(zero, one):
        return jnp.where(is_zero, zero, one)

    def halves(array, axis):
        size = array.shape[axis] // 2
        return (
            lax.slice_in_dim(array, 0, size, axis=axis),
            lax.slice_in_dim(array, size, 2 * size, axis=axis),
        )

    attn_parts = [
        jnp.concatenate([q.reshape(block, 3 * half), o.T], axis=1)
        for q, o in zip(halves(query_key_value_weight[0], 2), halves(out_weight[0], 0))
    ]
    ffn_parts = [
        jnp.concatenate([u, d.T], axis=1)
        for u, d in zip(halves(up_weight[0], 1), halves(down_weight[0], 0))
    ]

    def both_layers(parts):
        kept, given = pick(parts[0], parts[1]), pick(parts[1], parts[0])
        came = send(given, cols_count)
        return pick(kept, came), pick(came, kept)

    def gather_slice(piece):
        return lax.all_gather(piece, "row", axis=0, tiled=True)

    def both_slices(mine):
        size = mine.shape[0] // PIECES
        return mine, *[send(mine[i * size : (i + 1) * size], 1) for i in range(PIECES)]

    mine_small = jnp.concatenate(
        [norm_gain[0], norm_shift[0], proj_bias[0], up_bias[0].reshape(-1, width)], axis=0
    )
    all_small = lax.all_gather(mine_small, PLANE, axis=0, tiled=False)
    all_small = all_small.reshape((2, cols_count) + mine_small.shape)

    def layer_small(layer):
        table = all_small[layer]
        whole = jnp.transpose(table[:, :8], (1, 0, 2)).reshape(8, model)
        slices = []
        for index in (column, jnp.bitwise_xor(column, 1)):
            own = lax.dynamic_index_in_dim(table, index, axis=0, keepdims=False)
            hidden = own[8:].reshape(2, hidden_half)
            slices.append((pick(own[:, :half], own[:, half:]), pick(hidden[0:1], hidden[1:2])))
        return {
            "gain": (whole[0:1], whole[1:2]),
            "shift": (whole[2:3], whole[3:4]),
            "attn_bias": jnp.concatenate([own[4:6] for own, _ in slices], axis=0),
            "bias_out": whole[6:7],
            "bias_down": whole[7:8],
            "up_bias": jnp.concatenate([hidden for _, hidden in slices], axis=1),
        }

    source = owned_layout(lengths[section], deal[section], holder, rows_dev)[0]
    _, usable, segment, position = owned_layout(lengths[core], deal[core], holder, rows_dev)
    order = jnp.bitwise_xor(chip, jnp.arange(chips, dtype=jnp.int32))

    def in_spread_order(values):
        return values.reshape(chips, tokens)[order].reshape(rows_dev)

    own_usable = lax.dynamic_index_in_dim(
        usable.astype(jnp.int32).reshape(chips, tokens, 1), chip, axis=0, keepdims=False
    )
    head_ids = [
        index * (2 * heads_dev) + section * heads_dev + jnp.arange(heads_dev, dtype=jnp.int32)
        for index in (column, jnp.bitwise_xor(column, 1))
    ]
    head_ids = jnp.concatenate(head_ids)
    slopes = jnp.exp2(-8.0 * (head_ids.astype(F32) + 1.0) / (model // HEAD_DIM))
    segment, position = in_spread_order(segment), in_spread_order(position)
    layout = (segment[:, None], position[:, None], segment[None], position[None], slopes)

    pairs = cols_count // 2
    trades = [(a, b) for a in range(2) for b in range(pairs)]

    def trade(array, a, b, to_worker=False):
        where = [(s, x, c) for s in range(2) for x in range(pairs) for c in range(2)]
        flat = lambda s, x, c: (s * pairs + x) * 2 + c
        ways = [(flat(s, x, c), flat(c, x ^ b, s ^ a)) for s, x, c in where]
        if to_worker:
            ways = [(to, come) for come, to in ways]
        return lax.ppermute(array, PLANE, ways)

    def at(array, index):
        return lax.dynamic_index_in_dim(array, index, axis=0, keepdims=False)

    def in_order(blocks, first, second):
        table = jnp.stack(blocks)
        return [at(table, (i ^ first) * pairs + (x ^ second)) for i in range(2) for x in range(pairs)]

    mine_x = column // 2

    def to_workers(rows):
        blocks = [trade(at(rows, (core ^ a) * pairs + (mine_x ^ b)), a, b, True) for a, b in trades]
        return by_column(blocks)

    def all_to_workers(rows):
        return [trade(rows, a, b, True) for a, b in trades]

    def by_column(blocks):
        table = jnp.stack(blocks)
        return jnp.stack(
            [at(table, ((c % 2) ^ section) * pairs + ((c // 2) ^ mine_x)) for c in range(cols_count)]
        )

    def to_dealers(rows):
        blocks = [trade(at(rows, (mine_x ^ b) * 2 + (section ^ a)), a, b) for a, b in trades]
        return jnp.stack(in_order(blocks, core, mine_x))

    def deal_rows(portion):
        return pick_rows(portion.reshape(-1, width), source).astype(BF16)

    def to_tokens(owned):
        own = to_workers(owned.reshape(chips, tokens, width))
        return jnp.transpose(own, (1, 0, 2)).reshape(tokens, model)

    portion = gather_direct(pick(inputs[0], inputs[1]))
    attn_pieces = both_layers(attn_parts)
    ffn_pieces = both_layers(ffn_parts)
    all_small, attn_first = together(all_small, attn_pieces[0])
    attn_pieces = (attn_first, attn_pieces[1])
    portion, all_small, *ffn_pieces = together(portion, all_small, *ffn_pieces)
    first_rows = to_tokens(deal_rows(portion))
    attn_w = [gather_slice(piece) for piece in attn_pieces]
    ffn_w = [gather_slice(piece) for piece in ffn_pieces]
    smalls = [layer_small(0), layer_small(1)]

    def to_columns(own):
        return jnp.transpose(own.reshape(tokens, cols_count, width), (1, 0, 2))

    shape = (tokens, model)

    def middle_norm(parts, hidden, layer, work=()):
        small = smalls[layer]
        hidden, *work = together(hidden, *work)
        got = run(
            functools.partial(add_norm_kernel, len(parts)),
            [(shape, F32), (shape, BF16)],
            *parts,
            hidden,
            small["bias_out"],
            small["gain"][1],
            small["shift"][1],
            load=(0, len(parts)),
            store=(0,),
            cost=NORM_COST,
        )
        return *got, work

    def end_norm(parts, middle, layer, work=()):
        small, following = smalls[layer], smalls[min(layer + 1, 1)]
        middle, *work = together(middle, *work)
        got = run(
            functools.partial(end_norm_kernel, len(parts)),
            [(shape, BF16), (shape, BF16)],
            *parts,
            middle,
            small["bias_down"],
            following["gain"][0],
            following["shift"][0],
            own_usable,
            load=(0, len(parts)),
            store=(0,),
            cost=NORM_COST,
        )
        return *got, work

    small = smalls[0]
    normed = run(norm_kernel, [(shape, BF16)], first_rows, small["gain"][0], small["shift"][0])[0]
    attn_w[0] = both_slices(attn_w[0])
    parts, attn_zero, (cotangent,) = attn_forward(
        normed, layout, attn_w[0], small, (cotangent,)
    )
    given_grads = gather_direct(pick(cotangent[0], cotangent[1]))
    middle_zero, normed, (ffn_w[0],) = middle_norm(parts, first_rows, 0, (ffn_w[0],))
    ffn_w[0] = both_slices(ffn_w[0])
    parts, ffn_zero, _ = ffn_forward(normed, ffn_w[0], small)
    middle_in, normed, (given_grads, attn_w[1]) = end_norm(
        parts, middle_zero, 0, (given_grads, attn_w[1])
    )
    attn_w[1] = both_slices(attn_w[1])
    given_grads = deal_rows(given_grads)
    given_grads = all_to_workers(given_grads)
    parts, attn_one, given_grads = attn_forward(
        normed, layout, attn_w[1], smalls[1], given_grads
    )
    given_grads = by_column(given_grads)
    middle_one, normed, _ = middle_norm(parts, middle_in, 1)
    ffn_w[1] = both_slices(ffn_w[1])
    grad_parts, factors, up_sums, last_out = ffn_turn(
        normed, given_grads, order, ffn_w[1], smalls[1]
    )
    cotangent_rows = factors[2][:tokens]
    positions = holder * rows_dev + jnp.arange(rows_dev, dtype=jnp.int32)
    targets = given_targets(lengths[section], deal[section], positions, rows_dev)

    extra = 16

    def start_return(grad_in, a, b, *others):
        sums = jnp.stack([a[0], b[0], a[1], b[1], b[2], b[3]]).reshape(-1, cols_count, width)
        sums = jnp.transpose(sums, (1, 0, 2)).astype(BF16)
        sums = jnp.pad(sums, ((0, 0), (0, extra - 6), (0, len(others) * width)))
        rows = jnp.concatenate([to_columns(rows) for rows in (grad_in,) + others], axis=2)
        got = to_dealers(jnp.concatenate([rows, sums], axis=1))
        sums = jnp.sum(got[:, tokens : tokens + 6, :width].astype(F32), axis=0)
        return got[:, :tokens].reshape(rows_dev, -1), sums

    def with_sums(rows, sums, qkv_sums, up_sums):
        sums_by_core = []
        for k in range(2):
            qkv = qkv_sums[0, 3 * half * k : 3 * half * (k + 1)]
            up = up_sums[0, hidden_half * k : hidden_half * (k + 1)]
            sums_by_core.append(jnp.concatenate([qkv[:half], qkv[2 * half :], up]))
        columns = sums_by_core[0] + send(sums_by_core[1], 1)
        sums = jnp.concatenate([sums, columns.reshape(-1, width)], axis=0)
        sums = jnp.pad(sums, ((0, extra - sums.shape[0]), (0, rows.shape[1] - width)))
        return jnp.concatenate([rows, sums.astype(BF16)], axis=0)

    def finish_return(held):
        picked = pick_rows(held[:, :rows_dev].reshape(-1, held.shape[2]), targets)
        return picked.astype(BF16), jnp.sum(held[:, rows_dev:, :width].astype(F32), axis=0)

    def reduce_rows(total):
        return lax.psum_scatter(total, "row", scatter_dimension=0, tiled=True)

    terms = weight_terms(factors)
    down_sum = jnp.sum(cotangent_rows, axis=0, dtype=F32)
    mid, low, sums_b, terms = norm_back(
        grad_parts, middle_one, smalls[1]["gain"][1], cotangent_rows, terms
    )
    sums_b = [*sums_b, down_sum]
    mid, *terms = together(mid, *terms)
    ffn_term_one = reduce_rows(both_cores(*terms))
    output_parts = sum_up(*last_out)[0]
    parts, factors, qkv_sums, output_parts = attn_backward(low, attn_w[1], attn_one, output_parts)
    terms = weight_terms(factors)
    _, grad_one, sums_a, terms = norm_back(parts, middle_in, smalls[1]["gain"][0], mid, terms)
    grad_one, *terms = together(grad_one, *terms)
    attn_term_one = reduce_rows(both_cores(*terms))
    last_out = run(
        functools.partial(output_kernel, len(output_parts)),
        [(shape, BF16)],
        *output_parts,
        middle_one,
        smalls[1]["bias_down"],
        load=(0, len(output_parts)),
    )[0]
    late = start_return(grad_one, sums_a, sums_b, last_out, middle_in)
    late_sums = (qkv_sums, up_sums)
    grad_zero = jnp.where(own_usable > 0, grad_one, jnp.zeros_like(grad_one))
    down_sum = jnp.sum(grad_zero, axis=0, dtype=F32)
    grad_parts, factors, up_sums, late = ffn_backward(grad_zero, ffn_w[0], ffn_zero, late)
    terms = weight_terms(factors)
    mid, low, sums_b, (ffn_term_one, *terms) = norm_back(
        grad_parts, middle_zero, smalls[0]["gain"][1], grad_zero, (ffn_term_one, *terms)
    )
    sums_b = [*sums_b, down_sum]
    late = lax.all_gather(with_sums(*late, *late_sums), "row")
    mid, *terms = together(mid, *terms)
    ffn_term_zero = reduce_rows(both_cores(*terms))
    parts, factors, qkv_sums, _ = attn_backward(low, attn_w[0], attn_zero)
    terms = weight_terms(factors)
    _, grad_in, sums_a, (attn_term_one, *terms) = norm_back(
        parts, first_rows, smalls[0]["gain"][0], mid, (attn_term_one, *terms)
    )
    attn_term_zero = both_cores(*terms)
    back_zero = with_sums(*start_return(grad_in, sums_a, sums_b), qkv_sums, up_sums)
    back_zero = gather_direct(back_zero)
    late, sums_one = finish_return(late)
    ffn_term_zero, attn_term_zero, late = together(ffn_term_zero, attn_term_zero, late)
    attn_term_zero = reduce_rows(attn_term_zero)
    back_zero, ffn_term_zero, late = together(back_zero, ffn_term_zero, late)
    back_zero, sums_zero = finish_return(back_zero)
    back_one = late[:, :width]
    hidden = late[:, 2 * width :], late[:, width : 2 * width]
    stays, comes = pick(hidden[0], hidden[1]), send(pick(hidden[1], hidden[0]), cols_count)
    hidden_out = jnp.stack([pick(stays, comes), pick(comes, stays)])

    def both_halves(zero, one):
        mine = pick(zero, one)
        other = send(pick(one, zero), cols_count)
        return pick(mine, other).astype(F32), pick(other, mine).astype(F32)

    attn_grad = jnp.stack(
        [g.reshape(block, 4, half) for g in both_halves(attn_term_zero, attn_term_one)], axis=2
    ).reshape(block, 4, width)
    ffn_grad = both_halves(ffn_term_zero, ffn_term_one)
    up_grad = jnp.concatenate([g[:, :hidden_half] for g in ffn_grad], axis=1)
    down_grad = jnp.concatenate([g[:, hidden_half:].T for g in ffn_grad], axis=0)

    given = pick(back_one, back_zero)
    given = jnp.concatenate([given, pick(sums_one, sums_zero).astype(BF16)], axis=0)
    comes = send(given, cols_count).astype(F32)
    stays, came = pick(back_zero, back_one).astype(F32), comes[:rows_dev]
    in_grad = jnp.stack([pick(stays, came), pick(came, stays)])
    sums = pick(sums_zero, sums_one)
    sums = jnp.concatenate([sums[:6] + comes[rows_dev : rows_dev + 6], sums[6:]], axis=0)
    kept, came = sums[6:].reshape(-1), comes[rows_dev + 6 :].reshape(-1)
    first, second = pick(kept, came), pick(came, kept)
    bias_grad = jnp.stack(
        [
            jnp.concatenate([first[:half], second[:half]]),
            jnp.concatenate([first[half:width], second[half:width]]),
            sums[4],
            sums[5],
        ]
    )
    up_sums = jnp.concatenate(
        [first[width : width + hidden_half], second[width : width + hidden_half]]
    )
    return (
        hidden_out[None],
        in_grad[None],
        attn_grad[:, :3][None],
        attn_grad[:, 3].T[None],
        up_grad[None],
        down_grad[None],
        sums[0:2][None],
        sums[2:4][None],
        bias_grad[None],
        up_sums[None],
    )


def solution(mesh):
    placed = (
        P(None, "row", "col"),
        P(None, "row", "col"),
        P(),
        P(),
        P("section", "row", None, "col"),
        P("section", "col", "row"),
        P("section", "row", "col"),
        P("section", "col", "row"),
        P("section", None, "col"),
        P("section", None, "col"),
        P("section", None, "col"),
        P("section", "col"),
    )
    return jax.shard_map(
        on_device,
        mesh=mesh,
        in_specs=placed,
        out_specs=(
            P("section", None, "row", "col"),
            P("section", None, "row", "col"),
            P("section", "row", None, "col"),
            P("section", "col", "row"),
            P("section", "row", "col"),
            P("section", "col", "row"),
            P("section", None, "col"),
            P("section", None, "col"),
            P("section", None, "col"),
            P("section", "col"),
        ),
        check_vma=False,
    )
```

```python
import functools

import jax
import jax.numpy as jnp
from jax import lax
from jax.experimental import pallas as pl
from jax.experimental.pallas import tpu as pltpu
from jax.sharding import PartitionSpec as P

HEAD_DIM = 64
epsilon = 1e-05
far_away = 1e34
F32 = jnp.float32
BF16 = jnp.bfloat16
PLANE = ("section", "col")
ROOM = 28
PIECES = 4
BLOCK_COST = 9200000000
TERM_COST = 5000000000
NORM_COST = 2500000000


def mm(a, b, dims):
    return lax.dot_general(a, b, ((dims[0], dims[1]), ((), ())), preferred_element_type=F32)


def nn(a, b):
    return mm(a, b, ((1,), (0,)))


def nt(a, b):
    return mm(a, b, ((1,), (1,)))


def tn(a, b):
    return mm(a, b, ((0,), (0,)))


def plane_size():
    return lax.axis_size("section") * lax.axis_size("col")


def send(array, mask):
    return lax.ppermute(array, PLANE, [(i, i ^ mask) for i in range(plane_size())])


def far_masks():
    return list(range(2, plane_size(), 2))


def spread(own):
    return [own] + [send(own, m) for m in far_masks()]


def sum_up(kept, sends, later=()):
    if later:
        kept, *later = together(kept, *later)
    return [kept] + [send(o, m) for o, m in zip(sends, far_masks())], later


def together(*values):
    return lax.optimization_barrier(values)


def gather_direct(array):
    count = lax.axis_size("row")
    copies = jnp.broadcast_to(array[None], (count,) + array.shape)
    return lax.all_to_all(copies, "row", split_axis=0, concat_axis=0)


def owned_layout(lengths, deal, holder, rows_dev):
    starts = jnp.cumsum(lengths) - lengths
    first = deal == 2 * holder
    second = deal == 2 * holder + 1
    first_len = jnp.sum(jnp.where(first, lengths, 0))
    second_len = jnp.sum(jnp.where(second, lengths, 0))
    first_start = jnp.sum(jnp.where(first, starts, 0))
    second_start = jnp.sum(jnp.where(second, starts, 0))
    slots = jnp.arange(rows_dev, dtype=jnp.int32)
    in_first = slots < first_len
    in_second = jnp.logical_and(jnp.logical_not(in_first), slots < first_len + second_len)
    usable = jnp.logical_or(in_first, in_second)
    position = jnp.where(in_first, slots, slots - first_len)
    source = jnp.where(in_first, first_start + slots, second_start + position)
    source = jnp.where(usable, source, -1)
    segment = jnp.where(in_first, 0, jnp.where(in_second, 1, 2)).astype(jnp.int32)
    return source, usable, segment, position


def given_targets(lengths, deal, positions, rows_dev):
    starts = jnp.cumsum(lengths) - lengths
    before = deal[None, :] == (deal - 1)[:, None]
    partner_len = jnp.sum(jnp.where(before, lengths[None, :], 0), axis=1)
    offset = jnp.where(deal % 2 == 1, partner_len, 0)
    base = deal // 2 * rows_dev + offset - starts
    inside = jnp.logical_and(
        positions[:, None] >= starts[None, :], positions[:, None] < (starts + lengths)[None, :]
    )
    target = jnp.sum(jnp.where(inside, base[None, :] + positions[:, None], 0), axis=1)
    return jnp.where(jnp.any(inside, axis=1), target, -1)


def pick_rows(rows, wanted):
    onehot = (wanted[:, None] == jnp.arange(rows.shape[0], dtype=jnp.int32)[None, :]).astype(BF16)
    return nn(onehot, rows)


class Moves:
    def __init__(self):
        self.loads, self.stores, self.started = {}, {}, []

    def need(self, *refs):
        for ref in refs:
            if id(ref) in self.loads:
                self.loads.pop(id(ref)).wait()

    def put(self, *refs):
        for ref in refs:
            if id(ref) in self.stores:
                copy = self.stores.pop(id(ref))
                copy.start()
                self.started.append(copy)

    def finish(self):
        for copy in self.started:
            copy.wait()


def run(kernel, outs, *args, scalars=0, scratch=(), room=10, cost=0, load=(), store=()):
    vmem, hbm, smem = [pl.BlockSpec(memory_space=m) for m in (pltpu.VMEM, pltpu.HBM, pltpu.SMEM)]
    n_in, n_out = len(args), len(outs)
    load = [i % n_in for i in load]
    buffers = [(args[i].shape, args[i].dtype) for i in load] + [outs[i] for i in store]

    def body(*refs):
        refs = list(refs)
        ins, results, rest = refs[:n_in], refs[n_in : n_in + n_out], refs[n_in + n_out :]
        own, held = rest[: len(scratch)], rest[len(scratch) : len(scratch) + len(buffers)]
        moves = Moves()
        for i, place in enumerate(load):
            copy = pltpu.make_async_copy(ins[place], held[i], rest[-1].at[i])
            copy.start()
            moves.loads[id(held[i])] = copy
            ins[place] = held[i]
        for i, place in enumerate(store, len(load)):
            copy = pltpu.make_async_copy(held[i], results[place], rest[-1].at[i])
            moves.stores[id(held[i])] = copy
            results[place] = held[i]
        kernel(moves, *ins, *results, *own)
        moves.finish()

    shapes = [pltpu.VMEM(shape, kind) for shape, kind in [*scratch, *buffers]]
    call = pl.pallas_call(
        body,
        out_shape=[
            pltpu.HBM(shape, kind) if i in store else jax.ShapeDtypeStruct(shape, kind)
            for i, (shape, kind) in enumerate(outs)
        ],
        in_specs=[
            hbm if i in load else smem if i >= n_in - scalars else vmem for i in range(n_in)
        ],
        out_specs=[hbm if i in store else vmem for i in range(n_out)],
        scratch_shapes=shapes + [pltpu.SemaphoreType.DMA((len(buffers),))] * bool(buffers),
        cost_estimate=pl.CostEstimate(flops=cost, bytes_accessed=0, transcendentals=0),
        compiler_params=pltpu.CompilerParams(vmem_limit_bytes=room * 2**20),
    )
    args = [
        pltpu.with_memory_space_constraint(a, pltpu.HBM) if i in load else a
        for i, a in enumerate(args)
    ]
    return list(call(*args))


def collect(blocks, rows_ref):
    size = blocks[0].shape[0]
    for i, block in enumerate(blocks):
        rows_ref[i * size : (i + 1) * size, :] = block[...]


def tiles(total, most=256):
    size = min(total, most)
    return [slice(i, i + size) for i in range(0, total, size)]


def norm_stats(hidden):
    average = jnp.mean(hidden, axis=1, keepdims=True)
    square = jnp.mean(hidden * hidden, axis=1, keepdims=True)
    inverse = lax.rsqrt(square - average * average + epsilon)
    return (hidden - average) * inverse, inverse


def norm_kernel(moves, hidden, gain, shift, normed):
    centered, _ = norm_stats(hidden[...].astype(F32))
    normed[...] = (centered * gain[...] + shift[...]).astype(BF16)


def add_norm_kernel(count, moves, *refs):
    parts, (hidden, bias, gain, shift, middle, normed) = refs[:count], refs[count:]
    total = bias[...] + parts[1][...].astype(F32)
    for part in parts[2:]:
        total = total + part[...].astype(F32)
    moves.need(parts[0], hidden)
    total = total + parts[0][...] + hidden[...].astype(F32)
    middle[...] = total
    moves.put(middle)
    centered, _ = norm_stats(total)
    normed[...] = (centered * gain[...] + shift[...]).astype(BF16)


def end_norm_kernel(count, moves, *refs):
    parts, (hidden, bias, gain, shift, usable, result, normed) = refs[:count], refs[count:]
    total = bias[...] + parts[1][...].astype(F32)
    for part in parts[2:]:
        total = total + part[...].astype(F32)
    moves.need(parts[0], hidden)
    total = total + parts[0][...] + hidden[...]
    rounded = jnp.where(usable[...] > 0, total, 0.0).astype(BF16)
    result[...] = rounded
    moves.put(result)
    centered, _ = norm_stats(rounded.astype(F32))
    normed[...] = (centered * gain[...] + shift[...]).astype(BF16)


def norm_back_kernel(count, moves, *refs):
    parts, rest = refs[:count], refs[count:]
    hidden, gain, grad_out, grad_in, rounded, sums = rest
    grad = parts[1][...].astype(F32)
    for part in parts[2:]:
        grad = grad + part[...].astype(F32)
    moves.need(hidden, parts[0], grad_out)
    grad = grad + parts[0][...]
    centered, inverse = norm_stats(hidden[...].astype(F32))
    grad_cent = grad * gain[...]
    mean = jnp.mean(grad_cent, axis=1, keepdims=True)
    cross = jnp.mean(grad_cent * centered, axis=1, keepdims=True)
    total = grad_out[...].astype(F32) + inverse * (grad_cent - mean - centered * cross)
    low = total.astype(BF16)
    grad_in[...] = total
    moves.put(grad_in)
    rounded[...] = low
    sums[0:1, :] = jnp.sum(grad * centered, axis=0, keepdims=True)
    sums[1:2, :] = jnp.sum(grad, axis=0, keepdims=True)
    sums[2:3, :] = jnp.sum(low.astype(F32), axis=0, keepdims=True)


class Slices:
    def __init__(self, refs):
        self.mine, *self.other = refs
        self.rows = self.mine.shape[0] // PIECES

    def times(self, left, k, columns):
        if k == 0:
            return nn(left[...], self.mine[:, columns])
        total = 0.0
        for i, piece in enumerate(self.other):
            total = total + nn(left[:, i * self.rows : (i + 1) * self.rows], piece[:, columns])
        return total

    def back(self, lefts, part, columns):
        piece = self.other[part.start // self.rows]
        inside = slice(part.start % self.rows, part.start % self.rows + part.stop - part.start)
        return nt(lefts[0], self.mine[part, columns]) + nt(lefts[1], piece[inside, columns])


def put_partial(lefts, weights, columns, kept, sends):
    size = kept.shape[0]
    for part in tiles(weights.mine.shape[0], min(256, weights.rows)):
        got = weights.back(lefts, part, columns)
        kept[:, part] = got[:size]
        for i, out in enumerate(sends):
            out[:, part] = got[(i + 1) * size : (i + 2) * size].astype(BF16)


def attn_forward_kernel(count, moves, *refs):
    blocks, rest = refs[:count], refs[count:]
    weights, rest = Slices(rest[: PIECES + 1]), rest[PIECES + 1 :]
    biases, seg_col, pos_col, seg_row, pos_row, slopes = rest[:6]
    rows, qkv, soft, attended, kept, *sends, distance = rest[6:]
    collect(blocks, rows)
    moves.put(rows)
    width = weights.mine.shape[1] // 4
    heads = width // HEAD_DIM
    tokens = rows.shape[0]
    seg_r, pos_r, seg_c, pos_c = seg_row[...], pos_row[...], seg_col[...], pos_col[...]
    allowed = jnp.logical_and(seg_c == seg_r, jnp.logical_and(seg_r < 2, pos_r >= pos_c))
    distance[...] = jnp.where(allowed, (pos_r - pos_c).astype(F32), far_away)
    lefts = []
    for k in range(2):
        base = 3 * width * k
        full = weights.times(rows, k, slice(0, 3 * width))
        queries = (full[:, :width] + biases[2 * k : 2 * k + 1, :]).astype(BF16)
        key_rows = full[:, width : 2 * width].astype(BF16)
        value_rows = (full[:, 2 * width :] + biases[2 * k + 1 : 2 * k + 2, :]).astype(BF16)
        qkv[:, base : base + width] = queries
        qkv[:, base + width : base + 2 * width] = key_rows
        qkv[:, base + 2 * width : base + 3 * width] = value_rows
        values_t = value_rows.astype(F32).T.astype(BF16)
        mixed = []
        for j in range(heads):
            lanes = slice(j * HEAD_DIM, (j + 1) * HEAD_DIM)
            columns = []
            for part in tiles(tokens, 128):
                scores = nt(key_rows[:, lanes], queries[part, lanes])
                slope = slopes[k * heads + j]
                scores = scores * HEAD_DIM ** (-0.5) - slope * distance[:, part]
                highest = jnp.max(scores, axis=0, keepdims=True)
                raised = jnp.exp(scores - highest)
                weights_t = raised * (1.0 / jnp.sum(raised, axis=0, keepdims=True))
                weights_t = weights_t.astype(BF16)
                soft[k * heads + j, :, part] = weights_t
                columns.append(nn(values_t[lanes, :], weights_t))
            mixed.append(jnp.concatenate(columns, axis=1))
        out = jnp.concatenate(mixed, axis=0).T.astype(BF16)
        attended[:, k * width : (k + 1) * width] = out
        lefts.append(out)
    moves.put(qkv, soft, attended)
    put_partial(lefts, weights, slice(3 * width, 4 * width), kept, sends)
    moves.put(kept)


def attn_backward_kernel(count, moves, *refs):
    blocks, rest = refs[:count], refs[count:]
    weights, rest = Slices(rest[: PIECES + 1]), rest[PIECES + 1 :]
    qkv, soft, rows, grad_qkv, sums, kept, *sends, held = rest
    collect(blocks, rows)
    moves.put(rows)
    width = weights.mine.shape[1] // 4
    heads = width // HEAD_DIM
    tokens = rows.shape[0]
    scale = HEAD_DIM ** (-0.5)
    outs = slice(3 * width, 4 * width)
    grads_attended = [weights.times(rows, k, outs).astype(BF16) for k in range(2)]
    moves.need(qkv, soft)
    for k in range(2):
        base = 3 * width * k
        keys_t = qkv[:, base + width : base + 2 * width].astype(F32).T.astype(BF16)
        grads_q = []
        for j in range(heads):
            lanes = slice(j * HEAD_DIM, (j + 1) * HEAD_DIM)
            query_lanes, key_lanes, value_lanes = [
                slice(base + n * width + lanes.start, base + n * width + lanes.stop)
                for n in range(3)
            ]
            grad_head = grads_attended[k][:, lanes]
            for part in tiles(tokens, 128):
                grad_prob = nt(qkv[:, value_lanes], grad_head[part, :])
                weights_t = soft[k * heads + j, :, part].astype(F32)
                row_dot = jnp.sum(weights_t * grad_prob, axis=0, keepdims=True)
                held[:, part] = (weights_t * (grad_prob - row_dot)).astype(BF16)
            grad_score = held[...]
            grad_key = nn(grad_score, qkv[:, query_lanes]) * scale
            grad_qkv[:, key_lanes] = grad_key.astype(BF16)
            grad_qkv[:, value_lanes] = nn(soft[k * heads + j], grad_head).astype(BF16)
            grads_q.append(nn(keys_t[lanes, :], grad_score))
        grad_query = jnp.concatenate(grads_q, axis=0).T * scale
        grad_qkv[:, base : base + width] = grad_query.astype(BF16)
    moves.put(grad_qkv)
    sums[...] = jnp.sum(grad_qkv[...].astype(F32), axis=0, keepdims=True)
    lefts = [grad_qkv[:, : 3 * width], grad_qkv[:, 3 * width :]]
    put_partial(lefts, weights, slice(0, 3 * width), kept, sends)
    moves.put(kept)


def gelu_and_slope(u):
    root = (2.0 / 3.141592653589793) ** 0.5
    square = u * u
    tanh = jnp.tanh(u * (root + (root * 0.044715) * square))
    half = 0.5 + 0.5 * tanh
    inner = root + (3.0 * root * 0.044715) * square
    return u * half, half + (0.5 * u) * (1.0 - tanh * tanh) * inner


def ffn_slices(weights):
    hidden = weights.mine.shape[1] // 2
    for k in range(2):
        for part in tiles(hidden):
            down = slice(hidden + part.start, hidden + part.stop)
            yield k, part, down, slice(k * hidden + part.start, k * hidden + part.stop)


def put_down(activated, weights, kept, sends):
    hidden = weights.mine.shape[1] // 2
    lefts = [activated[:, :hidden], activated[:, hidden:]]
    put_partial(lefts, weights, slice(hidden, 2 * hidden), kept, sends)


def put_up(grad_upper, weights, kept, sends):
    hidden = weights.mine.shape[1] // 2
    lefts = [grad_upper[:, :hidden], grad_upper[:, hidden:]]
    put_partial(lefts, weights, slice(0, hidden), kept, sends)


def ffn_forward_kernel(count, moves, *refs):
    blocks, rest = refs[:count], refs[count:]
    weights, rest = Slices(rest[: PIECES + 1]), rest[PIECES + 1 :]
    up_bias, rows, activated, slope, kept, *sends = rest
    collect(blocks, rows)
    moves.put(rows)
    for k, up, _, units in ffn_slices(weights):
        u = weights.times(rows, k, up) + up_bias[:, units]
        act, grad = gelu_and_slope(u)
        activated[:, units] = act.astype(BF16)
        slope[:, units] = grad.astype(BF16)
    moves.put(activated, slope)
    put_down(activated, weights, kept, sends)
    moves.put(kept)


def ffn_turn_kernel(count, moves, *refs):
    blocks, rest = refs[:count], refs[count:]
    grads, weights, rest = rest[0], Slices(rest[1 : PIECES + 2]), rest[PIECES + 2 :]
    up_bias, order, rows, grad_rows, activated, grad_upper, sums, kept, *sends = rest
    collect(blocks, rows)
    size, width = blocks[0].shape[0], grads.shape[2]
    columns = rows.shape[1] // width
    for i in range(count):
        start = pl.multiple_of(order[i] * size, size)
        for j in range(columns):
            grad_rows[i * size : (i + 1) * size, j * width : (j + 1) * width] = grads[
                j, pl.ds(start, size), :
            ]
    moves.put(rows, grad_rows)
    for k, up, down, units in ffn_slices(weights):
        u = weights.times(rows, k, up) + up_bias[:, units]
        act, slope = gelu_and_slope(u)
        activated[:, units] = act.astype(BF16)
        grad = (weights.times(grad_rows, k, down) * slope).astype(BF16)
        grad_upper[:, units] = grad
        sums[:, units] = jnp.sum(grad.astype(F32), axis=0, keepdims=True)
    moves.put(activated, grad_upper)
    put_up(grad_upper, weights, kept, sends)
    moves.put(kept)


def down_kernel(moves, activated, *refs):
    weights, (kept, *sends) = Slices(refs[: PIECES + 1]), refs[PIECES + 1 :]
    put_down(activated, weights, kept, sends)
    moves.put(kept)


def output_kernel(count, moves, *refs):
    parts, (hidden, bias, result) = refs[:count], refs[count:]
    total = bias[...] + parts[1][...].astype(F32)
    for part in parts[2:]:
        total = total + part[...].astype(F32)
    moves.need(parts[0], hidden)
    result[...] = (total + parts[0][...] + hidden[...]).astype(BF16)


def ffn_backward_kernel(count, moves, *refs):
    blocks, rest = refs[:count], refs[count:]
    weights, rest = Slices(rest[: PIECES + 1]), rest[PIECES + 1 :]
    slope, rows, grad_upper, sums, kept, *sends = rest
    collect(blocks, rows)
    moves.put(rows)
    moves.need(slope)
    for k, _, down, units in ffn_slices(weights):
        grad = weights.times(rows, k, down) * slope[:, units].astype(F32)
        grad = grad.astype(BF16)
        grad_upper[:, units] = grad
        sums[:, units] = jnp.sum(grad.astype(F32), axis=0, keepdims=True)
    moves.put(grad_upper)
    put_up(grad_upper, weights, kept, sends)
    moves.put(kept)


def by_blocks(kernel, own, outs, operands, **settings):
    blocks = spread(own)
    count = len(blocks)
    shape = own.shape
    partial = [(shape, F32)] + [(shape, BF16)] * (count - 1)
    store = settings.pop("store", ()) + (len(outs),)
    beside = settings.pop("beside", ())
    got = run(
        functools.partial(kernel, count),
        outs + partial,
        *blocks,
        *operands,
        room=ROOM,
        cost=BLOCK_COST,
        store=store,
        **settings,
    )
    kept, *beside = together(got[len(outs)], *beside)
    return got[: len(outs)], kept, got[len(outs) + 1 :], beside


def attn_forward(normed, layout, weights, small, beside=()):
    size, model = normed.shape
    tokens, width = size * (plane_size() // 2), weights[0].shape[1] // 4
    results, kept, sends, beside = by_blocks(
        attn_forward_kernel,
        normed,
        [
            ((tokens, model), BF16),
            ((tokens, 6 * width), BF16),
            ((2 * width // HEAD_DIM, tokens, tokens), BF16),
            ((tokens, 2 * width), BF16),
        ],
        [*weights, small["attn_bias"], *layout],
        scalars=1,
        scratch=[((tokens, tokens), F32)],
        store=(0, 1, 2, 3),
        beside=beside,
    )
    return sum_up(kept, sends)[0], results, beside


def ffn_forward(normed, weights, small, beside=()):
    size, model = normed.shape
    tokens, hidden = size * (plane_size() // 2), weights[0].shape[1]
    results, kept, sends, beside = by_blocks(
        ffn_forward_kernel,
        normed,
        [((tokens, model), BF16), ((tokens, hidden), BF16), ((tokens, hidden), BF16)],
        [*weights, small["up_bias"]],
        store=(0, 1, 2),
        beside=beside,
    )
    return sum_up(kept, sends)[0], results, beside


def ffn_turn(normed, grads, order, weights, small):
    size, model = normed.shape
    tokens, hidden = size * (plane_size() // 2), weights[0].shape[1]
    (rows, grad_rows, activated, grad_upper, sums), kept, sends, _ = by_blocks(
        ffn_turn_kernel,
        normed,
        [
            ((tokens, model), BF16),
            ((tokens, model), BF16),
            ((tokens, hidden), BF16),
            ((tokens, hidden), BF16),
            ((1, hidden), F32),
        ],
        [grads, *weights, small["up_bias"], order],
        scalars=1,
        store=(0, 1, 2, 3),
    )
    grad_parts, factors = sum_up(kept, sends, (rows, grad_upper, grad_rows, activated))
    kept, *sends = run(
        down_kernel,
        [(a.shape, a.dtype) for a in [kept] + sends],
        factors[3],
        *weights,
        room=ROOM,
        store=(0,),
    )
    return grad_parts, factors, sums, (kept, sends)


def ffn_backward(grad_down, weights, stored, beside=()):
    size, model = grad_down.shape
    tokens, hidden = size * (plane_size() // 2), weights[0].shape[1]
    rows_two, activated, slope = stored
    (rows, grad_upper, sums), kept, sends, beside = by_blocks(
        ffn_backward_kernel,
        grad_down,
        [((tokens, model), BF16), ((tokens, hidden), BF16), ((1, hidden), F32)],
        [*weights, slope],
        load=(-1,),
        store=(0, 1),
        beside=beside,
    )
    return *sum_up(kept, sends, (rows_two, grad_upper, rows, activated)), sums, beside


def attn_backward(grad_branch, weights, stored, beside=()):
    size, model = grad_branch.shape
    tokens, width = size * (plane_size() // 2), weights[0].shape[1] // 4
    rows_one, qkv, soft, attended = stored
    (rows, grad_qkv, sums), kept, sends, beside = by_blocks(
        attn_backward_kernel,
        grad_branch,
        [((tokens, model), BF16), ((tokens, 6 * width), BF16), ((1, 6 * width), F32)],
        [*weights, qkv, soft],
        scratch=[((tokens, tokens), BF16)],
        load=(-1, -2),
        store=(0, 1),
        beside=beside,
    )
    return *sum_up(kept, sends, (rows_one, grad_qkv, rows, attended)), sums, beside


def norm_back(parts, hidden, gain, grad_out, work=()):
    shape = hidden.shape
    hidden, *work = together(hidden, *work)
    got = run(
        functools.partial(norm_back_kernel, len(parts)),
        [(shape, F32), (shape, BF16), ((3, shape[1]), F32)],
        *parts,
        hidden,
        gain,
        grad_out,
        load=(0, len(parts), len(parts) + 2),
        store=(0,),
        cost=NORM_COST,
    )
    return *got, work


def weight_kernel(moves, first, first_grad, second, second_grad, mine, *other):
    ends = first_grad.shape[1] // 2, second_grad.shape[1] // 2
    size = mine.shape[0] // PIECES

    def put(k, part, value, columns):
        if k == 0:
            mine[part, columns] = value
        else:
            inside = slice(part.start % size, part.start % size + part.stop - part.start)
            other[part.start // size][inside, columns] = value

    for k in (1, 0):
        moves.need(first, first_grad)
        for part in tiles(first.shape[1], min(256, size)):
            grad = first_grad[:, k * ends[0] : (k + 1) * ends[0]]
            put(k, part, tn(first[:, part], grad).astype(BF16), slice(0, ends[0]))
        moves.need(second, second_grad)
        for part in tiles(second.shape[1], min(256, size)):
            grad = second_grad[:, k * ends[1] : (k + 1) * ends[1]]
            put(k, part, tn(second[:, part], grad).astype(BF16), slice(ends[0], ends[0] + ends[1]))


def weight_terms(factors):
    columns = (factors[1].shape[1] + factors[3].shape[1]) // 2
    rows = factors[0].shape[1]
    return run(
        weight_kernel,
        [((rows, columns), BF16)] + [((rows // PIECES, columns), BF16)] * PIECES,
        *factors,
        room=ROOM,
        cost=TERM_COST,
        load=(0, 1, 2, 3),
    )


def both_cores(mine, *other):
    came = jnp.concatenate([send(piece, 1) for piece in other], axis=0)
    return (mine.astype(F32) + came.astype(F32)).astype(BF16)


def on_device(
    inputs,
    cotangent,
    lengths,
    deal,
    query_key_value_weight,
    out_weight,
    up_weight,
    down_weight,
    norm_gain,
    norm_shift,
    proj_bias,
    up_bias,
):
    section = lax.axis_index("section")
    holder = lax.axis_index("row")
    column = lax.axis_index("col")
    cols_count = lax.axis_size("col")
    micro_count, rows_dev, width = inputs.shape
    model = width * cols_count
    count = plane_size()
    place = section * cols_count + column
    chips = count // 2
    tokens = rows_dev // chips
    core, chip = place % 2, place // 2
    block = query_key_value_weight.shape[1]
    half = width // 2
    heads_dev = half // HEAD_DIM
    hidden_half = up_weight.shape[2] // 2
    is_zero = section == 0

    def pick(zero, one):
        return jnp.where(is_zero, zero, one)

    def halves(array, axis):
        size = array.shape[axis] // 2
        return (
            lax.slice_in_dim(array, 0, size, axis=axis),
            lax.slice_in_dim(array, size, 2 * size, axis=axis),
        )

    attn_parts = [
        jnp.concatenate([q.reshape(block, 3 * half), o.T], axis=1)
        for q, o in zip(halves(query_key_value_weight[0], 2), halves(out_weight[0], 0))
    ]
    ffn_parts = [
        jnp.concatenate([u, d.T], axis=1)
        for u, d in zip(halves(up_weight[0], 1), halves(down_weight[0], 0))
    ]

    def both_layers(parts):
        kept, given = pick(parts[0], parts[1]), pick(parts[1], parts[0])
        came = send(given, cols_count)
        return pick(kept, came), pick(came, kept)

    def gather_slice(piece):
        return lax.all_gather(piece, "row", axis=0, tiled=True)

    def both_slices(mine):
        size = mine.shape[0] // PIECES
        return mine, *[send(mine[i * size : (i + 1) * size], 1) for i in range(PIECES)]

    mine_small = jnp.concatenate(
        [norm_gain[0], norm_shift[0], proj_bias[0], up_bias[0].reshape(-1, width)], axis=0
    )
    all_small = lax.all_gather(mine_small, PLANE, axis=0, tiled=False)
    all_small = all_small.reshape((2, cols_count) + mine_small.shape)

    def layer_small(layer):
        table = all_small[layer]
        whole = jnp.transpose(table[:, :8], (1, 0, 2)).reshape(8, model)
        slices = []
        for index in (column, jnp.bitwise_xor(column, 1)):
            own = lax.dynamic_index_in_dim(table, index, axis=0, keepdims=False)
            hidden = own[8:].reshape(2, hidden_half)
            slices.append((pick(own[:, :half], own[:, half:]), pick(hidden[0:1], hidden[1:2])))
        return {
            "gain": (whole[0:1], whole[1:2]),
            "shift": (whole[2:3], whole[3:4]),
            "attn_bias": jnp.concatenate([own[4:6] for own, _ in slices], axis=0),
            "bias_out": whole[6:7],
            "bias_down": whole[7:8],
            "up_bias": jnp.concatenate([hidden for _, hidden in slices], axis=1),
        }

    source = owned_layout(lengths[section], deal[section], holder, rows_dev)[0]
    _, usable, segment, position = owned_layout(lengths[core], deal[core], holder, rows_dev)
    order = jnp.bitwise_xor(chip, jnp.arange(chips, dtype=jnp.int32))

    def in_spread_order(values):
        return values.reshape(chips, tokens)[order].reshape(rows_dev)

    own_usable = lax.dynamic_index_in_dim(
        usable.astype(jnp.int32).reshape(chips, tokens, 1), chip, axis=0, keepdims=False
    )
    head_ids = [
        index * (2 * heads_dev) + section * heads_dev + jnp.arange(heads_dev, dtype=jnp.int32)
        for index in (column, jnp.bitwise_xor(column, 1))
    ]
    head_ids = jnp.concatenate(head_ids)
    slopes = jnp.exp2(-8.0 * (head_ids.astype(F32) + 1.0) / (model // HEAD_DIM))
    segment, position = in_spread_order(segment), in_spread_order(position)
    layout = (segment[:, None], position[:, None], segment[None], position[None], slopes)

    pairs = cols_count // 2
    trades = [(a, b) for a in range(2) for b in range(pairs)]

    def trade(array, a, b, to_worker=False):
        where = [(s, x, c) for s in range(2) for x in range(pairs) for c in range(2)]
        flat = lambda s, x, c: (s * pairs + x) * 2 + c
        ways = [(flat(s, x, c), flat(c, x ^ b, s ^ a)) for s, x, c in where]
        if to_worker:
            ways = [(to, come) for come, to in ways]
        return lax.ppermute(array, PLANE, ways)

    def at(array, index):
        return lax.dynamic_index_in_dim(array, index, axis=0, keepdims=False)

    def in_order(blocks, first, second):
        table = jnp.stack(blocks)
        return [at(table, (i ^ first) * pairs + (x ^ second)) for i in range(2) for x in range(pairs)]

    mine_x = column // 2

    def to_workers(rows):
        blocks = [trade(at(rows, (core ^ a) * pairs + (mine_x ^ b)), a, b, True) for a, b in trades]
        return by_column(blocks)

    def all_to_workers(rows):
        return [trade(rows, a, b, True) for a, b in trades]

    def by_column(blocks):
        table = jnp.stack(blocks)
        return jnp.stack(
            [at(table, ((c % 2) ^ section) * pairs + ((c // 2) ^ mine_x)) for c in range(cols_count)]
        )

    def to_dealers_at_once(rows):
        blocks = jnp.broadcast_to(rows[None], (2,) + rows.shape)
        chosen = jnp.arange(2, dtype=jnp.int32)[:, None, None, None] == core
        blocks = jnp.where(chosen, blocks, jnp.zeros_like(blocks)).reshape((count,) + rows.shape[1:])
        got = lax.all_to_all(blocks, PLANE, split_axis=0, concat_axis=0)
        return lax.dynamic_index_in_dim(
            got.reshape((chips, 2) + rows.shape[1:]), section, axis=1, keepdims=False
        )

    def to_dealers(rows):
        blocks = [trade(block, a, b) for block, a, b in dealt(rows)]
        return jnp.stack(in_order(blocks, core, mine_x))

    def dealt(rows):
        return [(at(rows, (mine_x ^ b) * 2 + (section ^ a)), a, b) for a, b in trades]

    def deal_rows(portion):
        return pick_rows(portion.reshape(-1, width), source).astype(BF16)

    def to_tokens(owned):
        own = to_workers(owned.reshape(chips, tokens, width))
        return jnp.transpose(own, (1, 0, 2)).reshape(tokens, model)

    portion = gather_direct(pick(inputs[0], inputs[1]))
    attn_pieces = both_layers(attn_parts)
    ffn_pieces = both_layers(ffn_parts)
    all_small, attn_first = together(all_small, attn_pieces[0])
    attn_pieces = (attn_first, attn_pieces[1])
    portion, all_small, *ffn_pieces = together(portion, all_small, *ffn_pieces)
    first_rows = to_tokens(deal_rows(portion))
    attn_w = [gather_slice(piece) for piece in attn_pieces]
    ffn_w = [gather_slice(piece) for piece in ffn_pieces]
    smalls = [layer_small(0), layer_small(1)]

    def to_columns(own):
        return jnp.transpose(own.reshape(tokens, cols_count, width), (1, 0, 2))

    shape = (tokens, model)

    def middle_norm(parts, hidden, layer, work=()):
        small = smalls[layer]
        hidden, *work = together(hidden, *work)
        got = run(
            functools.partial(add_norm_kernel, len(parts)),
            [(shape, F32), (shape, BF16)],
            *parts,
            hidden,
            small["bias_out"],
            small["gain"][1],
            small["shift"][1],
            load=(0, len(parts)),
            store=(0,),
            cost=NORM_COST,
        )
        return *got, work

    def end_norm(parts, middle, layer, work=()):
        small, following = smalls[layer], smalls[min(layer + 1, 1)]
        middle, *work = together(middle, *work)
        got = run(
            functools.partial(end_norm_kernel, len(parts)),
            [(shape, BF16), (shape, BF16)],
            *parts,
            middle,
            small["bias_down"],
            following["gain"][0],
            following["shift"][0],
            own_usable,
            load=(0, len(parts)),
            store=(0,),
            cost=NORM_COST,
        )
        return *got, work

    small = smalls[0]
    normed = run(norm_kernel, [(shape, BF16)], first_rows, small["gain"][0], small["shift"][0])[0]
    attn_w[0] = both_slices(attn_w[0])
    parts, attn_zero, _ = attn_forward(
        normed, layout, attn_w[0], small
    )
    given_grads = gather_direct(pick(cotangent[0], cotangent[1]))
    middle_zero, normed, (ffn_w[0],) = middle_norm(parts, first_rows, 0, (ffn_w[0],))
    ffn_w[0] = both_slices(ffn_w[0])
    parts, ffn_zero, _ = ffn_forward(normed, ffn_w[0], small)
    middle_in, normed, (given_grads, attn_w[1]) = end_norm(
        parts, middle_zero, 0, (given_grads, attn_w[1])
    )
    attn_w[1] = both_slices(attn_w[1])
    given_grads = deal_rows(given_grads)
    given_grads = all_to_workers(given_grads)
    hidden_zero = to_dealers_at_once(to_columns(middle_in))
    parts, attn_one, (hidden_zero, *given_grads) = attn_forward(
        normed, layout, attn_w[1], smalls[1], (hidden_zero, *given_grads)
    )
    hidden_zero = lax.all_gather(hidden_zero.reshape(rows_dev, width), "row", tiled=True)
    given_grads = by_column(given_grads)
    middle_one, normed, _ = middle_norm(parts, middle_in, 1)
    ffn_w[1] = both_slices(ffn_w[1])
    grad_parts, factors, up_sums, last_out = ffn_turn(
        normed, given_grads, order, ffn_w[1], smalls[1]
    )
    cotangent_rows = factors[2][:tokens]
    positions = holder * rows_dev + jnp.arange(rows_dev, dtype=jnp.int32)
    targets = given_targets(lengths[section], deal[section], positions, rows_dev)

    extra = 16

    def start_return(grad_in, a, b, *others):
        sums = jnp.stack([a[0], b[0], a[1], b[1], b[2], b[3]]).reshape(-1, cols_count, width)
        sums = jnp.transpose(sums, (1, 0, 2)).astype(BF16)
        sums = jnp.pad(sums, ((0, 0), (0, extra - 6), (0, len(others) * width)))
        rows = jnp.concatenate([to_columns(rows) for rows in (grad_in,) + others], axis=2)
        got = to_dealers(jnp.concatenate([rows, sums], axis=1))
        sums = jnp.sum(got[:, tokens : tokens + 6, :width].astype(F32), axis=0)
        return got[:, :tokens].reshape(rows_dev, -1), sums

    def with_sums(rows, sums, qkv_sums, up_sums):
        sums_by_core = []
        for k in range(2):
            qkv = qkv_sums[0, 3 * half * k : 3 * half * (k + 1)]
            up = up_sums[0, hidden_half * k : hidden_half * (k + 1)]
            sums_by_core.append(jnp.concatenate([qkv[:half], qkv[2 * half :], up]))
        columns = sums_by_core[0] + send(sums_by_core[1], 1)
        sums = jnp.concatenate([sums, columns.reshape(-1, width)], axis=0)
        sums = jnp.pad(sums, ((0, extra - sums.shape[0]), (0, rows.shape[1] - width)))
        return jnp.concatenate([rows, sums.astype(BF16)], axis=0)

    def finish_return(held):
        picked = pick_rows(held[:, :rows_dev].reshape(-1, held.shape[2]), targets)
        return picked.astype(BF16), jnp.sum(held[:, rows_dev:, :width].astype(F32), axis=0)

    def reduce_rows(total):
        return lax.psum_scatter(total, "row", scatter_dimension=0, tiled=True)

    terms = weight_terms(factors)
    down_sum = jnp.sum(cotangent_rows, axis=0, dtype=F32)
    mid, low, sums_b, terms = norm_back(
        grad_parts, middle_one, smalls[1]["gain"][1], cotangent_rows, terms
    )
    sums_b = [*sums_b, down_sum]
    mid, hidden_zero, *terms = together(mid, hidden_zero, *terms)
    ffn_term_one = reduce_rows(both_cores(*terms))
    output_parts = sum_up(*last_out)[0]
    parts, factors, qkv_sums, output_parts = attn_backward(low, attn_w[1], attn_one, output_parts)
    terms = weight_terms(factors)
    _, grad_one, sums_a, terms = norm_back(parts, middle_in, smalls[1]["gain"][0], mid, terms)
    grad_one, *terms = together(grad_one, *terms)
    attn_term_one = reduce_rows(both_cores(*terms))
    last_out = run(
        functools.partial(output_kernel, len(output_parts)),
        [(shape, BF16)],
        *output_parts,
        middle_one,
        smalls[1]["bias_down"],
        load=(0, len(output_parts)),
    )[0]
    late = start_return(grad_one, sums_a, sums_b, last_out)
    late_sums = (qkv_sums, up_sums)
    grad_zero = jnp.where(own_usable > 0, grad_one, jnp.zeros_like(grad_one))
    down_sum = jnp.sum(grad_zero, axis=0, dtype=F32)
    grad_parts, factors, up_sums, late = ffn_backward(grad_zero, ffn_w[0], ffn_zero, late)
    terms = weight_terms(factors)
    mid, low, sums_b, (ffn_term_one, *terms) = norm_back(
        grad_parts, middle_zero, smalls[0]["gain"][1], grad_zero, (ffn_term_one, *terms)
    )
    sums_b = [*sums_b, down_sum]
    late = lax.all_gather(with_sums(*late, *late_sums), "row")
    mid, *terms = together(mid, *terms)
    ffn_term_zero = reduce_rows(both_cores(*terms))
    parts, factors, qkv_sums, _ = attn_backward(low, attn_w[0], attn_zero)
    terms = weight_terms(factors)
    _, grad_in, sums_a, (attn_term_one, *terms) = norm_back(
        parts, first_rows, smalls[0]["gain"][0], mid, (attn_term_one, *terms)
    )
    attn_term_zero = both_cores(*terms)
    back_zero = with_sums(*start_return(grad_in, sums_a, sums_b), qkv_sums, up_sums)
    back_zero = gather_direct(back_zero)
    late, sums_one = finish_return(late)
    ffn_term_zero, attn_term_zero, late = together(ffn_term_zero, attn_term_zero, late)
    attn_term_zero = reduce_rows(attn_term_zero)
    back_zero, ffn_term_zero, late = together(back_zero, ffn_term_zero, late)
    back_zero, sums_zero = finish_return(back_zero)
    back_one = late[:, :width]
    hidden = pick_rows(hidden_zero, targets).astype(BF16), late[:, width:]
    stays, comes = pick(hidden[0], hidden[1]), send(pick(hidden[1], hidden[0]), cols_count)
    hidden_out = jnp.stack([pick(stays, comes), pick(comes, stays)])

    def both_halves(zero, one):
        mine = pick(zero, one)
        other = send(pick(one, zero), cols_count)
        return pick(mine, other).astype(F32), pick(other, mine).astype(F32)

    attn_grad = jnp.stack(
        [g.reshape(block, 4, half) for g in both_halves(attn_term_zero, attn_term_one)], axis=2
    ).reshape(block, 4, width)
    ffn_grad = both_halves(ffn_term_zero, ffn_term_one)
    up_grad = jnp.concatenate([g[:, :hidden_half] for g in ffn_grad], axis=1)
    down_grad = jnp.concatenate([g[:, hidden_half:].T for g in ffn_grad], axis=0)

    given = pick(back_one, back_zero)
    given = jnp.concatenate([given, pick(sums_one, sums_zero).astype(BF16)], axis=0)
    comes = send(given, cols_count).astype(F32)
    stays, came = pick(back_zero, back_one).astype(F32), comes[:rows_dev]
    in_grad = jnp.stack([pick(stays, came), pick(came, stays)])
    sums = pick(sums_zero, sums_one)
    sums = jnp.concatenate([sums[:6] + comes[rows_dev : rows_dev + 6], sums[6:]], axis=0)
    kept, came = sums[6:].reshape(-1), comes[rows_dev + 6 :].reshape(-1)
    first, second = pick(kept, came), pick(came, kept)
    bias_grad = jnp.stack(
        [
            jnp.concatenate([first[:half], second[:half]]),
            jnp.concatenate([first[half:width], second[half:width]]),
            sums[4],
            sums[5],
        ]
    )
    up_sums = jnp.concatenate(
        [first[width : width + hidden_half], second[width : width + hidden_half]]
    )
    return (
        hidden_out[None],
        in_grad[None],
        attn_grad[:, :3][None],
        attn_grad[:, 3].T[None],
        up_grad[None],
        down_grad[None],
        sums[0:2][None],
        sums[2:4][None],
        bias_grad[None],
        up_sums[None],
    )


def solution(mesh):
    placed = (
        P(None, "row", "col"),
        P(None, "row", "col"),
        P(),
        P(),
        P("section", "row", None, "col"),
        P("section", "col", "row"),
        P("section", "row", "col"),
        P("section", "col", "row"),
        P("section", None, "col"),
        P("section", None, "col"),
        P("section", None, "col"),
        P("section", "col"),
    )
    return jax.shard_map(
        on_device,
        mesh=mesh,
        in_specs=placed,
        out_specs=(
            P("section", None, "row", "col"),
            P("section", None, "row", "col"),
            P("section", "row", None, "col"),
            P("section", "col", "row"),
            P("section", "row", "col"),
            P("section", "col", "row"),
            P("section", None, "col"),
            P("section", None, "col"),
            P("section", None, "col"),
            P("section", "col"),
        ),
        check_vma=False,
    )
```

```python
import functools

import jax
import jax.numpy as jnp
from jax import lax
from jax.experimental import pallas as pl
from jax.experimental.pallas import tpu as pltpu
from jax.sharding import PartitionSpec as P

HEAD_DIM = 64
epsilon = 1e-05
far_away = 1e34
F32 = jnp.float32
BF16 = jnp.bfloat16
PLANE = ("section", "col")
ROOM = 28
PIECES = 4
BLOCK_COST = 9200000000
TERM_COST = 5000000000
NORM_COST = 2500000000


def mm(a, b, dims):
    return lax.dot_general(a, b, ((dims[0], dims[1]), ((), ())), preferred_element_type=F32)


def nn(a, b):
    return mm(a, b, ((1,), (0,)))


def nt(a, b):
    return mm(a, b, ((1,), (1,)))


def tn(a, b):
    return mm(a, b, ((0,), (0,)))


def plane_size():
    return lax.axis_size("section") * lax.axis_size("col")


def send(array, mask):
    return lax.ppermute(array, PLANE, [(i, i ^ mask) for i in range(plane_size())])


def far_masks():
    return list(range(2, plane_size(), 2))


def spread(own):
    return [own] + [send(own, m) for m in far_masks()]


def sum_up(kept, sends, later=()):
    if later:
        kept, *later = together(kept, *later)
    return [kept] + [send(o, m) for o, m in zip(sends, far_masks())], later


def together(*values):
    return lax.optimization_barrier(values)


def gather_direct(array):
    count = lax.axis_size("row")
    copies = jnp.broadcast_to(array[None], (count,) + array.shape)
    return lax.all_to_all(copies, "row", split_axis=0, concat_axis=0)


def owned_layout(lengths, deal, holder, rows_dev):
    starts = jnp.cumsum(lengths) - lengths
    first = deal == 2 * holder
    second = deal == 2 * holder + 1
    first_len = jnp.sum(jnp.where(first, lengths, 0))
    second_len = jnp.sum(jnp.where(second, lengths, 0))
    first_start = jnp.sum(jnp.where(first, starts, 0))
    second_start = jnp.sum(jnp.where(second, starts, 0))
    slots = jnp.arange(rows_dev, dtype=jnp.int32)
    in_first = slots < first_len
    in_second = jnp.logical_and(jnp.logical_not(in_first), slots < first_len + second_len)
    usable = jnp.logical_or(in_first, in_second)
    position = jnp.where(in_first, slots, slots - first_len)
    source = jnp.where(in_first, first_start + slots, second_start + position)
    source = jnp.where(usable, source, -1)
    segment = jnp.where(in_first, 0, jnp.where(in_second, 1, 2)).astype(jnp.int32)
    return source, usable, segment, position


def given_targets(lengths, deal, positions, rows_dev):
    starts = jnp.cumsum(lengths) - lengths
    before = deal[None, :] == (deal - 1)[:, None]
    partner_len = jnp.sum(jnp.where(before, lengths[None, :], 0), axis=1)
    offset = jnp.where(deal % 2 == 1, partner_len, 0)
    base = deal // 2 * rows_dev + offset - starts
    inside = jnp.logical_and(
        positions[:, None] >= starts[None, :], positions[:, None] < (starts + lengths)[None, :]
    )
    target = jnp.sum(jnp.where(inside, base[None, :] + positions[:, None], 0), axis=1)
    return jnp.where(jnp.any(inside, axis=1), target, -1)


def pick_rows(rows, wanted):
    onehot = (wanted[:, None] == jnp.arange(rows.shape[0], dtype=jnp.int32)[None, :]).astype(BF16)
    return nn(onehot, rows)


class Moves:
    def __init__(self):
        self.loads, self.stores, self.started = {}, {}, []

    def need(self, *refs):
        for ref in refs:
            if id(ref) in self.loads:
                self.loads.pop(id(ref)).wait()

    def put(self, *refs):
        for ref in refs:
            if id(ref) in self.stores:
                copy = self.stores.pop(id(ref))
                copy.start()
                self.started.append(copy)

    def finish(self):
        for copy in self.started:
            copy.wait()


def run(kernel, outs, *args, scalars=0, scratch=(), room=10, cost=0, load=(), store=()):
    vmem, hbm, smem = [pl.BlockSpec(memory_space=m) for m in (pltpu.VMEM, pltpu.HBM, pltpu.SMEM)]
    n_in, n_out = len(args), len(outs)
    load = [i % n_in for i in load]
    buffers = [(args[i].shape, args[i].dtype) for i in load] + [outs[i] for i in store]

    def body(*refs):
        refs = list(refs)
        ins, results, rest = refs[:n_in], refs[n_in : n_in + n_out], refs[n_in + n_out :]
        own, held = rest[: len(scratch)], rest[len(scratch) : len(scratch) + len(buffers)]
        moves = Moves()
        for i, place in enumerate(load):
            copy = pltpu.make_async_copy(ins[place], held[i], rest[-1].at[i])
            copy.start()
            moves.loads[id(held[i])] = copy
            ins[place] = held[i]
        for i, place in enumerate(store, len(load)):
            copy = pltpu.make_async_copy(held[i], results[place], rest[-1].at[i])
            moves.stores[id(held[i])] = copy
            results[place] = held[i]
        kernel(moves, *ins, *results, *own)
        moves.finish()

    shapes = [pltpu.VMEM(shape, kind) for shape, kind in [*scratch, *buffers]]
    call = pl.pallas_call(
        body,
        out_shape=[
            pltpu.HBM(shape, kind) if i in store else jax.ShapeDtypeStruct(shape, kind)
            for i, (shape, kind) in enumerate(outs)
        ],
        in_specs=[
            hbm if i in load else smem if i >= n_in - scalars else vmem for i in range(n_in)
        ],
        out_specs=[hbm if i in store else vmem for i in range(n_out)],
        scratch_shapes=shapes + [pltpu.SemaphoreType.DMA((len(buffers),))] * bool(buffers),
        cost_estimate=pl.CostEstimate(flops=cost, bytes_accessed=0, transcendentals=0),
        compiler_params=pltpu.CompilerParams(vmem_limit_bytes=room * 2**20),
    )
    args = [
        pltpu.with_memory_space_constraint(a, pltpu.HBM) if i in load else a
        for i, a in enumerate(args)
    ]
    return list(call(*args))


def collect(blocks, rows_ref):
    size = blocks[0].shape[0]
    for i, block in enumerate(blocks):
        rows_ref[i * size : (i + 1) * size, :] = block[...]


def tiles(total, most=256):
    size = min(total, most)
    return [slice(i, i + size) for i in range(0, total, size)]


def norm_stats(hidden):
    average = jnp.mean(hidden, axis=1, keepdims=True)
    square = jnp.mean(hidden * hidden, axis=1, keepdims=True)
    inverse = lax.rsqrt(square - average * average + epsilon)
    return (hidden - average) * inverse, inverse


def norm_kernel(moves, hidden, gain, shift, normed):
    centered, _ = norm_stats(hidden[...].astype(F32))
    normed[...] = (centered * gain[...] + shift[...]).astype(BF16)


def add_norm_kernel(count, moves, *refs):
    parts, (hidden, bias, gain, shift, middle, normed) = refs[:count], refs[count:]
    total = bias[...] + parts[1][...].astype(F32)
    for part in parts[2:]:
        total = total + part[...].astype(F32)
    moves.need(parts[0], hidden)
    total = total + parts[0][...] + hidden[...].astype(F32)
    middle[...] = total
    moves.put(middle)
    centered, _ = norm_stats(total)
    normed[...] = (centered * gain[...] + shift[...]).astype(BF16)


def end_norm_kernel(count, moves, *refs):
    parts, (hidden, bias, gain, shift, usable, result, normed) = refs[:count], refs[count:]
    total = bias[...] + parts[1][...].astype(F32)
    for part in parts[2:]:
        total = total + part[...].astype(F32)
    moves.need(parts[0], hidden)
    total = total + parts[0][...] + hidden[...]
    rounded = jnp.where(usable[...] > 0, total, 0.0).astype(BF16)
    result[...] = rounded
    moves.put(result)
    centered, _ = norm_stats(rounded.astype(F32))
    normed[...] = (centered * gain[...] + shift[...]).astype(BF16)


def norm_back_kernel(count, moves, *refs):
    parts, rest = refs[:count], refs[count:]
    hidden, gain, grad_out, grad_in, rounded, sums = rest
    grad = parts[1][...].astype(F32)
    for part in parts[2:]:
        grad = grad + part[...].astype(F32)
    moves.need(hidden, parts[0], grad_out)
    grad = grad + parts[0][...]
    centered, inverse = norm_stats(hidden[...].astype(F32))
    grad_cent = grad * gain[...]
    mean = jnp.mean(grad_cent, axis=1, keepdims=True)
    cross = jnp.mean(grad_cent * centered, axis=1, keepdims=True)
    total = grad_out[...].astype(F32) + inverse * (grad_cent - mean - centered * cross)
    low = total.astype(BF16)
    grad_in[...] = total
    moves.put(grad_in)
    rounded[...] = low
    sums[0:1, :] = jnp.sum(grad * centered, axis=0, keepdims=True)
    sums[1:2, :] = jnp.sum(grad, axis=0, keepdims=True)
    sums[2:3, :] = jnp.sum(low.astype(F32), axis=0, keepdims=True)


class Slices:
    def __init__(self, refs):
        self.mine, *self.other = refs
        self.rows = self.mine.shape[0] // PIECES

    def times(self, left, k, columns):
        if k == 0:
            return nn(left[...], self.mine[:, columns])
        total = 0.0
        for i, piece in enumerate(self.other):
            total = total + nn(left[:, i * self.rows : (i + 1) * self.rows], piece[:, columns])
        return total

    def back(self, lefts, part, columns):
        piece = self.other[part.start // self.rows]
        inside = slice(part.start % self.rows, part.start % self.rows + part.stop - part.start)
        return nt(lefts[0], self.mine[part, columns]) + nt(lefts[1], piece[inside, columns])


def put_partial(lefts, weights, columns, kept, sends):
    size = kept.shape[0]
    for part in tiles(weights.mine.shape[0], min(256, weights.rows)):
        got = weights.back(lefts, part, columns)
        kept[:, part] = got[:size]
        for i, out in enumerate(sends):
            out[:, part] = got[(i + 1) * size : (i + 2) * size].astype(BF16)


def attn_forward_kernel(count, moves, *refs):
    blocks, rest = refs[:count], refs[count:]
    weights, rest = Slices(rest[: PIECES + 1]), rest[PIECES + 1 :]
    biases, seg_col, pos_col, seg_row, pos_row, slopes = rest[:6]
    rows, qkv, soft, attended, kept, *sends, distance = rest[6:]
    collect(blocks, rows)
    moves.put(rows)
    width = weights.mine.shape[1] // 4
    heads = width // HEAD_DIM
    tokens = rows.shape[0]
    seg_r, pos_r, seg_c, pos_c = seg_row[...], pos_row[...], seg_col[...], pos_col[...]
    allowed = jnp.logical_and(seg_c == seg_r, jnp.logical_and(seg_r < 2, pos_r >= pos_c))
    distance[...] = jnp.where(allowed, (pos_r - pos_c).astype(F32), far_away)
    lefts = []
    for k in range(2):
        base = 3 * width * k
        full = weights.times(rows, k, slice(0, 3 * width))
        queries = (full[:, :width] + biases[2 * k : 2 * k + 1, :]).astype(BF16)
        key_rows = full[:, width : 2 * width].astype(BF16)
        value_rows = (full[:, 2 * width :] + biases[2 * k + 1 : 2 * k + 2, :]).astype(BF16)
        qkv[:, base : base + width] = queries
        qkv[:, base + width : base + 2 * width] = key_rows
        qkv[:, base + 2 * width : base + 3 * width] = value_rows
        values_t = value_rows.astype(F32).T.astype(BF16)
        mixed = []
        for j in range(heads):
            lanes = slice(j * HEAD_DIM, (j + 1) * HEAD_DIM)
            columns = []
            for part in tiles(tokens, 128):
                scores = nt(key_rows[:, lanes], queries[part, lanes])
                slope = slopes[k * heads + j]
                scores = scores * HEAD_DIM ** (-0.5) - slope * distance[:, part]
                highest = jnp.max(scores, axis=0, keepdims=True)
                raised = jnp.exp(scores - highest)
                weights_t = raised * (1.0 / jnp.sum(raised, axis=0, keepdims=True))
                weights_t = weights_t.astype(BF16)
                soft[k * heads + j, :, part] = weights_t
                columns.append(nn(values_t[lanes, :], weights_t))
            mixed.append(jnp.concatenate(columns, axis=1))
        out = jnp.concatenate(mixed, axis=0).T.astype(BF16)
        attended[:, k * width : (k + 1) * width] = out
        lefts.append(out)
    moves.put(qkv, soft, attended)
    put_partial(lefts, weights, slice(3 * width, 4 * width), kept, sends)
    moves.put(kept)


def attn_backward_kernel(count, moves, *refs):
    blocks, rest = refs[:count], refs[count:]
    weights, rest = Slices(rest[: PIECES + 1]), rest[PIECES + 1 :]
    qkv, soft, rows, grad_qkv, sums, kept, *sends, held = rest
    collect(blocks, rows)
    moves.put(rows)
    width = weights.mine.shape[1] // 4
    heads = width // HEAD_DIM
    tokens = rows.shape[0]
    scale = HEAD_DIM ** (-0.5)
    outs = slice(3 * width, 4 * width)
    grads_attended = [weights.times(rows, k, outs).astype(BF16) for k in range(2)]
    moves.need(qkv, soft)
    for k in range(2):
        base = 3 * width * k
        keys_t = qkv[:, base + width : base + 2 * width].astype(F32).T.astype(BF16)
        grads_q = []
        for j in range(heads):
            lanes = slice(j * HEAD_DIM, (j + 1) * HEAD_DIM)
            query_lanes, key_lanes, value_lanes = [
                slice(base + n * width + lanes.start, base + n * width + lanes.stop)
                for n in range(3)
            ]
            grad_head = grads_attended[k][:, lanes]
            for part in tiles(tokens, 128):
                grad_prob = nt(qkv[:, value_lanes], grad_head[part, :])
                weights_t = soft[k * heads + j, :, part].astype(F32)
                row_dot = jnp.sum(weights_t * grad_prob, axis=0, keepdims=True)
                held[:, part] = (weights_t * (grad_prob - row_dot)).astype(BF16)
            grad_score = held[...]
            grad_key = nn(grad_score, qkv[:, query_lanes]) * scale
            grad_qkv[:, key_lanes] = grad_key.astype(BF16)
            grad_qkv[:, value_lanes] = nn(soft[k * heads + j], grad_head).astype(BF16)
            grads_q.append(nn(keys_t[lanes, :], grad_score))
        grad_query = jnp.concatenate(grads_q, axis=0).T * scale
        grad_qkv[:, base : base + width] = grad_query.astype(BF16)
    moves.put(grad_qkv)
    sums[...] = jnp.sum(grad_qkv[...].astype(F32), axis=0, keepdims=True)
    lefts = [grad_qkv[:, : 3 * width], grad_qkv[:, 3 * width :]]
    put_partial(lefts, weights, slice(0, 3 * width), kept, sends)
    moves.put(kept)


def gelu_and_slope(u):
    root = (2.0 / 3.141592653589793) ** 0.5
    square = u * u
    tanh = jnp.tanh(u * (root + (root * 0.044715) * square))
    half = 0.5 + 0.5 * tanh
    inner = root + (3.0 * root * 0.044715) * square
    return u * half, half + (0.5 * u) * (1.0 - tanh * tanh) * inner


def ffn_slices(weights):
    hidden = weights.mine.shape[1] // 2
    for k in range(2):
        for part in tiles(hidden):
            down = slice(hidden + part.start, hidden + part.stop)
            yield k, part, down, slice(k * hidden + part.start, k * hidden + part.stop)


def put_down(activated, weights, kept, sends):
    hidden = weights.mine.shape[1] // 2
    lefts = [activated[:, :hidden], activated[:, hidden:]]
    put_partial(lefts, weights, slice(hidden, 2 * hidden), kept, sends)


def put_up(grad_upper, weights, kept, sends):
    hidden = weights.mine.shape[1] // 2
    lefts = [grad_upper[:, :hidden], grad_upper[:, hidden:]]
    put_partial(lefts, weights, slice(0, hidden), kept, sends)


def ffn_forward_kernel(count, moves, *refs):
    blocks, rest = refs[:count], refs[count:]
    weights, rest = Slices(rest[: PIECES + 1]), rest[PIECES + 1 :]
    up_bias, rows, activated, slope, kept, *sends = rest
    collect(blocks, rows)
    moves.put(rows)
    for k, up, _, units in ffn_slices(weights):
        u = weights.times(rows, k, up) + up_bias[:, units]
        act, grad = gelu_and_slope(u)
        activated[:, units] = act.astype(BF16)
        slope[:, units] = grad.astype(BF16)
    moves.put(activated, slope)
    put_down(activated, weights, kept, sends)
    moves.put(kept)


def ffn_turn_kernel(count, moves, *refs):
    blocks, rest = refs[:count], refs[count:]
    grads, weights, rest = rest[0], Slices(rest[1 : PIECES + 2]), rest[PIECES + 2 :]
    up_bias, order, rows, grad_rows, activated, grad_upper, sums, kept, *sends = rest
    collect(blocks, rows)
    size, width = blocks[0].shape[0], grads.shape[2]
    columns = rows.shape[1] // width
    for i in range(count):
        start = pl.multiple_of(order[i] * size, size)
        for j in range(columns):
            grad_rows[i * size : (i + 1) * size, j * width : (j + 1) * width] = grads[
                j, pl.ds(start, size), :
            ]
    moves.put(rows, grad_rows)
    for k, up, down, units in ffn_slices(weights):
        u = weights.times(rows, k, up) + up_bias[:, units]
        act, slope = gelu_and_slope(u)
        activated[:, units] = act.astype(BF16)
        grad = (weights.times(grad_rows, k, down) * slope).astype(BF16)
        grad_upper[:, units] = grad
        sums[:, units] = jnp.sum(grad.astype(F32), axis=0, keepdims=True)
    moves.put(activated, grad_upper)
    put_up(grad_upper, weights, kept, sends)
    moves.put(kept)


def down_kernel(moves, activated, *refs):
    weights, (kept, *sends) = Slices(refs[: PIECES + 1]), refs[PIECES + 1 :]
    put_down(activated, weights, kept, sends)
    moves.put(kept)


def output_kernel(count, moves, *refs):
    parts, (hidden, bias, result) = refs[:count], refs[count:]
    total = bias[...] + parts[1][...].astype(F32)
    for part in parts[2:]:
        total = total + part[...].astype(F32)
    moves.need(parts[0], hidden)
    result[...] = (total + parts[0][...] + hidden[...]).astype(BF16)


def ffn_backward_kernel(count, moves, *refs):
    blocks, rest = refs[:count], refs[count:]
    weights, rest = Slices(rest[: PIECES + 1]), rest[PIECES + 1 :]
    slope, rows, grad_upper, sums, kept, *sends = rest
    collect(blocks, rows)
    moves.put(rows)
    moves.need(slope)
    for k, _, down, units in ffn_slices(weights):
        grad = weights.times(rows, k, down) * slope[:, units].astype(F32)
        grad = grad.astype(BF16)
        grad_upper[:, units] = grad
        sums[:, units] = jnp.sum(grad.astype(F32), axis=0, keepdims=True)
    moves.put(grad_upper)
    put_up(grad_upper, weights, kept, sends)
    moves.put(kept)


def by_blocks(kernel, own, outs, operands, **settings):
    blocks = spread(own)
    count = len(blocks)
    shape = own.shape
    partial = [(shape, F32)] + [(shape, BF16)] * (count - 1)
    store = settings.pop("store", ()) + (len(outs),)
    beside = settings.pop("beside", ())
    got = run(
        functools.partial(kernel, count),
        outs + partial,
        *blocks,
        *operands,
        room=ROOM,
        cost=BLOCK_COST,
        store=store,
        **settings,
    )
    kept, *beside = together(got[len(outs)], *beside)
    return got[: len(outs)], kept, got[len(outs) + 1 :], beside


def attn_forward(normed, layout, weights, small, beside=()):
    size, model = normed.shape
    tokens, width = size * (plane_size() // 2), weights[0].shape[1] // 4
    results, kept, sends, beside = by_blocks(
        attn_forward_kernel,
        normed,
        [
            ((tokens, model), BF16),
            ((tokens, 6 * width), BF16),
            ((2 * width // HEAD_DIM, tokens, tokens), BF16),
            ((tokens, 2 * width), BF16),
        ],
        [*weights, small["attn_bias"], *layout],
        scalars=1,
        scratch=[((tokens, tokens), F32)],
        store=(0, 1, 2, 3),
        beside=beside,
    )
    return sum_up(kept, sends)[0], results, beside


def ffn_forward(normed, weights, small, beside=()):
    size, model = normed.shape
    tokens, hidden = size * (plane_size() // 2), weights[0].shape[1]
    results, kept, sends, beside = by_blocks(
        ffn_forward_kernel,
        normed,
        [((tokens, model), BF16), ((tokens, hidden), BF16), ((tokens, hidden), BF16)],
        [*weights, small["up_bias"]],
        store=(0, 1, 2),
        beside=beside,
    )
    return sum_up(kept, sends)[0], results, beside


def ffn_turn(normed, grads, order, weights, small):
    size, model = normed.shape
    tokens, hidden = size * (plane_size() // 2), weights[0].shape[1]
    (rows, grad_rows, activated, grad_upper, sums), kept, sends, _ = by_blocks(
        ffn_turn_kernel,
        normed,
        [
            ((tokens, model), BF16),
            ((tokens, model), BF16),
            ((tokens, hidden), BF16),
            ((tokens, hidden), BF16),
            ((1, hidden), F32),
        ],
        [grads, *weights, small["up_bias"], order],
        scalars=1,
        store=(0, 1, 2, 3),
    )
    grad_parts, factors = sum_up(kept, sends, (rows, grad_upper, grad_rows, activated))
    kept, *sends = run(
        down_kernel,
        [(a.shape, a.dtype) for a in [kept] + sends],
        factors[3],
        *weights,
        room=ROOM,
        store=(0,),
    )
    return grad_parts, factors, sums, (kept, sends)


def ffn_backward(grad_down, weights, stored, beside=()):
    size, model = grad_down.shape
    tokens, hidden = size * (plane_size() // 2), weights[0].shape[1]
    rows_two, activated, slope = stored
    (rows, grad_upper, sums), kept, sends, beside = by_blocks(
        ffn_backward_kernel,
        grad_down,
        [((tokens, model), BF16), ((tokens, hidden), BF16), ((1, hidden), F32)],
        [*weights, slope],
        load=(-1,),
        store=(0, 1),
        beside=beside,
    )
    return *sum_up(kept, sends, (rows_two, grad_upper, rows, activated)), sums, beside


def attn_backward(grad_branch, weights, stored, beside=()):
    size, model = grad_branch.shape
    tokens, width = size * (plane_size() // 2), weights[0].shape[1] // 4
    rows_one, qkv, soft, attended = stored
    (rows, grad_qkv, sums), kept, sends, beside = by_blocks(
        attn_backward_kernel,
        grad_branch,
        [((tokens, model), BF16), ((tokens, 6 * width), BF16), ((1, 6 * width), F32)],
        [*weights, qkv, soft],
        scratch=[((tokens, tokens), BF16)],
        load=(-1, -2),
        store=(0, 1),
        beside=beside,
    )
    return *sum_up(kept, sends, (rows_one, grad_qkv, rows, attended)), sums, beside


def norm_back(parts, hidden, gain, grad_out, work=()):
    shape = hidden.shape
    hidden, *work = together(hidden, *work)
    got = run(
        functools.partial(norm_back_kernel, len(parts)),
        [(shape, F32), (shape, BF16), ((3, shape[1]), F32)],
        *parts,
        hidden,
        gain,
        grad_out,
        load=(0, len(parts), len(parts) + 2),
        store=(0,),
        cost=NORM_COST,
    )
    return *got, work


def weight_kernel(moves, first, first_grad, second, second_grad, mine, *other):
    ends = first_grad.shape[1] // 2, second_grad.shape[1] // 2
    size = mine.shape[0] // PIECES

    def put(k, part, value, columns):
        if k == 0:
            mine[part, columns] = value
        else:
            inside = slice(part.start % size, part.start % size + part.stop - part.start)
            other[part.start // size][inside, columns] = value

    for k in (1, 0):
        moves.need(first, first_grad)
        for part in tiles(first.shape[1], min(256, size)):
            grad = first_grad[:, k * ends[0] : (k + 1) * ends[0]]
            put(k, part, tn(first[:, part], grad).astype(BF16), slice(0, ends[0]))
        moves.need(second, second_grad)
        for part in tiles(second.shape[1], min(256, size)):
            grad = second_grad[:, k * ends[1] : (k + 1) * ends[1]]
            put(k, part, tn(second[:, part], grad).astype(BF16), slice(ends[0], ends[0] + ends[1]))


def weight_terms(factors):
    columns = (factors[1].shape[1] + factors[3].shape[1]) // 2
    rows = factors[0].shape[1]
    return run(
        weight_kernel,
        [((rows, columns), BF16)] + [((rows // PIECES, columns), BF16)] * PIECES,
        *factors,
        room=ROOM,
        cost=TERM_COST,
        load=(0, 1, 2, 3),
    )


def both_cores(mine, *other):
    came = jnp.concatenate([send(piece, 1) for piece in other], axis=0)
    return (mine.astype(F32) + came.astype(F32)).astype(BF16)


def on_device(
    inputs,
    cotangent,
    lengths,
    deal,
    query_key_value_weight,
    out_weight,
    up_weight,
    down_weight,
    norm_gain,
    norm_shift,
    proj_bias,
    up_bias,
):
    section = lax.axis_index("section")
    holder = lax.axis_index("row")
    column = lax.axis_index("col")
    cols_count = lax.axis_size("col")
    micro_count, rows_dev, width = inputs.shape
    model = width * cols_count
    count = plane_size()
    place = section * cols_count + column
    chips = count // 2
    tokens = rows_dev // chips
    core, chip = place % 2, place // 2
    block = query_key_value_weight.shape[1]
    half = width // 2
    heads_dev = half // HEAD_DIM
    hidden_half = up_weight.shape[2] // 2
    is_zero = section == 0

    def pick(zero, one):
        return jnp.where(is_zero, zero, one)

    def halves(array, axis):
        size = array.shape[axis] // 2
        return (
            lax.slice_in_dim(array, 0, size, axis=axis),
            lax.slice_in_dim(array, size, 2 * size, axis=axis),
        )

    attn_parts = [
        jnp.concatenate([q.reshape(block, 3 * half), o.T], axis=1)
        for q, o in zip(halves(query_key_value_weight[0], 2), halves(out_weight[0], 0))
    ]
    ffn_parts = [
        jnp.concatenate([u, d.T], axis=1)
        for u, d in zip(halves(up_weight[0], 1), halves(down_weight[0], 0))
    ]

    def both_layers(parts):
        kept, given = pick(parts[0], parts[1]), pick(parts[1], parts[0])
        came = send(given, cols_count)
        return pick(kept, came), pick(came, kept)

    def gather_slice(piece):
        return lax.all_gather(piece, "row", axis=0, tiled=True)

    def both_slices(mine):
        size = mine.shape[0] // PIECES
        return mine, *[send(mine[i * size : (i + 1) * size], 1) for i in range(PIECES)]

    mine_small = jnp.concatenate(
        [norm_gain[0], norm_shift[0], proj_bias[0], up_bias[0].reshape(-1, width)], axis=0
    )
    all_small = lax.all_gather(mine_small, PLANE, axis=0, tiled=False)
    all_small = all_small.reshape((2, cols_count) + mine_small.shape)

    def layer_small(layer):
        table = all_small[layer]
        whole = jnp.transpose(table[:, :8], (1, 0, 2)).reshape(8, model)
        slices = []
        for index in (column, jnp.bitwise_xor(column, 1)):
            own = lax.dynamic_index_in_dim(table, index, axis=0, keepdims=False)
            hidden = own[8:].reshape(2, hidden_half)
            slices.append((pick(own[:, :half], own[:, half:]), pick(hidden[0:1], hidden[1:2])))
        return {
            "gain": (whole[0:1], whole[1:2]),
            "shift": (whole[2:3], whole[3:4]),
            "attn_bias": jnp.concatenate([own[4:6] for own, _ in slices], axis=0),
            "bias_out": whole[6:7],
            "bias_down": whole[7:8],
            "up_bias": jnp.concatenate([hidden for _, hidden in slices], axis=1),
        }

    source = owned_layout(lengths[section], deal[section], holder, rows_dev)[0]
    _, usable, segment, position = owned_layout(lengths[core], deal[core], holder, rows_dev)
    order = jnp.bitwise_xor(chip, jnp.arange(chips, dtype=jnp.int32))

    def in_spread_order(values):
        return values.reshape(chips, tokens)[order].reshape(rows_dev)

    own_usable = lax.dynamic_index_in_dim(
        usable.astype(jnp.int32).reshape(chips, tokens, 1), chip, axis=0, keepdims=False
    )
    head_ids = [
        index * (2 * heads_dev) + section * heads_dev + jnp.arange(heads_dev, dtype=jnp.int32)
        for index in (column, jnp.bitwise_xor(column, 1))
    ]
    head_ids = jnp.concatenate(head_ids)
    slopes = jnp.exp2(-8.0 * (head_ids.astype(F32) + 1.0) / (model // HEAD_DIM))
    segment, position = in_spread_order(segment), in_spread_order(position)
    layout = (segment[:, None], position[:, None], segment[None], position[None], slopes)

    pairs = cols_count // 2
    trades = [(a, b) for a in range(2) for b in range(pairs)]

    def trade(array, a, b, to_worker=False):
        where = [(s, x, c) for s in range(2) for x in range(pairs) for c in range(2)]
        flat = lambda s, x, c: (s * pairs + x) * 2 + c
        ways = [(flat(s, x, c), flat(c, x ^ b, s ^ a)) for s, x, c in where]
        if to_worker:
            ways = [(to, come) for come, to in ways]
        return lax.ppermute(array, PLANE, ways)

    def at(array, index):
        return lax.dynamic_index_in_dim(array, index, axis=0, keepdims=False)

    def in_order(blocks, first, second):
        table = jnp.stack(blocks)
        return [at(table, (i ^ first) * pairs + (x ^ second)) for i in range(2) for x in range(pairs)]

    mine_x = column // 2

    def to_workers(rows):
        blocks = [trade(at(rows, (core ^ a) * pairs + (mine_x ^ b)), a, b, True) for a, b in trades]
        return by_column(blocks)

    def all_to_workers(rows):
        return [trade(rows, a, b, True) for a, b in trades]

    def by_column(blocks):
        table = jnp.stack(blocks)
        return jnp.stack(
            [at(table, ((c % 2) ^ section) * pairs + ((c // 2) ^ mine_x)) for c in range(cols_count)]
        )

    def to_dealers_at_once(rows):
        blocks = jnp.broadcast_to(rows[None], (2,) + rows.shape)
        chosen = jnp.arange(2, dtype=jnp.int32)[:, None, None, None] == core
        blocks = jnp.where(chosen, blocks, jnp.zeros_like(blocks)).reshape((count,) + rows.shape[1:])
        got = lax.all_to_all(blocks, PLANE, split_axis=0, concat_axis=0)
        return lax.dynamic_index_in_dim(
            got.reshape((chips, 2) + rows.shape[1:]), section, axis=1, keepdims=False
        )

    def to_dealers(rows):
        blocks = [trade(block, a, b) for block, a, b in dealt(rows)]
        return jnp.stack(in_order(blocks, core, mine_x))

    def dealt(rows):
        return [(at(rows, (mine_x ^ b) * 2 + (section ^ a)), a, b) for a, b in trades]

    def deal_rows(portion):
        return pick_rows(portion.reshape(-1, width), source).astype(BF16)

    def to_tokens(owned):
        own = to_workers(owned.reshape(chips, tokens, width))
        return jnp.transpose(own, (1, 0, 2)).reshape(tokens, model)

    portion = gather_direct(pick(inputs[0], inputs[1]))
    attn_pieces = both_layers(attn_parts)
    ffn_pieces = both_layers(ffn_parts)
    all_small, attn_first = together(all_small, attn_pieces[0])
    attn_pieces = (attn_first, attn_pieces[1])
    portion, all_small, *ffn_pieces = together(portion, all_small, *ffn_pieces)
    first_rows = to_tokens(deal_rows(portion))
    attn_w = [gather_slice(piece) for piece in attn_pieces]
    ffn_w = [gather_slice(piece) for piece in ffn_pieces]
    smalls = [layer_small(0), layer_small(1)]

    def to_columns(own):
        return jnp.transpose(own.reshape(tokens, cols_count, width), (1, 0, 2))

    shape = (tokens, model)

    def middle_norm(parts, hidden, layer, work=()):
        small = smalls[layer]
        hidden, *work = together(hidden, *work)
        got = run(
            functools.partial(add_norm_kernel, len(parts)),
            [(shape, F32), (shape, BF16)],
            *parts,
            hidden,
            small["bias_out"],
            small["gain"][1],
            small["shift"][1],
            load=(0, len(parts)),
            store=(0,),
            cost=NORM_COST,
        )
        return *got, work

    def end_norm(parts, middle, layer, work=()):
        small, following = smalls[layer], smalls[min(layer + 1, 1)]
        middle, *work = together(middle, *work)
        got = run(
            functools.partial(end_norm_kernel, len(parts)),
            [(shape, BF16), (shape, BF16)],
            *parts,
            middle,
            small["bias_down"],
            following["gain"][0],
            following["shift"][0],
            own_usable,
            load=(0, len(parts)),
            store=(0,),
            cost=NORM_COST,
        )
        return *got, work

    small = smalls[0]
    normed = run(norm_kernel, [(shape, BF16)], first_rows, small["gain"][0], small["shift"][0])[0]
    attn_w[0] = both_slices(attn_w[0])
    parts, attn_zero, _ = attn_forward(
        normed, layout, attn_w[0], small
    )
    given_grads = gather_direct(pick(cotangent[0], cotangent[1]))
    middle_zero, normed, (ffn_w[0],) = middle_norm(parts, first_rows, 0, (ffn_w[0],))
    ffn_w[0] = both_slices(ffn_w[0])
    parts, ffn_zero, _ = ffn_forward(normed, ffn_w[0], small)
    middle_in, normed, (given_grads,) = end_norm(parts, middle_zero, 0, (given_grads,))
    attn_w[1] = both_slices(attn_w[1])
    given_grads = deal_rows(given_grads)
    given_grads = all_to_workers(given_grads)
    hidden_zero = to_dealers_at_once(to_columns(middle_in))
    parts, attn_one, (hidden_zero, *given_grads) = attn_forward(
        normed, layout, attn_w[1], smalls[1], (hidden_zero, *given_grads)
    )
    hidden_zero = lax.all_gather(hidden_zero.reshape(rows_dev, width), "row", tiled=True)
    given_grads = by_column(given_grads)
    middle_one, normed, _ = middle_norm(parts, middle_in, 1)
    ffn_w[1] = both_slices(ffn_w[1])
    grad_parts, factors, up_sums, last_out = ffn_turn(
        normed, given_grads, order, ffn_w[1], smalls[1]
    )
    cotangent_rows = factors[2][:tokens]
    positions = holder * rows_dev + jnp.arange(rows_dev, dtype=jnp.int32)
    targets = given_targets(lengths[section], deal[section], positions, rows_dev)

    extra = 16

    def start_return(grad_in, a, b, *others):
        sums = jnp.stack([a[0], b[0], a[1], b[1], b[2], b[3]]).reshape(-1, cols_count, width)
        sums = jnp.transpose(sums, (1, 0, 2)).astype(BF16)
        sums = jnp.pad(sums, ((0, 0), (0, extra - 6), (0, len(others) * width)))
        rows = jnp.concatenate([to_columns(rows) for rows in (grad_in,) + others], axis=2)
        got = to_dealers(jnp.concatenate([rows, sums], axis=1))
        sums = jnp.sum(got[:, tokens : tokens + 6, :width].astype(F32), axis=0)
        return got[:, :tokens].reshape(rows_dev, -1), sums

    def with_sums(rows, sums, qkv_sums, up_sums):
        sums_by_core = []
        for k in range(2):
            qkv = qkv_sums[0, 3 * half * k : 3 * half * (k + 1)]
            up = up_sums[0, hidden_half * k : hidden_half * (k + 1)]
            sums_by_core.append(jnp.concatenate([qkv[:half], qkv[2 * half :], up]))
        columns = sums_by_core[0] + send(sums_by_core[1], 1)
        sums = jnp.concatenate([sums, columns.reshape(-1, width)], axis=0)
        sums = jnp.pad(sums, ((0, extra - sums.shape[0]), (0, rows.shape[1] - width)))
        return jnp.concatenate([rows, sums.astype(BF16)], axis=0)

    def finish_return(held):
        picked = pick_rows(held[:, :rows_dev].reshape(-1, held.shape[2]), targets)
        return picked.astype(BF16), jnp.sum(held[:, rows_dev:, :width].astype(F32), axis=0)

    def reduce_rows(total):
        return lax.psum_scatter(total, "row", scatter_dimension=0, tiled=True)

    terms = weight_terms(factors)
    down_sum = jnp.sum(cotangent_rows, axis=0, dtype=F32)
    mid, low, sums_b, terms = norm_back(
        grad_parts, middle_one, smalls[1]["gain"][1], cotangent_rows, terms
    )
    sums_b = [*sums_b, down_sum]
    mid, hidden_zero, *terms = together(mid, hidden_zero, *terms)
    ffn_term_one = reduce_rows(both_cores(*terms))
    output_parts = sum_up(*last_out)[0]
    parts, factors, qkv_sums, output_parts = attn_backward(low, attn_w[1], attn_one, output_parts)
    terms = weight_terms(factors)
    _, grad_one, sums_a, terms = norm_back(parts, middle_in, smalls[1]["gain"][0], mid, terms)
    grad_one, *terms = together(grad_one, *terms)
    attn_term_one = reduce_rows(both_cores(*terms))
    last_out = run(
        functools.partial(output_kernel, len(output_parts)),
        [(shape, BF16)],
        *output_parts,
        middle_one,
        smalls[1]["bias_down"],
        load=(0, len(output_parts)),
    )[0]
    late = start_return(grad_one, sums_a, sums_b, last_out)
    late_sums = (qkv_sums, up_sums)
    grad_zero = jnp.where(own_usable > 0, grad_one, jnp.zeros_like(grad_one))
    down_sum = jnp.sum(grad_zero, axis=0, dtype=F32)
    grad_parts, factors, up_sums, late = ffn_backward(grad_zero, ffn_w[0], ffn_zero, late)
    terms = weight_terms(factors)
    mid, low, sums_b, (ffn_term_one, *terms) = norm_back(
        grad_parts, middle_zero, smalls[0]["gain"][1], grad_zero, (ffn_term_one, *terms)
    )
    sums_b = [*sums_b, down_sum]
    late = lax.all_gather(with_sums(*late, *late_sums), "row")
    mid, *terms = together(mid, *terms)
    ffn_term_zero = reduce_rows(both_cores(*terms))
    parts, factors, qkv_sums, _ = attn_backward(low, attn_w[0], attn_zero)
    terms = weight_terms(factors)
    _, grad_in, sums_a, (attn_term_one, *terms) = norm_back(
        parts, first_rows, smalls[0]["gain"][0], mid, (attn_term_one, *terms)
    )
    attn_term_zero = both_cores(*terms)
    back_zero = with_sums(*start_return(grad_in, sums_a, sums_b), qkv_sums, up_sums)
    back_zero = gather_direct(back_zero)
    late, sums_one = finish_return(late)
    ffn_term_zero, attn_term_zero, late = together(ffn_term_zero, attn_term_zero, late)
    attn_term_zero = reduce_rows(attn_term_zero)
    back_zero, ffn_term_zero, late = together(back_zero, ffn_term_zero, late)
    back_zero, sums_zero = finish_return(back_zero)
    back_one = late[:, :width]
    hidden = pick_rows(hidden_zero, targets).astype(BF16), late[:, width:]
    stays, comes = pick(hidden[0], hidden[1]), send(pick(hidden[1], hidden[0]), cols_count)
    hidden_out = jnp.stack([pick(stays, comes), pick(comes, stays)])

    def both_halves(zero, one):
        mine = pick(zero, one)
        other = send(pick(one, zero), cols_count)
        return pick(mine, other).astype(F32), pick(other, mine).astype(F32)

    attn_grad = jnp.stack(
        [g.reshape(block, 4, half) for g in both_halves(attn_term_zero, attn_term_one)], axis=2
    ).reshape(block, 4, width)
    ffn_grad = both_halves(ffn_term_zero, ffn_term_one)
    up_grad = jnp.concatenate([g[:, :hidden_half] for g in ffn_grad], axis=1)
    down_grad = jnp.concatenate([g[:, hidden_half:].T for g in ffn_grad], axis=0)

    given = pick(back_one, back_zero)
    given = jnp.concatenate([given, pick(sums_one, sums_zero).astype(BF16)], axis=0)
    comes = send(given, cols_count).astype(F32)
    stays, came = pick(back_zero, back_one).astype(F32), comes[:rows_dev]
    in_grad = jnp.stack([pick(stays, came), pick(came, stays)])
    sums = pick(sums_zero, sums_one)
    sums = jnp.concatenate([sums[:6] + comes[rows_dev : rows_dev + 6], sums[6:]], axis=0)
    kept, came = sums[6:].reshape(-1), comes[rows_dev + 6 :].reshape(-1)
    first, second = pick(kept, came), pick(came, kept)
    bias_grad = jnp.stack(
        [
            jnp.concatenate([first[:half], second[:half]]),
            jnp.concatenate([first[half:width], second[half:width]]),
            sums[4],
            sums[5],
        ]
    )
    up_sums = jnp.concatenate(
        [first[width : width + hidden_half], second[width : width + hidden_half]]
    )
    return (
        hidden_out[None],
        in_grad[None],
        attn_grad[:, :3][None],
        attn_grad[:, 3].T[None],
        up_grad[None],
        down_grad[None],
        sums[0:2][None],
        sums[2:4][None],
        bias_grad[None],
        up_sums[None],
    )


def solution(mesh):
    placed = (
        P(None, "row", "col"),
        P(None, "row", "col"),
        P(),
        P(),
        P("section", "row", None, "col"),
        P("section", "col", "row"),
        P("section", "row", "col"),
        P("section", "col", "row"),
        P("section", None, "col"),
        P("section", None, "col"),
        P("section", None, "col"),
        P("section", "col"),
    )
    return jax.shard_map(
        on_device,
        mesh=mesh,
        in_specs=placed,
        out_specs=(
            P("section", None, "row", "col"),
            P("section", None, "row", "col"),
            P("section", "row", None, "col"),
            P("section", "col", "row"),
            P("section", "row", "col"),
            P("section", "col", "row"),
            P("section", None, "col"),
            P("section", None, "col"),
            P("section", None, "col"),
            P("section", "col"),
        ),
        check_vma=False,
    )
```

```python
import functools

import jax
import jax.numpy as jnp
from jax import lax
from jax.experimental import pallas as pl
from jax.experimental.pallas import tpu as pltpu
from jax.sharding import PartitionSpec as P

HEAD_DIM = 64
epsilon = 1e-05
far_away = 1e34
F32 = jnp.float32
BF16 = jnp.bfloat16
PLANE = ("section", "col")
ROOM = 28
PIECES = 4
BLOCK_COST = 9200000000
TERM_COST = 5000000000
NORM_COST = 2500000000


def mm(a, b, dims):
    return lax.dot_general(a, b, ((dims[0], dims[1]), ((), ())), preferred_element_type=F32)


def nn(a, b):
    return mm(a, b, ((1,), (0,)))


def nt(a, b):
    return mm(a, b, ((1,), (1,)))


def tn(a, b):
    return mm(a, b, ((0,), (0,)))


def plane_size():
    return lax.axis_size("section") * lax.axis_size("col")


def send(array, mask):
    return lax.ppermute(array, PLANE, [(i, i ^ mask) for i in range(plane_size())])


def far_masks():
    return list(range(2, plane_size(), 2))


def spread(own):
    return [own] + [send(own, m) for m in far_masks()]


def sum_up(kept, sends, later=()):
    if later:
        kept, *later = together(kept, *later)
    return [kept] + [send(o, m) for o, m in zip(sends, far_masks())], later


def together(*values):
    return lax.optimization_barrier(values)


def gather_direct(array):
    count = lax.axis_size("row")
    copies = jnp.broadcast_to(array[None], (count,) + array.shape)
    return lax.all_to_all(copies, "row", split_axis=0, concat_axis=0)


def owned_layout(lengths, deal, holder, rows_dev):
    starts = jnp.cumsum(lengths) - lengths
    first = deal == 2 * holder
    second = deal == 2 * holder + 1
    first_len = jnp.sum(jnp.where(first, lengths, 0))
    second_len = jnp.sum(jnp.where(second, lengths, 0))
    first_start = jnp.sum(jnp.where(first, starts, 0))
    second_start = jnp.sum(jnp.where(second, starts, 0))
    slots = jnp.arange(rows_dev, dtype=jnp.int32)
    in_first = slots < first_len
    in_second = jnp.logical_and(jnp.logical_not(in_first), slots < first_len + second_len)
    usable = jnp.logical_or(in_first, in_second)
    position = jnp.where(in_first, slots, slots - first_len)
    source = jnp.where(in_first, first_start + slots, second_start + position)
    source = jnp.where(usable, source, -1)
    segment = jnp.where(in_first, 0, jnp.where(in_second, 1, 2)).astype(jnp.int32)
    return source, usable, segment, position


def given_targets(lengths, deal, positions, rows_dev):
    starts = jnp.cumsum(lengths) - lengths
    before = deal[None, :] == (deal - 1)[:, None]
    partner_len = jnp.sum(jnp.where(before, lengths[None, :], 0), axis=1)
    offset = jnp.where(deal % 2 == 1, partner_len, 0)
    base = deal // 2 * rows_dev + offset - starts
    inside = jnp.logical_and(
        positions[:, None] >= starts[None, :], positions[:, None] < (starts + lengths)[None, :]
    )
    target = jnp.sum(jnp.where(inside, base[None, :] + positions[:, None], 0), axis=1)
    return jnp.where(jnp.any(inside, axis=1), target, -1)


def pick_rows(rows, wanted):
    onehot = (wanted[:, None] == jnp.arange(rows.shape[0], dtype=jnp.int32)[None, :]).astype(BF16)
    return nn(onehot, rows)


class Moves:
    def __init__(self):
        self.loads, self.stores, self.started = {}, {}, []

    def need(self, *refs):
        for ref in refs:
            if id(ref) in self.loads:
                self.loads.pop(id(ref)).wait()

    def put(self, *refs):
        for ref in refs:
            if id(ref) in self.stores:
                copy = self.stores.pop(id(ref))
                copy.start()
                self.started.append(copy)

    def finish(self):
        for copy in self.started:
            copy.wait()


def run(kernel, outs, *args, scalars=0, scratch=(), room=10, cost=0, load=(), store=()):
    vmem, hbm, smem = [pl.BlockSpec(memory_space=m) for m in (pltpu.VMEM, pltpu.HBM, pltpu.SMEM)]
    n_in, n_out = len(args), len(outs)
    load = [i % n_in for i in load]
    buffers = [(args[i].shape, args[i].dtype) for i in load] + [outs[i] for i in store]

    def body(*refs):
        refs = list(refs)
        ins, results, rest = refs[:n_in], refs[n_in : n_in + n_out], refs[n_in + n_out :]
        own, held = rest[: len(scratch)], rest[len(scratch) : len(scratch) + len(buffers)]
        moves = Moves()
        for i, place in enumerate(load):
            copy = pltpu.make_async_copy(ins[place], held[i], rest[-1].at[i])
            copy.start()
            moves.loads[id(held[i])] = copy
            ins[place] = held[i]
        for i, place in enumerate(store, len(load)):
            copy = pltpu.make_async_copy(held[i], results[place], rest[-1].at[i])
            moves.stores[id(held[i])] = copy
            results[place] = held[i]
        kernel(moves, *ins, *results, *own)
        moves.finish()

    shapes = [pltpu.VMEM(shape, kind) for shape, kind in [*scratch, *buffers]]
    call = pl.pallas_call(
        body,
        out_shape=[
            pltpu.HBM(shape, kind) if i in store else jax.ShapeDtypeStruct(shape, kind)
            for i, (shape, kind) in enumerate(outs)
        ],
        in_specs=[
            hbm if i in load else smem if i >= n_in - scalars else vmem for i in range(n_in)
        ],
        out_specs=[hbm if i in store else vmem for i in range(n_out)],
        scratch_shapes=shapes + [pltpu.SemaphoreType.DMA((len(buffers),))] * bool(buffers),
        cost_estimate=pl.CostEstimate(flops=cost, bytes_accessed=0, transcendentals=0),
        compiler_params=pltpu.CompilerParams(vmem_limit_bytes=room * 2**20),
    )
    args = [
        pltpu.with_memory_space_constraint(a, pltpu.HBM) if i in load else a
        for i, a in enumerate(args)
    ]
    return list(call(*args))


def collect(blocks, rows_ref):
    size = blocks[0].shape[0]
    for i, block in enumerate(blocks):
        rows_ref[i * size : (i + 1) * size, :] = block[...]


def tiles(total, most=256):
    size = min(total, most)
    return [slice(i, i + size) for i in range(0, total, size)]


def norm_stats(hidden):
    average = jnp.mean(hidden, axis=1, keepdims=True)
    square = jnp.mean(hidden * hidden, axis=1, keepdims=True)
    inverse = lax.rsqrt(square - average * average + epsilon)
    return (hidden - average) * inverse, inverse


def norm_kernel(moves, hidden, gain, shift, normed):
    centered, _ = norm_stats(hidden[...].astype(F32))
    normed[...] = (centered * gain[...] + shift[...]).astype(BF16)


def add_norm_kernel(count, moves, *refs):
    parts, (hidden, bias, gain, shift, middle, normed) = refs[:count], refs[count:]
    total = bias[...] + parts[1][...].astype(F32)
    for part in parts[2:]:
        total = total + part[...].astype(F32)
    moves.need(parts[0], hidden)
    total = total + parts[0][...] + hidden[...].astype(F32)
    middle[...] = total
    moves.put(middle)
    centered, _ = norm_stats(total)
    normed[...] = (centered * gain[...] + shift[...]).astype(BF16)


def end_norm_kernel(count, moves, *refs):
    parts, (hidden, bias, gain, shift, usable, result, normed) = refs[:count], refs[count:]
    total = bias[...] + parts[1][...].astype(F32)
    for part in parts[2:]:
        total = total + part[...].astype(F32)
    moves.need(parts[0], hidden)
    total = total + parts[0][...] + hidden[...]
    rounded = jnp.where(usable[...] > 0, total, 0.0).astype(BF16)
    result[...] = rounded
    moves.put(result)
    centered, _ = norm_stats(rounded.astype(F32))
    normed[...] = (centered * gain[...] + shift[...]).astype(BF16)


def norm_back_kernel(count, moves, *refs):
    parts, rest = refs[:count], refs[count:]
    hidden, gain, grad_out, grad_in, rounded, sums = rest
    grad = parts[1][...].astype(F32)
    for part in parts[2:]:
        grad = grad + part[...].astype(F32)
    moves.need(hidden, parts[0], grad_out)
    grad = grad + parts[0][...]
    centered, inverse = norm_stats(hidden[...].astype(F32))
    grad_cent = grad * gain[...]
    mean = jnp.mean(grad_cent, axis=1, keepdims=True)
    cross = jnp.mean(grad_cent * centered, axis=1, keepdims=True)
    total = grad_out[...].astype(F32) + inverse * (grad_cent - mean - centered * cross)
    low = total.astype(BF16)
    grad_in[...] = total
    moves.put(grad_in)
    rounded[...] = low
    sums[0:1, :] = jnp.sum(grad * centered, axis=0, keepdims=True)
    sums[1:2, :] = jnp.sum(grad, axis=0, keepdims=True)
    sums[2:3, :] = jnp.sum(low.astype(F32), axis=0, keepdims=True)


class Slices:
    def __init__(self, refs):
        self.mine, *self.other = refs
        self.rows = self.mine.shape[0] // PIECES

    def times(self, left, k, columns):
        if k == 0:
            return nn(left[...], self.mine[:, columns])
        total = 0.0
        for i, piece in enumerate(self.other):
            total = total + nn(left[:, i * self.rows : (i + 1) * self.rows], piece[:, columns])
        return total

    def back(self, lefts, part, columns):
        piece = self.other[part.start // self.rows]
        inside = slice(part.start % self.rows, part.start % self.rows + part.stop - part.start)
        return nt(lefts[0], self.mine[part, columns]) + nt(lefts[1], piece[inside, columns])


def put_partial(lefts, weights, columns, kept, sends):
    size = kept.shape[0]
    for part in tiles(weights.mine.shape[0], min(256, weights.rows)):
        got = weights.back(lefts, part, columns)
        kept[:, part] = got[:size]
        for i, out in enumerate(sends):
            out[:, part] = got[(i + 1) * size : (i + 2) * size].astype(BF16)


def attn_forward_kernel(count, moves, *refs):
    blocks, rest = refs[:count], refs[count:]
    weights, rest = Slices(rest[: PIECES + 1]), rest[PIECES + 1 :]
    biases, seg_col, pos_col, seg_row, pos_row, slopes = rest[:6]
    rows, qkv, soft, attended, kept, *sends, distance = rest[6:]
    collect(blocks, rows)
    moves.put(rows)
    width = weights.mine.shape[1] // 4
    heads = width // HEAD_DIM
    tokens = rows.shape[0]
    seg_r, pos_r, seg_c, pos_c = seg_row[...], pos_row[...], seg_col[...], pos_col[...]
    allowed = jnp.logical_and(seg_c == seg_r, jnp.logical_and(seg_r < 2, pos_r >= pos_c))
    distance[...] = jnp.where(allowed, (pos_r - pos_c).astype(F32), far_away)
    lefts = []
    for k in range(2):
        base = 3 * width * k
        full = weights.times(rows, k, slice(0, 3 * width))
        queries = (full[:, :width] + biases[2 * k : 2 * k + 1, :]).astype(BF16)
        key_rows = full[:, width : 2 * width].astype(BF16)
        value_rows = (full[:, 2 * width :] + biases[2 * k + 1 : 2 * k + 2, :]).astype(BF16)
        qkv[:, base : base + width] = queries
        qkv[:, base + width : base + 2 * width] = key_rows
        qkv[:, base + 2 * width : base + 3 * width] = value_rows
        values_t = value_rows.astype(F32).T.astype(BF16)
        mixed = []
        for j in range(heads):
            lanes = slice(j * HEAD_DIM, (j + 1) * HEAD_DIM)
            columns = []
            for part in tiles(tokens, 128):
                scores = nt(key_rows[:, lanes], queries[part, lanes])
                slope = slopes[k * heads + j]
                scores = scores * HEAD_DIM ** (-0.5) - slope * distance[:, part]
                highest = jnp.max(scores, axis=0, keepdims=True)
                raised = jnp.exp(scores - highest)
                weights_t = raised * (1.0 / jnp.sum(raised, axis=0, keepdims=True))
                weights_t = weights_t.astype(BF16)
                soft[k * heads + j, :, part] = weights_t
                columns.append(nn(values_t[lanes, :], weights_t))
            mixed.append(jnp.concatenate(columns, axis=1))
        out = jnp.concatenate(mixed, axis=0).T.astype(BF16)
        attended[:, k * width : (k + 1) * width] = out
        lefts.append(out)
    moves.put(qkv, soft, attended)
    put_partial(lefts, weights, slice(3 * width, 4 * width), kept, sends)
    moves.put(kept)


def attn_backward_kernel(count, moves, *refs):
    blocks, rest = refs[:count], refs[count:]
    weights, rest = Slices(rest[: PIECES + 1]), rest[PIECES + 1 :]
    qkv, soft, rows, grad_qkv, sums, kept, *sends, held = rest
    collect(blocks, rows)
    moves.put(rows)
    width = weights.mine.shape[1] // 4
    heads = width // HEAD_DIM
    tokens = rows.shape[0]
    scale = HEAD_DIM ** (-0.5)
    outs = slice(3 * width, 4 * width)
    grads_attended = [weights.times(rows, k, outs).astype(BF16) for k in range(2)]
    moves.need(qkv, soft)
    for k in range(2):
        base = 3 * width * k
        keys_t = qkv[:, base + width : base + 2 * width].astype(F32).T.astype(BF16)
        grads_q = []
        for j in range(heads):
            lanes = slice(j * HEAD_DIM, (j + 1) * HEAD_DIM)
            query_lanes, key_lanes, value_lanes = [
                slice(base + n * width + lanes.start, base + n * width + lanes.stop)
                for n in range(3)
            ]
            grad_head = grads_attended[k][:, lanes]
            for part in tiles(tokens, 128):
                grad_prob = nt(qkv[:, value_lanes], grad_head[part, :])
                weights_t = soft[k * heads + j, :, part].astype(F32)
                row_dot = jnp.sum(weights_t * grad_prob, axis=0, keepdims=True)
                held[:, part] = (weights_t * (grad_prob - row_dot)).astype(BF16)
            grad_score = held[...]
            grad_key = nn(grad_score, qkv[:, query_lanes]) * scale
            grad_qkv[:, key_lanes] = grad_key.astype(BF16)
            grad_qkv[:, value_lanes] = nn(soft[k * heads + j], grad_head).astype(BF16)
            grads_q.append(nn(keys_t[lanes, :], grad_score))
        grad_query = jnp.concatenate(grads_q, axis=0).T * scale
        grad_qkv[:, base : base + width] = grad_query.astype(BF16)
    moves.put(grad_qkv)
    sums[...] = jnp.sum(grad_qkv[...].astype(F32), axis=0, keepdims=True)
    lefts = [grad_qkv[:, : 3 * width], grad_qkv[:, 3 * width :]]
    put_partial(lefts, weights, slice(0, 3 * width), kept, sends)
    moves.put(kept)


def gelu_and_slope(u):
    root = (2.0 / 3.141592653589793) ** 0.5
    square = u * u
    tanh = jnp.tanh(u * (root + (root * 0.044715) * square))
    half = 0.5 + 0.5 * tanh
    inner = root + (3.0 * root * 0.044715) * square
    return u * half, half + (0.5 * u) * (1.0 - tanh * tanh) * inner


def ffn_slices(weights):
    hidden = weights.mine.shape[1] // 2
    for k in range(2):
        for part in tiles(hidden):
            down = slice(hidden + part.start, hidden + part.stop)
            yield k, part, down, slice(k * hidden + part.start, k * hidden + part.stop)


def put_down(activated, weights, kept, sends):
    hidden = weights.mine.shape[1] // 2
    lefts = [activated[:, :hidden], activated[:, hidden:]]
    put_partial(lefts, weights, slice(hidden, 2 * hidden), kept, sends)


def put_up(grad_upper, weights, kept, sends):
    hidden = weights.mine.shape[1] // 2
    lefts = [grad_upper[:, :hidden], grad_upper[:, hidden:]]
    put_partial(lefts, weights, slice(0, hidden), kept, sends)


def ffn_forward_kernel(count, moves, *refs):
    blocks, rest = refs[:count], refs[count:]
    weights, rest = Slices(rest[: PIECES + 1]), rest[PIECES + 1 :]
    up_bias, rows, activated, slope, kept, *sends = rest
    collect(blocks, rows)
    moves.put(rows)
    for k, up, _, units in ffn_slices(weights):
        u = weights.times(rows, k, up) + up_bias[:, units]
        act, grad = gelu_and_slope(u)
        activated[:, units] = act.astype(BF16)
        slope[:, units] = grad.astype(BF16)
    moves.put(activated, slope)
    put_down(activated, weights, kept, sends)
    moves.put(kept)


def ffn_turn_kernel(count, moves, *refs):
    blocks, rest = refs[:count], refs[count:]
    grads, weights, rest = rest[0], Slices(rest[1 : PIECES + 2]), rest[PIECES + 2 :]
    up_bias, order, rows, grad_rows, activated, grad_upper, sums, kept, *sends = rest
    collect(blocks, rows)
    size, width = blocks[0].shape[0], grads.shape[2]
    columns = rows.shape[1] // width
    for i in range(count):
        start = pl.multiple_of(order[i] * size, size)
        for j in range(columns):
            grad_rows[i * size : (i + 1) * size, j * width : (j + 1) * width] = grads[
                j, pl.ds(start, size), :
            ]
    moves.put(rows, grad_rows)
    for k, up, down, units in ffn_slices(weights):
        u = weights.times(rows, k, up) + up_bias[:, units]
        act, slope = gelu_and_slope(u)
        activated[:, units] = act.astype(BF16)
        grad = (weights.times(grad_rows, k, down) * slope).astype(BF16)
        grad_upper[:, units] = grad
        sums[:, units] = jnp.sum(grad.astype(F32), axis=0, keepdims=True)
    moves.put(activated, grad_upper)
    put_up(grad_upper, weights, kept, sends)
    moves.put(kept)


def down_kernel(moves, activated, *refs):
    weights, (kept, *sends) = Slices(refs[: PIECES + 1]), refs[PIECES + 1 :]
    put_down(activated, weights, kept, sends)
    moves.put(kept)


def output_kernel(count, moves, *refs):
    parts, (hidden, bias, result) = refs[:count], refs[count:]
    total = bias[...] + parts[1][...].astype(F32)
    for part in parts[2:]:
        total = total + part[...].astype(F32)
    moves.need(parts[0], hidden)
    result[...] = (total + parts[0][...] + hidden[...]).astype(BF16)


def ffn_backward_kernel(count, moves, *refs):
    blocks, rest = refs[:count], refs[count:]
    weights, rest = Slices(rest[: PIECES + 1]), rest[PIECES + 1 :]
    slope, rows, grad_upper, sums, kept, *sends = rest
    collect(blocks, rows)
    moves.put(rows)
    moves.need(slope)
    for k, _, down, units in ffn_slices(weights):
        grad = weights.times(rows, k, down) * slope[:, units].astype(F32)
        grad = grad.astype(BF16)
        grad_upper[:, units] = grad
        sums[:, units] = jnp.sum(grad.astype(F32), axis=0, keepdims=True)
    moves.put(grad_upper)
    put_up(grad_upper, weights, kept, sends)
    moves.put(kept)


def by_blocks(kernel, own, outs, operands, **settings):
    blocks = spread(own)
    count = len(blocks)
    shape = own.shape
    partial = [(shape, F32)] + [(shape, BF16)] * (count - 1)
    store = settings.pop("store", ()) + (len(outs),)
    beside = settings.pop("beside", ())
    got = run(
        functools.partial(kernel, count),
        outs + partial,
        *blocks,
        *operands,
        room=ROOM,
        cost=BLOCK_COST,
        store=store,
        **settings,
    )
    kept, *beside = together(got[len(outs)], *beside)
    return got[: len(outs)], kept, got[len(outs) + 1 :], beside


def attn_forward(normed, layout, weights, small, beside=()):
    size, model = normed.shape
    tokens, width = size * (plane_size() // 2), weights[0].shape[1] // 4
    results, kept, sends, beside = by_blocks(
        attn_forward_kernel,
        normed,
        [
            ((tokens, model), BF16),
            ((tokens, 6 * width), BF16),
            ((2 * width // HEAD_DIM, tokens, tokens), BF16),
            ((tokens, 2 * width), BF16),
        ],
        [*weights, small["attn_bias"], *layout],
        scalars=1,
        scratch=[((tokens, tokens), F32)],
        store=(0, 1, 2, 3),
        beside=beside,
    )
    return sum_up(kept, sends)[0], results, beside


def ffn_forward(normed, weights, small, beside=()):
    size, model = normed.shape
    tokens, hidden = size * (plane_size() // 2), weights[0].shape[1]
    results, kept, sends, beside = by_blocks(
        ffn_forward_kernel,
        normed,
        [((tokens, model), BF16), ((tokens, hidden), BF16), ((tokens, hidden), BF16)],
        [*weights, small["up_bias"]],
        store=(0, 1, 2),
        beside=beside,
    )
    return sum_up(kept, sends)[0], results, beside


def ffn_turn(normed, grads, order, weights, small):
    size, model = normed.shape
    tokens, hidden = size * (plane_size() // 2), weights[0].shape[1]
    (rows, grad_rows, activated, grad_upper, sums), kept, sends, _ = by_blocks(
        ffn_turn_kernel,
        normed,
        [
            ((tokens, model), BF16),
            ((tokens, model), BF16),
            ((tokens, hidden), BF16),
            ((tokens, hidden), BF16),
            ((1, hidden), F32),
        ],
        [grads, *weights, small["up_bias"], order],
        scalars=1,
        store=(0, 1, 2, 3),
    )
    grad_parts, factors = sum_up(kept, sends, (rows, grad_upper, grad_rows, activated))
    kept, *sends = run(
        down_kernel,
        [(a.shape, a.dtype) for a in [kept] + sends],
        factors[3],
        *weights,
        room=ROOM,
        store=(0,),
    )
    return grad_parts, factors, sums, (kept, sends)


def ffn_backward(grad_down, weights, stored, beside=()):
    size, model = grad_down.shape
    tokens, hidden = size * (plane_size() // 2), weights[0].shape[1]
    rows_two, activated, slope = stored
    (rows, grad_upper, sums), kept, sends, beside = by_blocks(
        ffn_backward_kernel,
        grad_down,
        [((tokens, model), BF16), ((tokens, hidden), BF16), ((1, hidden), F32)],
        [*weights, slope],
        load=(-1,),
        store=(0, 1),
        beside=beside,
    )
    return *sum_up(kept, sends, (rows_two, grad_upper, rows, activated)), sums, beside


def attn_backward(grad_branch, weights, stored, beside=()):
    size, model = grad_branch.shape
    tokens, width = size * (plane_size() // 2), weights[0].shape[1] // 4
    rows_one, qkv, soft, attended = stored
    (rows, grad_qkv, sums), kept, sends, beside = by_blocks(
        attn_backward_kernel,
        grad_branch,
        [((tokens, model), BF16), ((tokens, 6 * width), BF16), ((1, 6 * width), F32)],
        [*weights, qkv, soft],
        scratch=[((tokens, tokens), BF16)],
        load=(-1, -2),
        store=(0, 1),
        beside=beside,
    )
    return *sum_up(kept, sends, (rows_one, grad_qkv, rows, attended)), sums, beside


def norm_back(parts, hidden, gain, grad_out, work=()):
    shape = hidden.shape
    hidden, *work = together(hidden, *work)
    got = run(
        functools.partial(norm_back_kernel, len(parts)),
        [(shape, F32), (shape, BF16), ((3, shape[1]), F32)],
        *parts,
        hidden,
        gain,
        grad_out,
        load=(0, len(parts), len(parts) + 2),
        store=(0,),
        cost=NORM_COST,
    )
    return *got, work


def weight_kernel(moves, first, first_grad, second, second_grad, mine, *other):
    ends = first_grad.shape[1] // 2, second_grad.shape[1] // 2
    size = mine.shape[0] // PIECES

    def put(k, part, value, columns):
        if k == 0:
            mine[part, columns] = value
        else:
            inside = slice(part.start % size, part.start % size + part.stop - part.start)
            other[part.start // size][inside, columns] = value

    for k in (1, 0):
        moves.need(first, first_grad)
        for part in tiles(first.shape[1], min(256, size)):
            grad = first_grad[:, k * ends[0] : (k + 1) * ends[0]]
            put(k, part, tn(first[:, part], grad).astype(BF16), slice(0, ends[0]))
        moves.need(second, second_grad)
        for part in tiles(second.shape[1], min(256, size)):
            grad = second_grad[:, k * ends[1] : (k + 1) * ends[1]]
            put(k, part, tn(second[:, part], grad).astype(BF16), slice(ends[0], ends[0] + ends[1]))


def weight_terms(factors):
    columns = (factors[1].shape[1] + factors[3].shape[1]) // 2
    rows = factors[0].shape[1]
    return run(
        weight_kernel,
        [((rows, columns), BF16)] + [((rows // PIECES, columns), BF16)] * PIECES,
        *factors,
        room=ROOM,
        cost=TERM_COST,
        load=(0, 1, 2, 3),
    )


def both_cores(mine, *other):
    came = jnp.concatenate([send(piece, 1) for piece in other], axis=0)
    return (mine.astype(F32) + came.astype(F32)).astype(BF16)


def on_device(
    inputs,
    cotangent,
    lengths,
    deal,
    query_key_value_weight,
    out_weight,
    up_weight,
    down_weight,
    norm_gain,
    norm_shift,
    proj_bias,
    up_bias,
):
    section = lax.axis_index("section")
    holder = lax.axis_index("row")
    column = lax.axis_index("col")
    cols_count = lax.axis_size("col")
    micro_count, rows_dev, width = inputs.shape
    model = width * cols_count
    count = plane_size()
    place = section * cols_count + column
    chips = count // 2
    tokens = rows_dev // chips
    core, chip = place % 2, place // 2
    block = query_key_value_weight.shape[1]
    half = width // 2
    heads_dev = half // HEAD_DIM
    hidden_half = up_weight.shape[2] // 2
    is_zero = section == 0

    def pick(zero, one):
        return jnp.where(is_zero, zero, one)

    def halves(array, axis):
        size = array.shape[axis] // 2
        return (
            lax.slice_in_dim(array, 0, size, axis=axis),
            lax.slice_in_dim(array, size, 2 * size, axis=axis),
        )

    attn_parts = [
        jnp.concatenate([q.reshape(block, 3 * half), o.T], axis=1)
        for q, o in zip(halves(query_key_value_weight[0], 2), halves(out_weight[0], 0))
    ]
    ffn_parts = [
        jnp.concatenate([u, d.T], axis=1)
        for u, d in zip(halves(up_weight[0], 1), halves(down_weight[0], 0))
    ]

    def both_layers(parts):
        kept, given = pick(parts[0], parts[1]), pick(parts[1], parts[0])
        came = send(given, cols_count)
        return pick(kept, came), pick(came, kept)

    def gather_slice(piece):
        return lax.all_gather(piece, "row", axis=0, tiled=True)

    def both_slices(mine):
        size = mine.shape[0] // PIECES
        return mine, *[send(mine[i * size : (i + 1) * size], 1) for i in range(PIECES)]

    mine_small = jnp.concatenate(
        [norm_gain[0], norm_shift[0], proj_bias[0], up_bias[0].reshape(-1, width)], axis=0
    )
    all_small = lax.all_gather(mine_small, PLANE, axis=0, tiled=False)
    all_small = all_small.reshape((2, cols_count) + mine_small.shape)

    def layer_small(layer):
        table = all_small[layer]
        whole = jnp.transpose(table[:, :8], (1, 0, 2)).reshape(8, model)
        slices = []
        for index in (column, jnp.bitwise_xor(column, 1)):
            own = lax.dynamic_index_in_dim(table, index, axis=0, keepdims=False)
            hidden = own[8:].reshape(2, hidden_half)
            slices.append((pick(own[:, :half], own[:, half:]), pick(hidden[0:1], hidden[1:2])))
        return {
            "gain": (whole[0:1], whole[1:2]),
            "shift": (whole[2:3], whole[3:4]),
            "attn_bias": jnp.concatenate([own[4:6] for own, _ in slices], axis=0),
            "bias_out": whole[6:7],
            "bias_down": whole[7:8],
            "up_bias": jnp.concatenate([hidden for _, hidden in slices], axis=1),
        }

    source = owned_layout(lengths[section], deal[section], holder, rows_dev)[0]
    _, usable, segment, position = owned_layout(lengths[core], deal[core], holder, rows_dev)
    order = jnp.bitwise_xor(chip, jnp.arange(chips, dtype=jnp.int32))

    def in_spread_order(values):
        return values.reshape(chips, tokens)[order].reshape(rows_dev)

    own_usable = lax.dynamic_index_in_dim(
        usable.astype(jnp.int32).reshape(chips, tokens, 1), chip, axis=0, keepdims=False
    )
    head_ids = [
        index * (2 * heads_dev) + section * heads_dev + jnp.arange(heads_dev, dtype=jnp.int32)
        for index in (column, jnp.bitwise_xor(column, 1))
    ]
    head_ids = jnp.concatenate(head_ids)
    slopes = jnp.exp2(-8.0 * (head_ids.astype(F32) + 1.0) / (model // HEAD_DIM))
    segment, position = in_spread_order(segment), in_spread_order(position)
    layout = (segment[:, None], position[:, None], segment[None], position[None], slopes)

    pairs = cols_count // 2
    trades = [(a, b) for a in range(2) for b in range(pairs)]

    def trade(array, a, b, to_worker=False):
        where = [(s, x, c) for s in range(2) for x in range(pairs) for c in range(2)]
        flat = lambda s, x, c: (s * pairs + x) * 2 + c
        ways = [(flat(s, x, c), flat(c, x ^ b, s ^ a)) for s, x, c in where]
        if to_worker:
            ways = [(to, come) for come, to in ways]
        return lax.ppermute(array, PLANE, ways)

    def at(array, index):
        return lax.dynamic_index_in_dim(array, index, axis=0, keepdims=False)

    def in_order(blocks, first, second):
        table = jnp.stack(blocks)
        return [at(table, (i ^ first) * pairs + (x ^ second)) for i in range(2) for x in range(pairs)]

    mine_x = column // 2

    def to_workers(rows):
        blocks = [trade(at(rows, (core ^ a) * pairs + (mine_x ^ b)), a, b, True) for a, b in trades]
        return by_column(blocks)

    def all_to_workers(rows):
        return [trade(rows, a, b, True) for a, b in trades]

    def by_column(blocks):
        table = jnp.stack(blocks)
        return jnp.stack(
            [at(table, ((c % 2) ^ section) * pairs + ((c // 2) ^ mine_x)) for c in range(cols_count)]
        )

    def to_dealers_at_once(rows):
        blocks = jnp.broadcast_to(rows[None], (2,) + rows.shape)
        chosen = jnp.arange(2, dtype=jnp.int32)[:, None, None, None] == core
        blocks = jnp.where(chosen, blocks, jnp.zeros_like(blocks)).reshape((count,) + rows.shape[1:])
        got = lax.all_to_all(blocks, PLANE, split_axis=0, concat_axis=0)
        return lax.dynamic_index_in_dim(
            got.reshape((chips, 2) + rows.shape[1:]), section, axis=1, keepdims=False
        )

    def to_dealers(rows):
        blocks = [trade(block, a, b) for block, a, b in dealt(rows)]
        return jnp.stack(in_order(blocks, core, mine_x))

    def dealt(rows):
        return [(at(rows, (mine_x ^ b) * 2 + (section ^ a)), a, b) for a, b in trades]

    def deal_rows(portion):
        return pick_rows(portion.reshape(-1, width), source).astype(BF16)

    def to_tokens(owned):
        own = to_workers(owned.reshape(chips, tokens, width))
        return jnp.transpose(own, (1, 0, 2)).reshape(tokens, model)

    portion = gather_direct(pick(inputs[0], inputs[1]))
    attn_pieces = both_layers(attn_parts)
    ffn_pieces = both_layers(ffn_parts)
    all_small, attn_first = together(all_small, attn_pieces[0])
    attn_pieces = (attn_first, attn_pieces[1])
    portion, all_small, *ffn_pieces = together(portion, all_small, *ffn_pieces)
    first_rows = to_tokens(deal_rows(portion))
    attn_w = [gather_slice(piece) for piece in attn_pieces]
    ffn_w = [gather_slice(piece) for piece in ffn_pieces]
    smalls = [layer_small(0), layer_small(1)]

    def to_columns(own):
        return jnp.transpose(own.reshape(tokens, cols_count, width), (1, 0, 2))

    shape = (tokens, model)

    def middle_norm(parts, hidden, layer, work=()):
        small = smalls[layer]
        hidden, *work = together(hidden, *work)
        got = run(
            functools.partial(add_norm_kernel, len(parts)),
            [(shape, F32), (shape, BF16)],
            *parts,
            hidden,
            small["bias_out"],
            small["gain"][1],
            small["shift"][1],
            load=(0, len(parts)),
            store=(0,),
            cost=NORM_COST,
        )
        return *got, work

    def end_norm(parts, middle, layer, work=()):
        small, following = smalls[layer], smalls[min(layer + 1, 1)]
        middle, *work = together(middle, *work)
        got = run(
            functools.partial(end_norm_kernel, len(parts)),
            [(shape, BF16), (shape, BF16)],
            *parts,
            middle,
            small["bias_down"],
            following["gain"][0],
            following["shift"][0],
            own_usable,
            load=(0, len(parts)),
            store=(0,),
            cost=NORM_COST,
        )
        return *got, work

    small = smalls[0]
    normed = run(norm_kernel, [(shape, BF16)], first_rows, small["gain"][0], small["shift"][0])[0]
    attn_w[0] = both_slices(attn_w[0])
    parts, attn_zero, _ = attn_forward(
        normed, layout, attn_w[0], small
    )
    given_grads = gather_direct(pick(cotangent[0], cotangent[1]))
    middle_zero, normed, (ffn_w[0],) = middle_norm(parts, first_rows, 0, (ffn_w[0],))
    ffn_w[0] = both_slices(ffn_w[0])
    parts, ffn_zero, (given_grads, attn_w[1]) = ffn_forward(
        normed, ffn_w[0], small, (given_grads, attn_w[1])
    )
    given_grads = deal_rows(given_grads)
    attn_w[1] = both_slices(attn_w[1])
    middle_in, normed, (given_grads,) = end_norm(parts, middle_zero, 0, (given_grads,))
    given_grads = all_to_workers(given_grads)
    hidden_zero = to_dealers_at_once(to_columns(middle_in))
    parts, attn_one, (hidden_zero, *given_grads) = attn_forward(
        normed, layout, attn_w[1], smalls[1], (hidden_zero, *given_grads)
    )
    hidden_zero = lax.all_gather(hidden_zero.reshape(rows_dev, width), "row", tiled=True)
    given_grads = by_column(given_grads)
    middle_one, normed, _ = middle_norm(parts, middle_in, 1)
    ffn_w[1] = both_slices(ffn_w[1])
    grad_parts, factors, up_sums, last_out = ffn_turn(
        normed, given_grads, order, ffn_w[1], smalls[1]
    )
    cotangent_rows = factors[2][:tokens]
    positions = holder * rows_dev + jnp.arange(rows_dev, dtype=jnp.int32)
    targets = given_targets(lengths[section], deal[section], positions, rows_dev)

    extra = 16

    def start_return(grad_in, a, b, *others):
        sums = jnp.stack([a[0], b[0], a[1], b[1], b[2], b[3]]).reshape(-1, cols_count, width)
        sums = jnp.transpose(sums, (1, 0, 2)).astype(BF16)
        sums = jnp.pad(sums, ((0, 0), (0, extra - 6), (0, len(others) * width)))
        rows = jnp.concatenate([to_columns(rows) for rows in (grad_in,) + others], axis=2)
        got = to_dealers(jnp.concatenate([rows, sums], axis=1))
        sums = jnp.sum(got[:, tokens : tokens + 6, :width].astype(F32), axis=0)
        return got[:, :tokens].reshape(rows_dev, -1), sums

    def with_sums(rows, sums, qkv_sums, up_sums):
        sums_by_core = []
        for k in range(2):
            qkv = qkv_sums[0, 3 * half * k : 3 * half * (k + 1)]
            up = up_sums[0, hidden_half * k : hidden_half * (k + 1)]
            sums_by_core.append(jnp.concatenate([qkv[:half], qkv[2 * half :], up]))
        columns = sums_by_core[0] + send(sums_by_core[1], 1)
        sums = jnp.concatenate([sums, columns.reshape(-1, width)], axis=0)
        sums = jnp.pad(sums, ((0, extra - sums.shape[0]), (0, rows.shape[1] - width)))
        return jnp.concatenate([rows, sums.astype(BF16)], axis=0)

    def finish_return(held):
        picked = pick_rows(held[:, :rows_dev].reshape(-1, held.shape[2]), targets)
        return picked.astype(BF16), jnp.sum(held[:, rows_dev:, :width].astype(F32), axis=0)

    def reduce_rows(total):
        return lax.psum_scatter(total, "row", scatter_dimension=0, tiled=True)

    terms = weight_terms(factors)
    down_sum = jnp.sum(cotangent_rows, axis=0, dtype=F32)
    mid, low, sums_b, terms = norm_back(
        grad_parts, middle_one, smalls[1]["gain"][1], cotangent_rows, terms
    )
    sums_b = [*sums_b, down_sum]
    mid, hidden_zero, *terms = together(mid, hidden_zero, *terms)
    ffn_term_one = reduce_rows(both_cores(*terms))
    output_parts = sum_up(*last_out)[0]
    parts, factors, qkv_sums, output_parts = attn_backward(low, attn_w[1], attn_one, output_parts)
    terms = weight_terms(factors)
    _, grad_one, sums_a, terms = norm_back(parts, middle_in, smalls[1]["gain"][0], mid, terms)
    grad_one, *terms = together(grad_one, *terms)
    attn_term_one = reduce_rows(both_cores(*terms))
    last_out = run(
        functools.partial(output_kernel, len(output_parts)),
        [(shape, BF16)],
        *output_parts,
        middle_one,
        smalls[1]["bias_down"],
        load=(0, len(output_parts)),
    )[0]
    late = start_return(grad_one, sums_a, sums_b, last_out)
    late_sums = (qkv_sums, up_sums)
    grad_zero = jnp.where(own_usable > 0, grad_one, jnp.zeros_like(grad_one))
    down_sum = jnp.sum(grad_zero, axis=0, dtype=F32)
    grad_parts, factors, up_sums, late = ffn_backward(grad_zero, ffn_w[0], ffn_zero, late)
    terms = weight_terms(factors)
    mid, low, sums_b, (ffn_term_one, *terms) = norm_back(
        grad_parts, middle_zero, smalls[0]["gain"][1], grad_zero, (ffn_term_one, *terms)
    )
    sums_b = [*sums_b, down_sum]
    late = lax.all_gather(with_sums(*late, *late_sums), "row")
    mid, *terms = together(mid, *terms)
    ffn_term_zero = reduce_rows(both_cores(*terms))
    parts, factors, qkv_sums, _ = attn_backward(low, attn_w[0], attn_zero)
    terms = weight_terms(factors)
    _, grad_in, sums_a, (attn_term_one, *terms) = norm_back(
        parts, first_rows, smalls[0]["gain"][0], mid, (attn_term_one, *terms)
    )
    attn_term_zero = both_cores(*terms)
    back_zero = with_sums(*start_return(grad_in, sums_a, sums_b), qkv_sums, up_sums)
    back_zero = gather_direct(back_zero)
    late, sums_one = finish_return(late)
    ffn_term_zero, attn_term_zero, late = together(ffn_term_zero, attn_term_zero, late)
    attn_term_zero = reduce_rows(attn_term_zero)
    back_zero, ffn_term_zero, late = together(back_zero, ffn_term_zero, late)
    back_zero, sums_zero = finish_return(back_zero)
    back_one = late[:, :width]
    hidden = pick_rows(hidden_zero, targets).astype(BF16), late[:, width:]
    stays, comes = pick(hidden[0], hidden[1]), send(pick(hidden[1], hidden[0]), cols_count)
    hidden_out = jnp.stack([pick(stays, comes), pick(comes, stays)])

    def both_halves(zero, one):
        mine = pick(zero, one)
        other = send(pick(one, zero), cols_count)
        return pick(mine, other).astype(F32), pick(other, mine).astype(F32)

    attn_grad = jnp.stack(
        [g.reshape(block, 4, half) for g in both_halves(attn_term_zero, attn_term_one)], axis=2
    ).reshape(block, 4, width)
    ffn_grad = both_halves(ffn_term_zero, ffn_term_one)
    up_grad = jnp.concatenate([g[:, :hidden_half] for g in ffn_grad], axis=1)
    down_grad = jnp.concatenate([g[:, hidden_half:].T for g in ffn_grad], axis=0)

    given = pick(back_one, back_zero)
    given = jnp.concatenate([given, pick(sums_one, sums_zero).astype(BF16)], axis=0)
    comes = send(given, cols_count).astype(F32)
    stays, came = pick(back_zero, back_one).astype(F32), comes[:rows_dev]
    in_grad = jnp.stack([pick(stays, came), pick(came, stays)])
    sums = pick(sums_zero, sums_one)
    sums = jnp.concatenate([sums[:6] + comes[rows_dev : rows_dev + 6], sums[6:]], axis=0)
    kept, came = sums[6:].reshape(-1), comes[rows_dev + 6 :].reshape(-1)
    first, second = pick(kept, came), pick(came, kept)
    bias_grad = jnp.stack(
        [
            jnp.concatenate([first[:half], second[:half]]),
            jnp.concatenate([first[half:width], second[half:width]]),
            sums[4],
            sums[5],
        ]
    )
    up_sums = jnp.concatenate(
        [first[width : width + hidden_half], second[width : width + hidden_half]]
    )
    return (
        hidden_out[None],
        in_grad[None],
        attn_grad[:, :3][None],
        attn_grad[:, 3].T[None],
        up_grad[None],
        down_grad[None],
        sums[0:2][None],
        sums[2:4][None],
        bias_grad[None],
        up_sums[None],
    )


def solution(mesh):
    placed = (
        P(None, "row", "col"),
        P(None, "row", "col"),
        P(),
        P(),
        P("section", "row", None, "col"),
        P("section", "col", "row"),
        P("section", "row", "col"),
        P("section", "col", "row"),
        P("section", None, "col"),
        P("section", None, "col"),
        P("section", None, "col"),
        P("section", "col"),
    )
    return jax.shard_map(
        on_device,
        mesh=mesh,
        in_specs=placed,
        out_specs=(
            P("section", None, "row", "col"),
            P("section", None, "row", "col"),
            P("section", "row", None, "col"),
            P("section", "col", "row"),
            P("section", "row", "col"),
            P("section", "col", "row"),
            P("section", None, "col"),
            P("section", None, "col"),
            P("section", None, "col"),
            P("section", "col"),
        ),
        check_vma=False,
    )
```
